256 devices in a mesh: lat: 32 (over y, x, core), lon: 8 (over z).
Axes of the slice: x: 4, y: 4, z: 8, core: 2. Of those that a mesh axis runs over, the one named last changes fastest.
Arguments:
- snapshots: float32 [1024, 512, 1024], P(None, 'lat', 'lon'), may hold values from -60 to 60
- land_sea: int32 [512, 1024], P('lat', 'lon'), may hold values 0 or 1
- penalty: float32 [512, 1024], P('lat', 'lon'), may hold values from 0.003 to 0.03
- initial_basis: float32 [64, 512, 1024], P(None, 'lat', 'lon'), may hold values from -6 to 6
Outputs:
- leading_basis: float32 [64, 512, 1024], P(None, 'lat', 'lon')
- rayleigh_matrix: float32 [64, 64], replicated
The draws below stay inside these ranges and needn't reach their ends.
All inputs are finite; a program needn't handle non-finite values. No bound on the sum of `land_sea` on one device may be relied on, other than what follows from the above.
Results may differ from the reference program's by a relative error of at most 0.0003.
Values sent between devices are 32-bit elements; how exact they have to be, the bound alone decides.
No kernel may reach another device: no remote copies, remote signals or barrier semaphores. Data moves between devices by JAX's collectives and lax.ppermute only.
A program may use at most 64 MiB of HBM per device.

```python
import math
import jax
import jax.numpy as jnp
from jax import lax

K = 64
NSNAP = 1024
STEPS = 2
NLAT = 512
NLON = 1024
NPTS = 524288


def draw_snapshots(key, part):
    streams = jax.random.split(jax.random.fold_in(key, 7), 9)
    snapshot_scale = 10.0 ** jax.random.uniform(streams[0], (NSNAP, 1, 1), dtype=jnp.float32) / 4.637
    point_scale = 10.0 ** jax.random.uniform(streams[1], (1, NLAT, NLON), dtype=jnp.float32) / 4.637
    latitude_ramp = (1.0 + 2.0 * jnp.arange(NLAT, dtype=jnp.float32) / max(NLAT - 1, 1)).reshape(1, NLAT, 1) / 2.082
    lat_frac = (jnp.arange(NLAT, dtype=jnp.float32) / NLAT).reshape(1, NLAT, 1)
    lon_frac = (jnp.arange(NLON, dtype=jnp.float32) / NLON).reshape(1, 1, NLON)
    wave_lat = jax.random.randint(streams[4], (4,), 1, 5).astype(jnp.float32)
    wave_lon = jax.random.randint(streams[5], (4,), 1, 5).astype(jnp.float32)
    phases = jax.random.uniform(streams[6], (4,), dtype=jnp.float32, minval=0.0, maxval=2.0 * math.pi)
    strength = 6.0 * 5.0 ** jax.random.uniform(streams[7], (4,), dtype=jnp.float32)
    amplitude = jnp.sqrt(2.0 * strength / NSNAP)
    series = jnp.clip(jax.random.normal(streams[8], (4, NSNAP), dtype=jnp.float32), -3.0, 3.0)
    modes_sum = jnp.zeros((NSNAP, NLAT, NLON), jnp.float32)
    for mode in range(4):
        pattern = jnp.cos(2.0 * math.pi * (wave_lat[mode] * lat_frac + wave_lon[mode] * lon_frac) + phases[mode])
        modes_sum = modes_sum + (amplitude[mode] * series[mode]).reshape(NSNAP, 1, 1) * pattern
    values = jnp.clip(jax.random.normal(streams[2], (NSNAP, NLAT, NLON), dtype=jnp.float32), -6.0, 6.0)
    return ((values * snapshot_scale * point_scale + modes_sum) * latitude_ramp).astype(jnp.float32)


def place_ends(entries, own_key, low, high):
    spot = [jax.random.randint(jax.random.fold_in(own_key, axis), (), 0, length) for axis, length in enumerate(entries.shape)]
    longest = entries.shape.index(max(entries.shape))
    next_to = spot[:longest] + [(spot[longest] + 1) % entries.shape[longest]] + spot[longest + 1:]
    return entries.at[tuple(spot)].set(low).at[tuple(next_to)].set(high)


def shard_levels(key, extent, cuts, least, largest):
    level, own = 1.0, jax.random.fold_in(key, 6)
    for position, blocks in cuts:
        steps = jnp.exp(jax.random.uniform(jax.random.fold_in(own, position), (blocks,), jnp.float32, least / len(cuts), largest / len(cuts)))
        level = level * jnp.repeat(steps, extent[position] // blocks).reshape([-1 if axis == position else 1 for axis in range(len(extent))])
    return level


def centred(stream_key, shape, spread, most, cuts=(), held_as=jnp.bfloat16):
    entries = spread * jax.random.normal(stream_key, shape, jnp.float32)
    if cuts:
        entries = entries * shard_levels(stream_key, shape, cuts, -0.22, 0.18)
    return jnp.clip(entries, -most, most).astype(held_as)


def setup_inputs(seed: int = 0) -> dict:
    arg_keys = jax.random.split(jax.random.key(seed), 5)
    return {
        "snapshots": draw_snapshots(jax.random.fold_in(arg_keys[4], 71), 0),
        "land_sea": place_ends((jax.random.randint(arg_keys[1], (NLAT, NLON), 0, 4) < 3).astype(jnp.int32), jax.random.fold_in(arg_keys[1], 1), 0, 1),
        "penalty": jnp.clip(jnp.exp(math.log(0.03) - 2.3025851 * jax.random.uniform(arg_keys[2], (NLAT, NLON), jnp.float32) ** shard_levels(arg_keys[2], (NLAT, NLON), ((0, 32), (1, 8)), -0.2, 0.2)), 0.003, 0.03),
        "initial_basis": centred(arg_keys[3], (K, NLAT, NLON), 1.0, 6.0, ((1, 32), (2, 8)), jnp.float32),
    }


def apply_operator(current_basis, snapshots, ocean_mask, penalty):
    masked_field = current_basis * ocean_mask
    coeffs = jnp.einsum('tab,kab->tk', snapshots, masked_field, precision=lax.Precision.HIGHEST)
    expanded = jnp.einsum('tab,tk->kab', snapshots, coeffs, precision=lax.Precision.HIGHEST)
    padded = jnp.pad(masked_field, ((0, 0), (1, 1), (1, 1)))
    neighbours = padded[:, 2:, 1:-1] + padded[:, :-2, 1:-1] + padded[:, 1:-1, 2:] + padded[:, 1:-1, :-2]
    return ocean_mask * (expanded / NPTS + penalty * (neighbours - 4.0 * masked_field))

def inner_products(left_field, right_field):
    return jnp.einsum('kab,jab->kj', left_field, right_field, precision=lax.Precision.HIGHEST)

def reference(snapshots, land_sea, penalty, initial_basis):
    ocean_mask = land_sea.astype(jnp.float32)
    current_basis = initial_basis * ocean_mask
    for iteration in range(STEPS):
        applied = apply_operator(current_basis, snapshots, ocean_mask, penalty)
        moments = inner_products(applied, applied) / NPTS
        factor = jnp.linalg.cholesky(moments)
        solved = jax.scipy.linalg.solve_triangular(factor, applied.reshape(K, -1), lower=True)
        current_basis = solved.reshape(applied.shape)
    final_image = apply_operator(current_basis, snapshots, ocean_mask, penalty)
    rayleigh_matrix = inner_products(current_basis, final_image) / NPTS
    return (current_basis, rayleigh_matrix)
```

```python
import jax
import jax.numpy as jnp
from jax import lax
from jax.experimental import pallas as pl
from jax.experimental.pallas import tpu as pltpu
from jax.sharding import Mesh, PartitionSpec as P

K = 64
NSNAP = 1024
NPTS = 524288
ROWS = 16
LANES = 128
PTS = ROWS * LANES
BLOCK = 256
NBLOCK = NSNAP // BLOCK
SHARD = 24
F32 = jnp.float32
BF16 = jnp.bfloat16
HIGHEST = lax.Precision.HIGHEST
CHIPS = ("y", "x")
LAT = ("y", "x", "core")
SWAP = [(0, 1), (1, 0)]
VMEM_LIMIT = 40 * 1024 * 1024


def parts(value):
    high = value.astype(BF16)
    return high, (value - high.astype(F32)).astype(BF16)


def dot_nt(left, right, precision=None):
    return lax.dot_general(
        left, right, (((1,), (1,)), ((), ())), precision=precision, preferred_element_type=F32
    )


def dot_nn(left, right, precision=None):
    return lax.dot_general(
        left, right, (((1,), (0,)), ((), ())), precision=precision, preferred_element_type=F32
    )


def lane_of(shape):
    return lax.broadcasted_iota(jnp.int32, shape, len(shape) - 1)


def cols(a):
    return slice(a * LANES, (a + 1) * LANES)


def store_split(split_ref, a, value):
    high, low = parts(value)
    split_ref[0:K, cols(a)] = high
    split_ref[K : 2 * K, cols(a)] = low


def edge_columns(field_ref):
    lane = lane_of((K, LANES))
    first = jnp.zeros((K, LANES), F32)
    last = jnp.zeros((K, LANES), F32)
    for a in range(ROWS):
        block = field_ref[:, cols(a)]
        first = jnp.where(lane == a, block[:, 0:1], first)
        last = jnp.where(lane == a, block[:, LANES - 1 : LANES], last)
    return first, last


def smooth(field_ref, a, north, south, west, east):
    lane = lane_of((K, LANES))
    here = field_ref[:, cols(a)]
    up = field_ref[:, cols(a - 1)] if a > 0 else north
    down = field_ref[:, cols(a + 1)] if a < ROWS - 1 else south
    left = pltpu.roll(here, 1, 1)
    right = pltpu.roll(here, LANES - 1, 1)
    left = jnp.where(lane == 0, 0.0 if west is None else west[:, a : a + 1], left)
    right = jnp.where(lane == LANES - 1, 0.0 if east is None else east[:, a : a + 1], right)
    total = left + right
    if up is not None:
        total = total + up
    if down is not None:
        total = total + down
    return total - 4.0 * here


def hand_out(pay, mine, other):
    me = lax.axis_index("core")
    mine[...] = pay[me]
    other[...] = pay[1 - me]


def take_in(mine, other, full):
    me = lax.axis_index("core")
    full[me] = mine[...]
    full[1 - me] = other[...]


def row_of_shards(full, row):
    return jnp.concatenate(
        [full[half, chip, row : row + 1, :] for half in range(2) for chip in range(16)], axis=0
    )


def put_square(pay, row, doubled):
    packed = jnp.where(lane_of((K // 2, LANES)) < K, doubled[0 : K // 2], doubled[K // 2 : K])
    for half in range(2):
        for chip in range(16):
            at = half * 16 + chip
            pay[half, chip, row : row + 1, :] = packed[at : at + 1]


def square_of(full, row):
    packed = row_of_shards(full, row)
    return jnp.concatenate([packed, pltpu.roll(packed, K, 1)], axis=0)


def folded(product):
    rows = product[0:K] + product[K : 2 * K]
    return rows + pltpu.roll(rows, K, 1)


def inverse_factor(square):
    lane = lane_of((8, LANES))
    sub = lax.broadcasted_iota(jnp.int32, (8, LANES), 0)
    blocks = []
    for b in range(K // 8):
        unit = jnp.where(lane - K == sub + 8 * b, 1.0, 0.0)
        blocks.append(jnp.where(lane < K, square[8 * b : 8 * b + 8] * (1.0 / NPTS), unit))
    for j in range(K):
        home, inner = j // 8, j % 8
        row = blocks[home][inner : inner + 1, :]
        scaled = row / blocks[home][inner : inner + 1, j : j + 1]
        for b in range(home, K // 8):
            column = blocks[b][:, j : j + 1]
            if b == home:
                if inner == 7:
                    continue
                column = jnp.where(sub > inner, column, 0.0)
            blocks[b] = blocks[b] - column * scaled
    done = []
    for b in range(K // 8):
        diagonal = jnp.sum(jnp.where(lane == sub + 8 * b, blocks[b], 0.0), axis=1, keepdims=True)
        done.append(blocks[b] * lax.rsqrt(diagonal))
    return pltpu.roll(jnp.concatenate(done, axis=0), K, 1)[:, 0:K]


def put_coefficients(pay, block, both):
    half = block % 2
    summed = both + pltpu.roll(both, K, 1)
    summed = summed.reshape(16, 16, LANES)
    if block < 2:
        pay[half, :, 0:16, :] = summed
    else:
        old = pay[half, :, 0:16, :]
        pay[half, :, 0:16, :] = jnp.where(lane_of(old.shape) < K, old, summed)


def coefficients_of(full, spread):
    packed = full[:, :, 0:16, :].reshape(NSNAP // 2, LANES)
    turned = packed.T
    if spread is not None:
        for block in range(NBLOCK):
            top = (block // 2) * K
            left = (block % 2) * BLOCK
            high, low = parts(turned[top : top + K, left : left + BLOCK])
            spread[block, 0:K, :] = high
            spread[block, K : 2 * K, :] = low
    return turned


def begin_kernel(
    snap, basis, sea, split_out, flat, top, bottom, first, last, mine, other, split, pay
):
    step = pl.program_id(0)

    @pl.when(step == 0)
    def _():
        pay[...] = jnp.zeros_like(pay)
        for a in range(ROWS):
            value = basis[pl.ds(a, K, stride=ROWS), :] * sea[a : a + 1, :].astype(F32)
            flat[:, cols(a)] = value
            store_split(split, a, value)
        top[...] = flat[:, cols(0)]
        bottom[...] = flat[:, cols(ROWS - 1)]
        first[...], last[...] = edge_columns(flat)

    depth = BLOCK // 2
    for a in range(ROWS):
        high, low = parts(snap[pl.ds(a, depth, stride=ROWS), :])
        split_out[0, 0, :, cols(a)] = high
        split_out[0, 1, :, cols(a)] = low
    both = dot_nt(split_out[0, 0], split[...]) + dot_nt(split_out[0, 1], split[...])
    summed = (both + pltpu.roll(both, K, 1)).reshape(8, 16, LANES)
    half = (step // 2) % 2
    at = pl.ds((step % 2) * 8, 8)
    keep = (lane_of(summed.shape) < K) & (step >= 4)
    pay[half, at, 0:16, :] = jnp.where(keep, pay[half, at, 0:16, :], summed)

    @pl.when(step == pl.num_programs(0) - 1)
    def _():
        hand_out(pay, mine, other)


def whole(shape):
    return pl.BlockSpec(shape, lambda i: (0,) * len(shape))


def begin(snapshots, basis, sea):
    depth = BLOCK // 2
    halo = jax.ShapeDtypeStruct((K, LANES), F32)
    share = jax.ShapeDtypeStruct((16, SHARD, LANES), F32)
    return pl.pallas_call(
        begin_kernel,
        grid=(NSNAP // depth,),
        in_specs=[
            pl.BlockSpec((depth * ROWS, LANES), lambda i: (i, 0)),
            whole((K * ROWS, LANES)),
            whole((ROWS, LANES)),
        ],
        out_specs=[
            pl.BlockSpec((1, 2, depth, PTS), lambda i: (i // 2, 0, i % 2, 0)),
            whole((K, PTS)),
            *[whole((K, LANES))] * 4,
            *[whole((16, SHARD, LANES))] * 2,
        ],
        out_shape=[
            jax.ShapeDtypeStruct((NBLOCK, 2, BLOCK, PTS), BF16),
            jax.ShapeDtypeStruct((K, PTS), F32),
            halo,
            halo,
            halo,
            halo,
            share,
            share,
        ],
        scratch_shapes=[
            pltpu.VMEM((2 * K, PTS), BF16),
            pltpu.VMEM((2, 16, SHARD, LANES), F32),
        ],
        compiler_params=pltpu.CompilerParams(vmem_limit_bytes=VMEM_LIMIT),
        name="split_and_project",
    )(snapshots.reshape(NSNAP * ROWS, LANES), basis.reshape(K * ROWS, LANES), sea)


def copy_of(snap, held, sems, block):
    return pltpu.make_async_copy(snap.at[block], held.at[block], sems.at[block])


def expand(spread, snap, held, sems, total):
    width = 512
    for block in range(NBLOCK):
        copy_of(snap, held, sems, block).wait()
        for left in range(0, PTS, width):
            at = slice(left, left + width)
            both = dot_nn(spread[block], held[block, 0, :, at]) + dot_nn(
                spread[block], held[block, 1, :, at]
            )
            piece = both[0:K] + both[K : 2 * K]
            total[:, at] = piece if block == 0 else total[:, at] + piece


def project(held, split, pay):
    for block in range(NBLOCK):
        both = dot_nt(held[block, 0], split[...]) + dot_nt(held[block, 1], split[...])
        put_coefficients(pay, block, both)


def applied_field(total, prev, sides, sea, pen, out):
    north, south, west, east = (side[...] for side in sides)
    for a in range(ROWS):
        lap = smooth(prev, a, north, south, west, east)
        mask = sea[a : a + 1, :].astype(F32)
        out[:, cols(a)] = mask * (total[:, cols(a)] * (1.0 / NPTS) + pen[a : a + 1, :] * lap)


def first_kernel(
    got_mine, got_other, snap, prev, north, south, west, east, sea, pen,
    field, top, bottom, first, last, mine, other,
    full, held, spread, total, split, pay, sems,
):
    for block in range(NBLOCK):
        copy_of(snap, held, sems, block).start()
    take_in(got_mine, got_other, full)
    coefficients_of(full, spread)
    expand(spread, snap, held, sems, total)
    applied_field(total, prev, (north, south, west, east), sea, pen, field)
    for a in range(ROWS):
        store_split(split, a, field[:, cols(a)])
    top[...] = field[:, cols(0)]
    bottom[...] = field[:, cols(ROWS - 1)]
    first[...], last[...] = edge_columns(field)
    pay[...] = jnp.zeros_like(pay)
    put_square(pay, 16, folded(dot_nt(split[...], split[...])))
    project(held, split, pay)
    hand_out(pay, mine, other)


def scratch_for_expand():
    return [
        pltpu.VMEM((2, 16, SHARD, LANES), F32),
        pltpu.VMEM((NBLOCK, 2, BLOCK, PTS), BF16),
        pltpu.VMEM((NBLOCK, 2 * K, BLOCK), BF16),
        pltpu.VMEM((K, PTS), F32),
    ]


VM = pl.BlockSpec(memory_space=pltpu.VMEM)
HB = pl.BlockSpec(memory_space=pl.ANY)


def first_step(got, snap, prev, sides, sea, pen):
    halo = jax.ShapeDtypeStruct((K, LANES), F32)
    share = jax.ShapeDtypeStruct((16, SHARD, LANES), F32)
    return pl.pallas_call(
        first_kernel,
        in_specs=[VM, VM, HB, *[VM] * 7],
        out_specs=[VM] * 7,
        out_shape=[jax.ShapeDtypeStruct((K, PTS), F32), halo, halo, halo, halo, share, share],
        scratch_shapes=[
            *scratch_for_expand(),
            pltpu.VMEM((2 * K, PTS), BF16),
            pltpu.VMEM((2, 16, SHARD, LANES), F32),
            pltpu.SemaphoreType.DMA((NBLOCK,)),
        ],
        compiler_params=pltpu.CompilerParams(vmem_limit_bytes=VMEM_LIMIT),
        name="expand_and_project",
    )(*got, snap, prev, *sides, sea, pen)


def second_kernel(
    got_mine, got_other, snap, prev, north, south, west, east, sea, pen,
    field, bottom, last,
    full, held, spread, total, raw, sems,
):
    for block in range(NBLOCK):
        copy_of(snap, held, sems, block).start()
    take_in(got_mine, got_other, full)
    coefficients_of(full, spread)
    inverse = inverse_factor(square_of(full, 16))
    expand(spread, snap, held, sems, total)
    applied_field(total, prev, (north, south, west, east), sea, pen, raw)
    field[...] = dot_nn(inverse, raw[...], HIGHEST)
    bottom[0:K, :] = field[:, cols(ROWS - 1)]
    bottom[K : 2 * K, :] = field[:, cols(ROWS - 1)] * pen[ROWS - 1 : ROWS, :]
    _, last[0:K, :] = edge_columns(field)
    for a in range(ROWS):
        raw[:, cols(a)] = field[:, cols(a)] * pen[a : a + 1, :]
    _, last[K : 2 * K, :] = edge_columns(raw)


def second_step(got, snap, prev, sides, sea, pen):
    halo = jax.ShapeDtypeStruct((2 * K, LANES), F32)
    return pl.pallas_call(
        second_kernel,
        in_specs=[VM, VM, HB, *[VM] * 7],
        out_specs=[VM] * 3,
        out_shape=[jax.ShapeDtypeStruct((K, PTS), F32), halo, halo],
        scratch_shapes=[
            *scratch_for_expand(),
            pltpu.VMEM((K, PTS), F32),
            pltpu.SemaphoreType.DMA((NBLOCK,)),
        ],
        compiler_params=pltpu.CompilerParams(vmem_limit_bytes=VMEM_LIMIT),
        name="factor_and_expand",
    )(*got, snap, prev, *sides, sea, pen)


def project_kernel(snap, field, pay, held, split, sems):
    for block in range(NBLOCK):
        copy_of(snap, held, sems, block).start()
    for a in range(ROWS):
        store_split(split, a, field[:, cols(a)])
    pay[...] = jnp.zeros_like(pay)
    put_square(pay, 16, folded(dot_nt(split[...], split[...])))
    for block in range(NBLOCK):
        copy_of(snap, held, sems, block).wait()
        both = dot_nt(held[block, 0], split[...]) + dot_nt(held[block, 1], split[...])
        put_coefficients(pay, block, both)


def project_step(snap, field):
    return pl.pallas_call(
        project_kernel,
        in_specs=[HB, VM],
        out_specs=VM,
        out_shape=jax.ShapeDtypeStruct((2, 16, SHARD, LANES), F32),
        scratch_shapes=[
            pltpu.VMEM((NBLOCK, 2, BLOCK, PTS), BF16),
            pltpu.VMEM((2 * K, PTS), BF16),
            pltpu.SemaphoreType.DMA((NBLOCK,)),
        ],
        compiler_params=pltpu.CompilerParams(vmem_limit_bytes=VMEM_LIMIT),
        name="project",
    )(snap, field)


def rough_kernel(field, north, west, pen, base, mine, other, left, right, pay):
    def put(at, first, second):
        high, low = parts(first)
        left[0:K, cols(at)] = high
        left[K : 2 * K, cols(at)] = low
        high, low = parts(second)
        right[0:K, cols(at)] = high
        right[K : 2 * K, cols(at)] = low

    first = jnp.zeros((K, LANES), F32)
    first_weighted = jnp.zeros((K, LANES), F32)
    lane = lane_of((K, LANES))
    for a in range(ROWS):
        here = field[:, cols(a)]
        weighted = here * pen[a : a + 1, :]
        put(a, weighted, smooth(field, a, None, None, None, None))
        first = jnp.where(lane == a, here[:, 0:1], first)
        first_weighted = jnp.where(lane == a, weighted[:, 0:1], first_weighted)
        if a == 0:
            put(ROWS, weighted, north[0:K, :])
            put(ROWS + 1, north[K : 2 * K, :], here)
    put(ROWS + 2, first_weighted, west[0:K, :])
    put(ROWS + 3, west[K : 2 * K, :], first)
    pay[...] = base[...]
    put_square(pay, 17, folded(dot_nt(left[...], right[...])))
    hand_out(pay, mine, other)


def rough_step(field, north, west, pen, base):
    share = jax.ShapeDtypeStruct((16, SHARD, LANES), F32)
    return pl.pallas_call(
        rough_kernel,
        in_specs=[VM] * 5,
        out_specs=[VM] * 2,
        out_shape=[share, share],
        scratch_shapes=[
            pltpu.VMEM((2 * K, PTS + 4 * LANES), BF16),
            pltpu.VMEM((2 * K, PTS + 4 * LANES), BF16),
            pltpu.VMEM((2, 16, SHARD, LANES), F32),
        ],
        compiler_params=pltpu.CompilerParams(vmem_limit_bytes=VMEM_LIMIT),
        name="roughness_products",
    )(field, north, west, pen, base)


def last_kernel(got_mine, got_other, field, basis, matrix, full):
    take_in(got_mine, got_other, full)
    inverse = inverse_factor(square_of(full, 16))
    solved = dot_nn(inverse, field[...], HIGHEST)
    for a in range(ROWS):
        basis[pl.ds(a, K, stride=ROWS), :] = solved[:, cols(a)]
    turned = coefficients_of(full, None)
    rough = square_of(full, 17)[:, 0:K]
    low, high = turned[0:K], turned[K : 2 * K]
    gram = dot_nt(low, low, HIGHEST) + dot_nt(high, high, HIGHEST)
    middle = (gram * (1.0 / NPTS) + rough) * (1.0 / NPTS)
    matrix[...] = dot_nt(dot_nn(inverse, middle, HIGHEST), inverse, HIGHEST)


def last_step(got, field):
    basis, matrix = pl.pallas_call(
        last_kernel,
        in_specs=[VM] * 3,
        out_specs=[VM] * 2,
        out_shape=[
            jax.ShapeDtypeStruct((K * ROWS, LANES), F32),
            jax.ShapeDtypeStruct((K, K), F32),
        ],
        scratch_shapes=[pltpu.VMEM((2, 16, SHARD, LANES), F32)],
        compiler_params=pltpu.CompilerParams(vmem_limit_bytes=VMEM_LIMIT),
        name="factor_and_finish",
    )(*got, field)
    return basis.reshape(K, ROWS, LANES), matrix


def to_each(value, axis, count):
    return lax.all_to_all(
        jnp.broadcast_to(value[None], (count, *value.shape)), axis, 0, 0, tiled=True
    )


def summed_everywhere(mine, other):
    pair = mine + lax.ppermute(other, "core", SWAP)
    share = lax.all_to_all(pair, CHIPS, 0, 0, tiled=True).sum(axis=0)
    share = to_each(share, "z", 8).sum(axis=0)
    half = to_each(share, CHIPS, 16)
    return half, lax.ppermute(half, "core", SWAP)


def from_below(value, axis, count):
    return lax.ppermute(value, axis, [(i, i + 1) for i in range(count - 1)])


def from_above(value, axis, count):
    return lax.ppermute(value, axis, [(i + 1, i) for i in range(count - 1)])


def sides_of(top, bottom, first, last):
    return (
        from_below(bottom, LAT, 32),
        from_above(top, LAT, 32),
        from_below(last, "z", 8),
        from_above(first, "z", 8),
    )


def local(snapshots, land_sea, penalty, initial_basis):
    snap, start, *edges, mine, other = begin(snapshots, initial_basis, land_sea)
    sides = sides_of(*edges)
    got = summed_everywhere(mine, other)
    applied, *edges, mine, other = first_step(got, snap, start, sides, land_sea, penalty)
    sides = sides_of(*edges)
    got = summed_everywhere(mine, other)
    applied, bottom, last = second_step(got, snap, applied, sides, land_sea, penalty)
    north = from_below(bottom, LAT, 32)
    west = from_below(last, "z", 8)
    base = project_step(snap, applied)
    mine, other = rough_step(applied, north, west, penalty, base)
    got = summed_everywhere(mine, other)
    return last_step(got, applied)


def solution(mesh):
    split_mesh = Mesh(mesh.devices.reshape(4, 4, 2, 8), ("y", "x", "core", "z"))
    flat = P(LAT, "z")
    deep = P(None, LAT, "z")
    return jax.shard_map(
        local,
        mesh=split_mesh,
        in_specs=(deep, flat, flat, deep),
        out_specs=(deep, P()),
        check_vma=False,
    )
```

```python
import jax
import jax.numpy as jnp
from jax import lax
from jax.experimental import pallas as pl
from jax.experimental.pallas import tpu as pltpu
from jax.sharding import Mesh, PartitionSpec as P

K = 64
NSNAP = 1024
NPTS = 524288
ROWS = 16
LANES = 128
PTS = ROWS * LANES
BLOCK = 256
NBLOCK = NSNAP // BLOCK
SHARD = 24
DEPTH = 16
F32 = jnp.float32
BF16 = jnp.bfloat16
HIGHEST = lax.Precision.HIGHEST
CHIPS = ("y", "x")
LAT = ("y", "x", "core")
SWAP = [(0, 1), (1, 0)]
VMEM_LIMIT = 50 * 1024 * 1024
SMALL_LIMIT = 20 * 1024 * 1024


def parts(value):
    high = value.astype(BF16)
    return high, (value - high.astype(F32)).astype(BF16)


def dot_nt(left, right, precision=None):
    return lax.dot_general(
        left, right, (((1,), (1,)), ((), ())), precision=precision, preferred_element_type=F32
    )


def dot_nn(left, right, precision=None):
    return lax.dot_general(
        left, right, (((1,), (0,)), ((), ())), precision=precision, preferred_element_type=F32
    )


def lane_of(shape):
    return lax.broadcasted_iota(jnp.int32, shape, len(shape) - 1)


def cols(a):
    return slice(a * LANES, (a + 1) * LANES)


def store_split(split_ref, a, value):
    high, low = parts(value)
    split_ref[0:K, cols(a)] = high
    split_ref[K : 2 * K, cols(a)] = low


def edge_columns(field_ref):
    lane = lane_of((K, LANES))
    first = jnp.zeros((K, LANES), F32)
    last = jnp.zeros((K, LANES), F32)
    for a in range(ROWS):
        block = field_ref[:, cols(a)]
        first = jnp.where(lane == a, block[:, 0:1], first)
        last = jnp.where(lane == a, block[:, LANES - 1 : LANES], last)
    return first, last


def smooth(field_ref, a, north, south, west, east):
    lane = lane_of((K, LANES))
    here = field_ref[:, cols(a)]
    up = field_ref[:, cols(a - 1)] if a > 0 else north
    down = field_ref[:, cols(a + 1)] if a < ROWS - 1 else south
    left = pltpu.roll(here, 1, 1)
    right = pltpu.roll(here, LANES - 1, 1)
    left = jnp.where(lane == 0, 0.0 if west is None else west[:, a : a + 1], left)
    right = jnp.where(lane == LANES - 1, 0.0 if east is None else east[:, a : a + 1], right)
    total = left + right
    if up is not None:
        total = total + up
    if down is not None:
        total = total + down
    return total - 4.0 * here


def hand_out(pay, mine, other):
    me = lax.axis_index("core")
    mine[...] = pay[me]
    other[...] = pay[1 - me]


def take_in(mine, other, full):
    me = lax.axis_index("core")
    full[me] = mine[...]
    full[1 - me] = other[...]


def row_of_shards(full, row):
    return jnp.concatenate(
        [full[half, chip, row : row + 1, :] for half in range(2) for chip in range(16)], axis=0
    )


def put_square(pay, row, doubled):
    packed = jnp.where(lane_of((K // 2, LANES)) < K, doubled[0 : K // 2], doubled[K // 2 : K])
    for half in range(2):
        for chip in range(16):
            at = half * 16 + chip
            pay[half, chip, row : row + 1, :] = packed[at : at + 1]


def square_of(full, row):
    packed = row_of_shards(full, row)
    return jnp.concatenate([packed, pltpu.roll(packed, K, 1)], axis=0)


def folded(product):
    rows = product[0:K] + product[K : 2 * K]
    return rows + pltpu.roll(rows, K, 1)


def inverse_factor(square):
    lane = lane_of((8, LANES))
    sub = lax.broadcasted_iota(jnp.int32, (8, LANES), 0)
    blocks = []
    for b in range(K // 8):
        unit = jnp.where(lane - K == sub + 8 * b, 1.0, 0.0)
        blocks.append(jnp.where(lane < K, square[8 * b : 8 * b + 8] * (1.0 / NPTS), unit))
    for j in range(K):
        home, inner = j // 8, j % 8
        row = blocks[home][inner : inner + 1, :]
        scaled = row / blocks[home][inner : inner + 1, j : j + 1]
        for b in range(home, K // 8):
            column = blocks[b][:, j : j + 1]
            if b == home:
                if inner == 7:
                    continue
                column = jnp.where(sub > inner, column, 0.0)
            blocks[b] = blocks[b] - column * scaled
    done = []
    for b in range(K // 8):
        diagonal = jnp.sum(jnp.where(lane == sub + 8 * b, blocks[b], 0.0), axis=1, keepdims=True)
        done.append(blocks[b] * lax.rsqrt(diagonal))
    return pltpu.roll(jnp.concatenate(done, axis=0), K, 1)[:, 0:K]


def put_coefficients(pay, block, both):
    half = block % 2
    summed = both + pltpu.roll(both, K, 1)
    summed = summed.reshape(16, 16, LANES)
    if block < 2:
        pay[half, :, 0:16, :] = summed
    else:
        old = pay[half, :, 0:16, :]
        pay[half, :, 0:16, :] = jnp.where(lane_of(old.shape) < K, old, summed)


def coefficients_of(full, spread):
    packed = full[:, :, 0:16, :].reshape(NSNAP // 2, LANES)
    turned = packed.T
    if spread is not None:
        for block in range(NBLOCK):
            top = (block // 2) * K
            left = (block % 2) * BLOCK
            high, low = parts(turned[top : top + K, left : left + BLOCK])
            spread[block, 0:K, :] = high
            spread[block, K : 2 * K, :] = low
    return turned


def begin_kernel(
    snap, basis, sea, split_out, flat, top, bottom, first, last, mine, other, split, pay
):
    step = pl.program_id(0)

    @pl.when(step == 0)
    def _():
        pay[...] = jnp.zeros_like(pay)
        for a in range(ROWS):
            value = basis[pl.ds(a, K, stride=ROWS), :] * sea[a : a + 1, :].astype(F32)
            flat[:, cols(a)] = value
            store_split(split, a, value)
        top[...] = flat[:, cols(0)]
        bottom[...] = flat[:, cols(ROWS - 1)]
        first[...], last[...] = edge_columns(flat)

    for a in range(ROWS):
        high, low = parts(snap[pl.ds(a, BLOCK, stride=ROWS), :])
        split_out[0, 0, :, cols(a)] = high
        split_out[0, 1, :, cols(a)] = low
    both = dot_nt(split_out[0].reshape(2 * BLOCK, PTS), split[...])
    both = both[0:BLOCK] + both[BLOCK : 2 * BLOCK]
    summed = (both + pltpu.roll(both, K, 1)).reshape(16, 16, LANES)
    half = step % 2
    keep = (lane_of(summed.shape) < K) & (step >= 2)
    pay[half, :, 0:16, :] = jnp.where(keep, pay[half, :, 0:16, :], summed)

    @pl.when(step == pl.num_programs(0) - 1)
    def _():
        hand_out(pay, mine, other)


def whole(shape):
    return pl.BlockSpec(shape, lambda i: (0,) * len(shape))


def begin(snapshots, basis, sea):
    halo = jax.ShapeDtypeStruct((K, LANES), F32)
    share = jax.ShapeDtypeStruct((16, DEPTH, LANES), F32)
    return pl.pallas_call(
        begin_kernel,
        grid=(NBLOCK,),
        in_specs=[
            pl.BlockSpec((BLOCK * ROWS, LANES), lambda i: (i, 0)),
            whole((K * ROWS, LANES)),
            whole((ROWS, LANES)),
        ],
        out_specs=[
            pl.BlockSpec((1, 2, BLOCK, PTS), lambda i: (i, 0, 0, 0)),
            whole((K, PTS)),
            *[whole((K, LANES))] * 4,
            *[whole((16, DEPTH, LANES))] * 2,
        ],
        out_shape=[
            jax.ShapeDtypeStruct((NBLOCK, 2, BLOCK, PTS), BF16),
            jax.ShapeDtypeStruct((K, PTS), F32),
            halo,
            halo,
            halo,
            halo,
            share,
            share,
        ],
        scratch_shapes=[
            pltpu.VMEM((2 * K, PTS), BF16),
            pltpu.VMEM((2, 16, DEPTH, LANES), F32),
        ],
        compiler_params=pltpu.CompilerParams(vmem_limit_bytes=VMEM_LIMIT),
        name="split_and_project",
    )(snapshots.reshape(NSNAP * ROWS, LANES), basis.reshape(K * ROWS, LANES), sea)


def copy_of(snap, held, sems, block):
    return pltpu.make_async_copy(snap.at[block], held.at[block], sems.at[block])


def begin_copies(snap, held, sems):
    for block in range(NBLOCK):
        copy_of(snap, held, sems, block).start()


def expand(spread, snap, held, sems, total):
    width = 512
    for block in range(NBLOCK):
        copy_of(snap, held, sems, block).wait()
        for left in range(0, PTS, width):
            at = slice(left, left + width)
            both = dot_nn(spread[block], held[block, 0, :, at]) + dot_nn(
                spread[block], held[block, 1, :, at]
            )
            piece = both[0:K] + both[K : 2 * K]
            total[:, at] = piece if block == 0 else total[:, at] + piece


def project(held, split, pay, arrive=None):
    for block in range(NBLOCK):
        if arrive is not None:
            arrive(block)
        both = dot_nt(held[block].reshape(2 * BLOCK, PTS), split[...])
        put_coefficients(pay, block, both[0:BLOCK] + both[BLOCK : 2 * BLOCK])


def applied_field(total, prev, sides, sea, pen, out):
    north, south, west, east = (side[...] for side in sides)
    for a in range(ROWS):
        lap = smooth(prev, a, north, south, west, east)
        mask = sea[a : a + 1, :].astype(F32)
        out[:, cols(a)] = mask * (total[:, cols(a)] * (1.0 / NPTS) + pen[a : a + 1, :] * lap)


def first_kernel(
    got_mine, got_other, snap, prev, north, south, west, east, sea, pen,
    field, top, bottom, first, last, mine, other,
    full, held, spread, total, split, pay, sems,
):
    begin_copies(snap, held, sems)
    take_in(got_mine, got_other, full)
    coefficients_of(full, spread)
    expand(spread, snap, held, sems, total)
    applied_field(total, prev, (north, south, west, east), sea, pen, field)
    for a in range(ROWS):
        store_split(split, a, field[:, cols(a)])
    top[...] = field[:, cols(0)]
    bottom[...] = field[:, cols(ROWS - 1)]
    first[...], last[...] = edge_columns(field)
    pay[...] = jnp.zeros_like(pay)
    put_square(pay, 16, folded(dot_nt(split[...], split[...])))
    project(held, split, pay)
    hand_out(pay, mine, other)


def scratch_for_expand(depth):
    return [
        pltpu.VMEM((2, 16, depth, LANES), F32),
        pltpu.VMEM((NBLOCK, 2, BLOCK, PTS), BF16),
        pltpu.VMEM((NBLOCK, 2 * K, BLOCK), BF16),
        pltpu.VMEM((K, PTS), F32),
    ]


VM = pl.BlockSpec(memory_space=pltpu.VMEM)
HB = pl.BlockSpec(memory_space=pl.ANY)


def first_step(got, snap, prev, sides, sea, pen):
    halo = jax.ShapeDtypeStruct((K, LANES), F32)
    share = jax.ShapeDtypeStruct((16, SHARD, LANES), F32)
    return pl.pallas_call(
        first_kernel,
        in_specs=[VM, VM, HB, *[VM] * 7],
        out_specs=[VM] * 7,
        out_shape=[jax.ShapeDtypeStruct((K, PTS), F32), halo, halo, halo, halo, share, share],
        scratch_shapes=[
            *scratch_for_expand(DEPTH),
            pltpu.VMEM((2 * K, PTS), BF16),
            pltpu.VMEM((2, 16, SHARD, LANES), F32),
            pltpu.SemaphoreType.DMA((NBLOCK,)),
        ],
        compiler_params=pltpu.CompilerParams(vmem_limit_bytes=VMEM_LIMIT),
        name="expand_and_project",
    )(*got, snap, prev, *sides, sea, pen)


def second_kernel(
    got_mine, got_other, snap, prev, north, south, west, east, sea, pen,
    field, bottom, last,
    full, held, spread, total, raw, sems,
):
    begin_copies(snap, held, sems)
    take_in(got_mine, got_other, full)
    coefficients_of(full, spread)
    inverse = inverse_factor(square_of(full, 16))
    expand(spread, snap, held, sems, total)
    applied_field(total, prev, (north, south, west, east), sea, pen, raw)
    field[...] = dot_nn(inverse, raw[...], HIGHEST)
    bottom[0:K, :] = field[:, cols(ROWS - 1)]
    bottom[K : 2 * K, :] = field[:, cols(ROWS - 1)] * pen[ROWS - 1 : ROWS, :]
    _, last[0:K, :] = edge_columns(field)
    for a in range(ROWS):
        raw[:, cols(a)] = field[:, cols(a)] * pen[a : a + 1, :]
    _, last[K : 2 * K, :] = edge_columns(raw)


def second_step(got, snap, prev, sides, sea, pen):
    halo = jax.ShapeDtypeStruct((2 * K, LANES), F32)
    return pl.pallas_call(
        second_kernel,
        in_specs=[VM, VM, HB, *[VM] * 7],
        out_specs=[VM] * 3,
        out_shape=[jax.ShapeDtypeStruct((K, PTS), F32), halo, halo],
        scratch_shapes=[
            *scratch_for_expand(SHARD),
            pltpu.VMEM((K, PTS), F32),
            pltpu.SemaphoreType.DMA((NBLOCK,)),
        ],
        compiler_params=pltpu.CompilerParams(vmem_limit_bytes=VMEM_LIMIT),
        name="factor_and_expand",
    )(*got, snap, prev, *sides, sea, pen)


def project_kernel(snap, field, pay, held, split, sems):
    begin_copies(snap, held, sems)
    for a in range(ROWS):
        store_split(split, a, field[:, cols(a)])
    pay[...] = jnp.zeros_like(pay)
    put_square(pay, 16, folded(dot_nt(split[...], split[...])))
    project(held, split, pay, lambda block: copy_of(snap, held, sems, block).wait())


def project_step(snap, field):
    return pl.pallas_call(
        project_kernel,
        in_specs=[HB, VM],
        out_specs=VM,
        out_shape=jax.ShapeDtypeStruct((2, 16, SHARD, LANES), F32),
        scratch_shapes=[
            pltpu.VMEM((NBLOCK, 2, BLOCK, PTS), BF16),
            pltpu.VMEM((2 * K, PTS), BF16),
            pltpu.SemaphoreType.DMA((NBLOCK,)),
        ],
        compiler_params=pltpu.CompilerParams(vmem_limit_bytes=VMEM_LIMIT),
        name="project",
    )(snap, field)


def rough_kernel(field, north, west, pen, base, mine, other, left, right, pay):
    def put(at, first, second):
        high, low = parts(first)
        left[0:K, cols(at)] = high
        left[K : 2 * K, cols(at)] = low
        high, low = parts(second)
        right[0:K, cols(at)] = high
        right[K : 2 * K, cols(at)] = low

    first = jnp.zeros((K, LANES), F32)
    first_weighted = jnp.zeros((K, LANES), F32)
    lane = lane_of((K, LANES))
    for a in range(ROWS):
        here = field[:, cols(a)]
        weighted = here * pen[a : a + 1, :]
        put(a, weighted, smooth(field, a, None, None, None, None))
        first = jnp.where(lane == a, here[:, 0:1], first)
        first_weighted = jnp.where(lane == a, weighted[:, 0:1], first_weighted)
        if a == 0:
            put(ROWS, weighted, north[0:K, :])
            put(ROWS + 1, north[K : 2 * K, :], here)
    put(ROWS + 2, first_weighted, west[0:K, :])
    put(ROWS + 3, west[K : 2 * K, :], first)
    pay[...] = base[...]
    put_square(pay, 17, folded(dot_nt(left[...], right[...])))
    hand_out(pay, mine, other)


def rough_step(field, north, west, pen, base):
    share = jax.ShapeDtypeStruct((16, SHARD, LANES), F32)
    return pl.pallas_call(
        rough_kernel,
        in_specs=[VM] * 5,
        out_specs=[VM] * 2,
        out_shape=[share, share],
        scratch_shapes=[
            pltpu.VMEM((2 * K, PTS + 4 * LANES), BF16),
            pltpu.VMEM((2 * K, PTS + 4 * LANES), BF16),
            pltpu.VMEM((2, 16, SHARD, LANES), F32),
        ],
        compiler_params=pltpu.CompilerParams(vmem_limit_bytes=SMALL_LIMIT),
        name="roughness_products",
    )(field, north, west, pen, base)


def last_kernel(got_mine, got_other, field, basis, matrix, full):
    take_in(got_mine, got_other, full)
    inverse = inverse_factor(square_of(full, 16))
    solved = dot_nn(inverse, field[...], HIGHEST)
    for a in range(ROWS):
        basis[pl.ds(a, K, stride=ROWS), :] = solved[:, cols(a)]
    turned = coefficients_of(full, None)
    rough = square_of(full, 17)[:, 0:K]
    low, high = turned[0:K], turned[K : 2 * K]
    gram = dot_nt(low, low, HIGHEST) + dot_nt(high, high, HIGHEST)
    middle = (gram * (1.0 / NPTS) + rough) * (1.0 / NPTS)
    matrix[...] = dot_nt(dot_nn(inverse, middle, HIGHEST), inverse, HIGHEST)


def last_step(got, field):
    basis, matrix = pl.pallas_call(
        last_kernel,
        in_specs=[VM] * 3,
        out_specs=[VM] * 2,
        out_shape=[
            jax.ShapeDtypeStruct((K * ROWS, LANES), F32),
            jax.ShapeDtypeStruct((K, K), F32),
        ],
        scratch_shapes=[pltpu.VMEM((2, 16, SHARD, LANES), F32)],
        compiler_params=pltpu.CompilerParams(vmem_limit_bytes=SMALL_LIMIT),
        name="factor_and_finish",
    )(*got, field)
    return basis.reshape(K, ROWS, LANES), matrix


def exchange(value, axis):
    return lax.all_to_all(value, axis, 0, 0, tiled=True)


def copies(value, count):
    return jnp.broadcast_to(value[None], (count, *value.shape))


def summed_everywhere(mine, other, edges=None):
    sides = None
    pair = mine + lax.ppermute(other, "core", SWAP)
    if edges is not None:
        pair, edges = lax.optimization_barrier((pair, edges))
        sides = sides_of(*edges)
    shares = exchange(pair, CHIPS)
    if edges is not None:
        shares, sides = lax.optimization_barrier((shares, sides))
    shares = exchange(copies(shares.sum(axis=0), 8), "z")
    half = exchange(copies(shares.sum(axis=0), 16), CHIPS)
    return (half, lax.ppermute(half, "core", SWAP)), sides


def from_below(value, axis, count):
    return lax.ppermute(value, axis, [(i, i + 1) for i in range(count - 1)])


def from_above(value, axis, count):
    return lax.ppermute(value, axis, [(i + 1, i) for i in range(count - 1)])


def sides_of(top, bottom, first, last):
    return (
        from_below(bottom, LAT, 32),
        from_above(top, LAT, 32),
        from_below(last, "z", 8),
        from_above(first, "z", 8),
    )


def local(snapshots, land_sea, penalty, initial_basis):
    snap, start, *edges, mine, other = begin(snapshots, initial_basis, land_sea)
    got, sides = summed_everywhere(mine, other, edges)
    applied, *edges, mine, other = first_step(got, snap, start, sides, land_sea, penalty)
    got, sides = summed_everywhere(mine, other, edges)
    applied, bottom, last = second_step(got, snap, applied, sides, land_sea, penalty)
    north = from_below(bottom, LAT, 32)
    west = from_below(last, "z", 8)
    base = project_step(snap, applied)
    mine, other = rough_step(applied, north, west, penalty, base)
    got, _ = summed_everywhere(mine, other)
    return last_step(got, applied)


def solution(mesh):
    split_mesh = Mesh(mesh.devices.reshape(4, 4, 2, 8), ("y", "x", "core", "z"))
    flat = P(LAT, "z")
    deep = P(None, LAT, "z")
    return jax.shard_map(
        local,
        mesh=split_mesh,
        in_specs=(deep, flat, flat, deep),
        out_specs=(deep, P()),
        check_vma=False,
    )
```

```python
import jax
import jax.numpy as jnp
from jax import lax
from jax.experimental import pallas as pl
from jax.experimental.pallas import tpu as pltpu
from jax.sharding import Mesh, PartitionSpec as P

K = 64
NSNAP = 1024
NPTS = 524288
ROWS = 16
LANES = 128
PTS = ROWS * LANES
BLOCK = 256
NBLOCK = NSNAP // BLOCK
SHARD = 24
DEPTH = 16
F32 = jnp.float32
BF16 = jnp.bfloat16
HIGHEST = lax.Precision.HIGHEST
CHIPS = ("y", "x")
LAT = ("y", "x", "core")
SWAP = [(0, 1), (1, 0)]
CROSS = [pair for i in range(1, 31, 2) for pair in ((i, i + 1), (i + 1, i))]
VMEM_LIMIT = 50 * 1024 * 1024
SMALL_LIMIT = 20 * 1024 * 1024


def parts(value):
    high = value.astype(BF16)
    return high, (value - high.astype(F32)).astype(BF16)


def dot_nt(left, right, precision=None):
    return lax.dot_general(
        left, right, (((1,), (1,)), ((), ())), precision=precision, preferred_element_type=F32
    )


def dot_nn(left, right, precision=None):
    return lax.dot_general(
        left, right, (((1,), (0,)), ((), ())), precision=precision, preferred_element_type=F32
    )


def lane_of(shape):
    return lax.broadcasted_iota(jnp.int32, shape, len(shape) - 1)


def cols(a):
    return slice(a * LANES, (a + 1) * LANES)


def store_split(split_ref, a, value):
    high, low = parts(value)
    split_ref[0:K, cols(a)] = high
    split_ref[K : 2 * K, cols(a)] = low


def edge_columns(field_ref):
    lane = lane_of((K, LANES))
    first = jnp.zeros((K, LANES), F32)
    last = jnp.zeros((K, LANES), F32)
    for a in range(ROWS):
        block = field_ref[:, cols(a)]
        first = jnp.where(lane == a, block[:, 0:1], first)
        last = jnp.where(lane == a, block[:, LANES - 1 : LANES], last)
    return first, last


def packed_columns(strip):
    total = strip[0:8]
    for g in range(1, 8):
        total = total + pltpu.roll(strip[8 * g : 8 * g + 8], 16 * g, 1)
    return total


def unpacked_columns(packed):
    return jnp.concatenate(
        [packed if g == 0 else pltpu.roll(packed, LANES - 16 * g, 1) for g in range(8)], axis=0
    )


def smooth(field_ref, a, north, south, west, east):
    lane = lane_of((K, LANES))
    here = field_ref[:, cols(a)]
    up = field_ref[:, cols(a - 1)] if a > 0 else north
    down = field_ref[:, cols(a + 1)] if a < ROWS - 1 else south
    left = pltpu.roll(here, 1, 1)
    right = pltpu.roll(here, LANES - 1, 1)
    left = jnp.where(lane == 0, 0.0 if west is None else west[:, a : a + 1], left)
    right = jnp.where(lane == LANES - 1, 0.0 if east is None else east[:, a : a + 1], right)
    total = left + right
    if up is not None:
        total = total + up
    if down is not None:
        total = total + down
    return total - 4.0 * here


def hand_out(pay, mine, other):
    me = lax.axis_index("core")
    mine[...] = pay[me]
    depth = pay.shape[2]
    for chip in range(16):
        other[chip * depth : (chip + 1) * depth, :] = pay[1 - me, chip]


def hand_out_edges(field, depth, other, cross, columns):
    me = lax.axis_index("core")
    top = field[:, cols(0)]
    bottom = field[:, cols(ROWS - 1)]
    other[16 * depth : 16 * depth + K, :] = jnp.where(me == 0, bottom, top)
    cross[...] = jnp.where(me == 0, top, bottom)
    first, last = edge_columns(field)
    columns[0:8, :] = packed_columns(first)
    columns[8:16, :] = packed_columns(last)


def take_in_edges(pair, cross, columns):
    me = lax.axis_index("core")
    z = lax.axis_index("z")
    depth = columns.shape[1] - 16
    north = jnp.where(me == 0, cross[...], pair[...])
    south = jnp.where(me == 0, pair[...], cross[...])
    before = columns[jnp.maximum(z - 1, 0), depth + 8 : depth + 16, :]
    after = columns[jnp.minimum(z + 1, 7), depth : depth + 8, :]
    west = unpacked_columns(jnp.where(z > 0, before, 0.0))
    east = unpacked_columns(jnp.where(z < 7, after, 0.0))
    return north, south, west, east


def take_in(mine, other, full):
    me = lax.axis_index("core")
    full[me] = mine[...]
    full[1 - me] = other[...]


def row_of_shards(full, row):
    return jnp.concatenate(
        [full[half, chip, row : row + 1, :] for half in range(2) for chip in range(16)], axis=0
    )


def put_square(pay, row, doubled):
    packed = jnp.where(lane_of((K // 2, LANES)) < K, doubled[0 : K // 2], doubled[K // 2 : K])
    for half in range(2):
        for chip in range(16):
            at = half * 16 + chip
            pay[half, chip, row : row + 1, :] = packed[at : at + 1]


def square_of(full, row):
    packed = row_of_shards(full, row)
    return jnp.concatenate([packed, pltpu.roll(packed, K, 1)], axis=0)


def folded(product):
    rows = product[0:K] + product[K : 2 * K]
    return rows + pltpu.roll(rows, K, 1)


def inverse_factor(square):
    lane = lane_of((8, LANES))
    sub = lax.broadcasted_iota(jnp.int32, (8, LANES), 0)
    count = K // 8
    held = []
    for b in range(count):
        unit = jnp.where(lane - K == sub + 8 * b, 1.0, 0.0)
        held.append(jnp.where(lane < K, square[8 * b : 8 * b + 8] * (1.0 / NPTS), unit))
    for home in range(count):
        columns = [
            [
                jnp.broadcast_to(held[b][:, 8 * home + q : 8 * home + q + 1], (8, LANES))
                for b in range(home, count)
            ]
            for q in range(8)
        ]
        rows, scales = [], []
        for q in range(8):
            inverse = 1.0 / columns[q][0][q : q + 1, :]
            row = held[home][q : q + 1, :]
            scale = [column * inverse for column in columns[q]]
            scale[0] = jnp.where(sub > q, scale[0], 0.0)
            if q < 7:
                held[home] = held[home] - scale[0] * row
            for p in range(q + 1, 8):
                entry = columns[p][0][q : q + 1, :]
                columns[p] = [c - m * entry for c, m in zip(columns[p], scale)]
            rows.append(row)
            scales.append(scale)
        for at, b in enumerate(range(home + 1, count), 1):
            update = scales[0][at] * rows[0]
            for q in range(1, 8):
                update = update + scales[q][at] * rows[q]
            held[b] = held[b] - update
    done = []
    for b in range(count):
        diagonal = jnp.sum(jnp.where(lane == sub + 8 * b, held[b], 0.0), axis=1, keepdims=True)
        done.append(held[b] * lax.rsqrt(diagonal))
    return pltpu.roll(jnp.concatenate(done, axis=0), K, 1)[:, 0:K]


def put_coefficients(pay, block, both):
    half = block % 2
    summed = both + pltpu.roll(both, K, 1)
    summed = summed.reshape(16, 16, LANES)
    if block < 2:
        pay[half, :, 0:16, :] = summed
    else:
        old = pay[half, :, 0:16, :]
        pay[half, :, 0:16, :] = jnp.where(lane_of(old.shape) < K, old, summed)


def coefficients_of(full, spread):
    packed = full[:, :, 0:16, :].reshape(NSNAP // 2, LANES)
    turned = packed.T
    if spread is not None:
        for block in range(NBLOCK):
            top = (block // 2) * K
            left = (block % 2) * BLOCK
            high, low = parts(turned[top : top + K, left : left + BLOCK])
            spread[block, 0:K, :] = high
            spread[block, K : 2 * K, :] = low
    return turned


def begin_kernel(
    snap, basis, sea, snap_out, flat, mine, other, cross, columns,
    raw, held, split, pay, in_sems, out_sems,
):
    deep = BLOCK // 2

    def arrive(piece):
        span = pl.ds(piece * deep * ROWS, deep * ROWS)
        return pltpu.make_async_copy(snap.at[span], raw.at[span], in_sems.at[piece])

    def leave(piece):
        at = (piece // 2, slice(None), pl.ds((piece % 2) * deep, deep))
        return pltpu.make_async_copy(held.at[at], snap_out.at[at], out_sems.at[piece])

    for piece in range(2 * NBLOCK):
        arrive(piece).start()
    for a in range(ROWS):
        value = basis[pl.ds(a, K, stride=ROWS), :] * sea[a : a + 1, :].astype(F32)
        flat[:, cols(a)] = value
        store_split(split, a, value)
    hand_out_edges(flat, DEPTH, other, cross, columns)
    for block in range(NBLOCK):
        for piece in (2 * block, 2 * block + 1):
            arrive(piece).wait()
            span = slice((piece % 2) * deep, (piece % 2 + 1) * deep)
            for a in range(ROWS):
                high, low = parts(raw[pl.ds(piece * deep * ROWS + a, deep, stride=ROWS), :])
                held[block, 0, span, cols(a)] = high
                held[block, 1, span, cols(a)] = low
            leave(piece).start()
        both = dot_nt(held[block].reshape(2 * BLOCK, PTS), split[...])
        put_coefficients(pay, block, both[0:BLOCK] + both[BLOCK : 2 * BLOCK])
    hand_out(pay, mine, other)
    for piece in range(2 * NBLOCK):
        leave(piece).wait()


VM = pl.BlockSpec(memory_space=pltpu.VMEM)
HB = pl.BlockSpec(memory_space=pl.ANY)


def shared_outputs(depth):
    return [
        jax.ShapeDtypeStruct((K, PTS), F32),
        jax.ShapeDtypeStruct((16, depth, LANES), F32),
        jax.ShapeDtypeStruct((16 * depth + K, LANES), F32),
        jax.ShapeDtypeStruct((K, LANES), F32),
        jax.ShapeDtypeStruct((16, LANES), F32),
    ]


def begin(snapshots, basis, sea):
    return pl.pallas_call(
        begin_kernel,
        in_specs=[HB, VM, VM],
        out_specs=[HB, *[VM] * 5],
        out_shape=[jax.ShapeDtypeStruct((NBLOCK, 2, BLOCK, PTS), BF16), *shared_outputs(DEPTH)],
        scratch_shapes=[
            pltpu.VMEM((NSNAP * ROWS, LANES), F32),
            pltpu.VMEM((NBLOCK, 2, BLOCK, PTS), BF16),
            pltpu.VMEM((2 * K, PTS), BF16),
            pltpu.VMEM((2, 16, DEPTH, LANES), F32),
            pltpu.SemaphoreType.DMA((2 * NBLOCK,)),
            pltpu.SemaphoreType.DMA((2 * NBLOCK,)),
        ],
        compiler_params=pltpu.CompilerParams(vmem_limit_bytes=VMEM_LIMIT),
        name="split_and_project",
    )(snapshots.reshape(NSNAP * ROWS, LANES), basis.reshape(K * ROWS, LANES), sea)


def copy_of(snap, held, sems, block):
    return pltpu.make_async_copy(snap.at[block], held.at[block], sems.at[block])


def begin_copies(snap, held, sems):
    for block in range(NBLOCK):
        copy_of(snap, held, sems, block).start()


def expand(spread, snap, held, sems, total):
    width = 512
    for block in range(NBLOCK):
        copy_of(snap, held, sems, block).wait()
        for left in range(0, PTS, width):
            at = slice(left, left + width)
            both = dot_nn(spread[block], held[block, 0, :, at]) + dot_nn(
                spread[block], held[block, 1, :, at]
            )
            piece = both[0:K] + both[K : 2 * K]
            total[:, at] = piece if block == 0 else total[:, at] + piece


def project(held, split, pay, arrive=None):
    for block in range(NBLOCK):
        if arrive is not None:
            arrive(block)
        both = dot_nt(held[block].reshape(2 * BLOCK, PTS), split[...])
        put_coefficients(pay, block, both[0:BLOCK] + both[BLOCK : 2 * BLOCK])


def applied_field(total, prev, sides, sea, pen, out):
    north, south, west, east = sides
    for a in range(ROWS):
        lap = smooth(prev, a, north, south, west, east)
        mask = sea[a : a + 1, :].astype(F32)
        out[:, cols(a)] = mask * (total[:, cols(a)] * (1.0 / NPTS) + pen[a : a + 1, :] * lap)


def first_kernel(
    got_mine, got_other, snap, prev, pair, near, around, sea, pen,
    field, mine, other, cross, columns,
    full, held, spread, total, split, pay, sems,
):
    begin_copies(snap, held, sems)
    take_in(got_mine, got_other, full)
    coefficients_of(full, spread)
    sides = take_in_edges(pair, near, around)
    expand(spread, snap, held, sems, total)
    applied_field(total, prev, sides, sea, pen, field)
    for a in range(ROWS):
        store_split(split, a, field[:, cols(a)])
    hand_out_edges(field, SHARD, other, cross, columns)
    pay[...] = jnp.zeros_like(pay)
    put_square(pay, 16, folded(dot_nt(split[...], split[...])))
    project(held, split, pay)
    hand_out(pay, mine, other)


def scratch_for_expand(depth):
    return [
        pltpu.VMEM((2, 16, depth, LANES), F32),
        pltpu.VMEM((NBLOCK, 2, BLOCK, PTS), BF16),
        pltpu.VMEM((NBLOCK, 2 * K, BLOCK), BF16),
        pltpu.VMEM((K, PTS), F32),
    ]


def first_step(got, snap, prev, sides, sea, pen):
    return pl.pallas_call(
        first_kernel,
        in_specs=[VM, VM, HB, *[VM] * 6],
        out_specs=[VM] * 5,
        out_shape=shared_outputs(SHARD),
        scratch_shapes=[
            *scratch_for_expand(DEPTH),
            pltpu.VMEM((2 * K, PTS), BF16),
            pltpu.VMEM((2, 16, SHARD, LANES), F32),
            pltpu.SemaphoreType.DMA((NBLOCK,)),
        ],
        compiler_params=pltpu.CompilerParams(vmem_limit_bytes=VMEM_LIMIT),
        name="expand_and_project",
    )(*got, snap, prev, *sides, sea, pen)


def second_kernel(
    got_mine, got_other, snap, prev, pair, near, around, sea, pen,
    field, bottom, last,
    full, held, spread, total, raw, sems,
):
    begin_copies(snap, held, sems)
    take_in(got_mine, got_other, full)
    coefficients_of(full, spread)
    inverse = inverse_factor(square_of(full, 16))
    sides = take_in_edges(pair, near, around)
    expand(spread, snap, held, sems, total)
    applied_field(total, prev, sides, sea, pen, raw)
    field[...] = dot_nn(inverse, raw[...], HIGHEST)
    bottom[0:K, :] = field[:, cols(ROWS - 1)]
    bottom[K : 2 * K, :] = field[:, cols(ROWS - 1)] * pen[ROWS - 1 : ROWS, :]
    _, last[0:K, :] = edge_columns(field)
    for a in range(ROWS):
        raw[:, cols(a)] = field[:, cols(a)] * pen[a : a + 1, :]
    _, last[K : 2 * K, :] = edge_columns(raw)


def second_step(got, snap, prev, sides, sea, pen):
    halo = jax.ShapeDtypeStruct((2 * K, LANES), F32)
    return pl.pallas_call(
        second_kernel,
        in_specs=[VM, VM, HB, *[VM] * 6],
        out_specs=[VM] * 3,
        out_shape=[jax.ShapeDtypeStruct((K, PTS), F32), halo, halo],
        scratch_shapes=[
            *scratch_for_expand(SHARD),
            pltpu.VMEM((K, PTS), F32),
            pltpu.SemaphoreType.DMA((NBLOCK,)),
        ],
        compiler_params=pltpu.CompilerParams(vmem_limit_bytes=VMEM_LIMIT),
        name="factor_and_expand",
    )(*got, snap, prev, *sides, sea, pen)


def project_kernel(snap, field, pay, held, split, sems):
    begin_copies(snap, held, sems)
    for a in range(ROWS):
        store_split(split, a, field[:, cols(a)])
    pay[...] = jnp.zeros_like(pay)
    put_square(pay, 16, folded(dot_nt(split[...], split[...])))
    project(held, split, pay, lambda block: copy_of(snap, held, sems, block).wait())


def project_step(snap, field):
    return pl.pallas_call(
        project_kernel,
        in_specs=[HB, VM],
        out_specs=VM,
        out_shape=jax.ShapeDtypeStruct((2, 16, SHARD, LANES), F32),
        scratch_shapes=[
            pltpu.VMEM((NBLOCK, 2, BLOCK, PTS), BF16),
            pltpu.VMEM((2 * K, PTS), BF16),
            pltpu.SemaphoreType.DMA((NBLOCK,)),
        ],
        compiler_params=pltpu.CompilerParams(vmem_limit_bytes=VMEM_LIMIT),
        name="project",
    )(snap, field)


def rough_kernel(field, north, west, pen, base, mine, other, left, right, pay):
    def put(at, first, second):
        high, low = parts(first)
        left[0:K, cols(at)] = high
        left[K : 2 * K, cols(at)] = low
        high, low = parts(second)
        right[0:K, cols(at)] = high
        right[K : 2 * K, cols(at)] = low

    first = jnp.zeros((K, LANES), F32)
    first_weighted = jnp.zeros((K, LANES), F32)
    lane = lane_of((K, LANES))
    for a in range(ROWS):
        here = field[:, cols(a)]
        weighted = here * pen[a : a + 1, :]
        put(a, weighted, smooth(field, a, None, None, None, None))
        first = jnp.where(lane == a, here[:, 0:1], first)
        first_weighted = jnp.where(lane == a, weighted[:, 0:1], first_weighted)
        if a == 0:
            put(ROWS, weighted, north[0:K, :])
            put(ROWS + 1, north[K : 2 * K, :], here)
    put(ROWS + 2, first_weighted, west[0:K, :])
    put(ROWS + 3, west[K : 2 * K, :], first)
    pay[...] = base[...]
    put_square(pay, 17, folded(dot_nt(left[...], right[...])))
    hand_out(pay, mine, other)


def rough_step(field, north, west, pen, base):
    return pl.pallas_call(
        rough_kernel,
        in_specs=[VM] * 5,
        out_specs=[VM] * 2,
        out_shape=[
            jax.ShapeDtypeStruct((16, SHARD, LANES), F32),
            jax.ShapeDtypeStruct((16 * SHARD, LANES), F32),
        ],
        scratch_shapes=[
            pltpu.VMEM((2 * K, PTS + 4 * LANES), BF16),
            pltpu.VMEM((2 * K, PTS + 4 * LANES), BF16),
            pltpu.VMEM((2, 16, SHARD, LANES), F32),
        ],
        compiler_params=pltpu.CompilerParams(vmem_limit_bytes=SMALL_LIMIT),
        name="roughness_products",
    )(field, north, west, pen, base)


def last_kernel(got_mine, got_other, field, basis, matrix, full):
    take_in(got_mine, got_other, full)
    inverse = inverse_factor(square_of(full, 16))
    solved = dot_nn(inverse, field[...], HIGHEST)
    for a in range(ROWS):
        basis[pl.ds(a, K, stride=ROWS), :] = solved[:, cols(a)]
    turned = coefficients_of(full, None)
    rough = square_of(full, 17)[:, 0:K]
    low, high = turned[0:K], turned[K : 2 * K]
    gram = dot_nt(low, low, HIGHEST) + dot_nt(high, high, HIGHEST)
    middle = (gram * (1.0 / NPTS) + rough) * (1.0 / NPTS)
    matrix[...] = dot_nt(dot_nn(inverse, middle, HIGHEST), inverse, HIGHEST)


def last_step(got, field):
    basis, matrix = pl.pallas_call(
        last_kernel,
        in_specs=[VM] * 3,
        out_specs=[VM] * 2,
        out_shape=[
            jax.ShapeDtypeStruct((K * ROWS, LANES), F32),
            jax.ShapeDtypeStruct((K, K), F32),
        ],
        scratch_shapes=[pltpu.VMEM((2, 16, SHARD, LANES), F32)],
        compiler_params=pltpu.CompilerParams(vmem_limit_bytes=SMALL_LIMIT),
        name="factor_and_finish",
    )(*got, field)
    return basis.reshape(K, ROWS, LANES), matrix


def exchange(value, axis):
    return lax.all_to_all(value, axis, 0, 0, tiled=True)


def copies(value, count):
    return jnp.broadcast_to(value[None], (count, *value.shape))


def summed_everywhere(mine, other, edges=None):
    depth = mine.shape[1]
    got = lax.ppermute(other, "core", SWAP)
    pair = mine + got[: 16 * depth].reshape(mine.shape)
    if edges is not None:
        cross, columns = edges
        pair, cross = lax.optimization_barrier((pair, cross))
        near = lax.ppermute(cross, LAT, CROSS)
    shares = exchange(pair, CHIPS)
    if edges is not None:
        shares, near = lax.optimization_barrier((shares, near))
    share = shares.sum(axis=0)
    if edges is not None:
        share = jnp.concatenate([share, columns], axis=0)
    around = exchange(copies(share, 8), "z")
    half = exchange(copies(around[:, :depth].sum(axis=0), 16), CHIPS)
    both = (half, lax.ppermute(half, "core", SWAP))
    if edges is None:
        return both, None
    return both, (got[16 * depth :], near, around)


def from_below(value, axis, count):
    return lax.ppermute(value, axis, [(i, i + 1) for i in range(count - 1)])


def local(snapshots, land_sea, penalty, initial_basis):
    snap, start, mine, other, *edges = begin(snapshots, initial_basis, land_sea)
    got, sides = summed_everywhere(mine, other, edges)
    applied, mine, other, *edges = first_step(got, snap, start, sides, land_sea, penalty)
    got, sides = summed_everywhere(mine, other, edges)
    applied, bottom, last = second_step(got, snap, applied, sides, land_sea, penalty)
    north = from_below(bottom, LAT, 32)
    west = from_below(last, "z", 8)
    base = project_step(snap, applied)
    mine, other = rough_step(applied, north, west, penalty, base)
    got, _ = summed_everywhere(mine, other)
    return last_step(got, applied)


def solution(mesh):
    split_mesh = Mesh(mesh.devices.reshape(4, 4, 2, 8), ("y", "x", "core", "z"))
    flat = P(LAT, "z")
    deep = P(None, LAT, "z")
    return jax.shard_map(
        local,
        mesh=split_mesh,
        in_specs=(deep, flat, flat, deep),
        out_specs=(deep, P()),
        check_vma=False,
    )
```

```python
import jax
import jax.numpy as jnp
from jax import lax
from jax.experimental import pallas as pl
from jax.experimental.pallas import tpu as pltpu
from jax.sharding import Mesh, PartitionSpec as P

K = 64
NSNAP = 1024
NPTS = 524288
ROWS = 16
LANES = 128
PTS = ROWS * LANES
BLOCK = 256
NBLOCK = NSNAP // BLOCK
SHARD = 24
DEPTH = 16
F32 = jnp.float32
BF16 = jnp.bfloat16
HIGHEST = lax.Precision.HIGHEST
CHIPS = ("y", "x")
LAT = ("y", "x", "core")
SWAP = [(0, 1), (1, 0)]
CROSS = [pair for i in range(1, 31, 2) for pair in ((i, i + 1), (i + 1, i))]
VMEM_LIMIT = 50 * 1024 * 1024
MIDDLE_LIMIT = 36 * 1024 * 1024
SMALL_LIMIT = 20 * 1024 * 1024


def parts(value):
    high = value.astype(BF16)
    return high, (value - high.astype(F32)).astype(BF16)


def dot_nt(left, right, precision=None):
    return lax.dot_general(
        left, right, (((1,), (1,)), ((), ())), precision=precision, preferred_element_type=F32
    )


def dot_nn(left, right, precision=None):
    return lax.dot_general(
        left, right, (((1,), (0,)), ((), ())), precision=precision, preferred_element_type=F32
    )


def lane_of(shape):
    return lax.broadcasted_iota(jnp.int32, shape, len(shape) - 1)


def cols(a):
    return slice(a * LANES, (a + 1) * LANES)


def store_split(split_ref, a, value):
    high, low = parts(value)
    split_ref[0:K, cols(a)] = high
    split_ref[K : 2 * K, cols(a)] = low


def edge_columns(field_ref):
    lane = lane_of((K, LANES))
    first = jnp.zeros((K, LANES), F32)
    last = jnp.zeros((K, LANES), F32)
    for a in range(ROWS):
        block = field_ref[:, cols(a)]
        first = jnp.where(lane == a, block[:, 0:1], first)
        last = jnp.where(lane == a, block[:, LANES - 1 : LANES], last)
    return first, last


def packed_columns(strip):
    total = strip[0:8]
    for g in range(1, 8):
        total = total + pltpu.roll(strip[8 * g : 8 * g + 8], 16 * g, 1)
    return total


def unpacked_columns(packed):
    return jnp.concatenate(
        [packed if g == 0 else pltpu.roll(packed, LANES - 16 * g, 1) for g in range(8)], axis=0
    )


def smooth(field_ref, a, north, south, west, east):
    lane = lane_of((K, LANES))
    here = field_ref[:, cols(a)]
    up = field_ref[:, cols(a - 1)] if a > 0 else north
    down = field_ref[:, cols(a + 1)] if a < ROWS - 1 else south
    left = pltpu.roll(here, 1, 1)
    right = pltpu.roll(here, LANES - 1, 1)
    left = jnp.where(lane == 0, 0.0 if west is None else west[:, a : a + 1], left)
    right = jnp.where(lane == LANES - 1, 0.0 if east is None else east[:, a : a + 1], right)
    total = left + right
    if up is not None:
        total = total + up
    if down is not None:
        total = total + down
    return total - 4.0 * here


def hand_out(pay, mine, other):
    me = lax.axis_index("core")
    mine[...] = pay[me]
    depth = pay.shape[2]
    for chip in range(16):
        other[chip * depth : (chip + 1) * depth, :] = pay[1 - me, chip]


def hand_out_edges(field, depth, other, cross, columns):
    me = lax.axis_index("core")
    top = field[:, cols(0)]
    bottom = field[:, cols(ROWS - 1)]
    other[16 * depth : 16 * depth + K, :] = jnp.where(me == 0, bottom, top)
    cross[...] = jnp.where(me == 0, top, bottom)
    first, last = edge_columns(field)
    columns[0:8, :] = packed_columns(first)
    columns[8:16, :] = packed_columns(last)


def take_in_edges(pair, cross, columns):
    me = lax.axis_index("core")
    z = lax.axis_index("z")
    depth = columns.shape[1] - 16
    north = jnp.where(me == 0, cross[...], pair[...])
    south = jnp.where(me == 0, pair[...], cross[...])
    before = columns[jnp.maximum(z - 1, 0), depth + 8 : depth + 16, :]
    after = columns[jnp.minimum(z + 1, 7), depth : depth + 8, :]
    west = unpacked_columns(jnp.where(z > 0, before, 0.0))
    east = unpacked_columns(jnp.where(z < 7, after, 0.0))
    return north, south, west, east


def take_in(mine, other, full):
    me = lax.axis_index("core")
    full[me] = mine[...]
    full[1 - me] = other[...]


def row_of_shards(full, row):
    return jnp.concatenate(
        [full[half, chip, row : row + 1, :] for half in range(2) for chip in range(16)], axis=0
    )


def put_square(pay, row, doubled):
    packed = jnp.where(lane_of((K // 2, LANES)) < K, doubled[0 : K // 2], doubled[K // 2 : K])
    for half in range(2):
        for chip in range(16):
            at = half * 16 + chip
            pay[half, chip, row : row + 1, :] = packed[at : at + 1]


def square_of(full, row):
    packed = row_of_shards(full, row)
    return jnp.concatenate([packed, pltpu.roll(packed, K, 1)], axis=0)


def folded(product):
    rows = product[0:K] + product[K : 2 * K]
    return rows + pltpu.roll(rows, K, 1)


def inverse_factor(square):
    lane = lane_of((8, LANES))
    sub = lax.broadcasted_iota(jnp.int32, (8, LANES), 0)
    count = K // 8
    held = []
    for b in range(count):
        unit = jnp.where(lane - K == sub + 8 * b, 1.0, 0.0)
        held.append(jnp.where(lane < K, square[8 * b : 8 * b + 8] * (1.0 / NPTS), unit))
    for home in range(count):
        columns = [
            [
                jnp.broadcast_to(held[b][:, 8 * home + q : 8 * home + q + 1], (8, LANES))
                for b in range(home, count)
            ]
            for q in range(8)
        ]
        rows, scales = [], []
        for q in range(8):
            inverse = 1.0 / columns[q][0][q : q + 1, :]
            row = held[home][q : q + 1, :]
            scale = [column * inverse for column in columns[q]]
            scale[0] = jnp.where(sub > q, scale[0], 0.0)
            if q < 7:
                held[home] = held[home] - scale[0] * row
            for p in range(q + 1, 8):
                entry = columns[p][0][q : q + 1, :]
                columns[p] = [c - m * entry for c, m in zip(columns[p], scale)]
            rows.append(row)
            scales.append(scale)
        for at, b in enumerate(range(home + 1, count), 1):
            update = scales[0][at] * rows[0]
            for q in range(1, 8):
                update = update + scales[q][at] * rows[q]
            held[b] = held[b] - update
    done = []
    for b in range(count):
        diagonal = jnp.sum(jnp.where(lane == sub + 8 * b, held[b], 0.0), axis=1, keepdims=True)
        done.append(held[b] * lax.rsqrt(diagonal))
    return pltpu.roll(jnp.concatenate(done, axis=0), K, 1)[:, 0:K]


def put_coefficients(pay, block, held, split):
    both = dot_nt(split[...], held[block].reshape(2 * BLOCK, PTS))
    rows = both[0:K] + both[K : 2 * K]
    turned = rows[:, 0:BLOCK] + rows[:, BLOCK : 2 * BLOCK]
    for part in range(BLOCK // LANES):
        at = block * (BLOCK // LANES) + part
        chips = slice(4 * (at % 4), 4 * (at % 4) + 4)
        pay[at // 4, chips, 0:16, :] = turned[:, cols(part)].reshape(4, 16, LANES)


def coefficients_of(full, at):
    chips = slice(4 * (at % 4), 4 * (at % 4) + 4)
    return full[at // 4, chips, 0:16, :].reshape(K, LANES)


def spread_coefficients(full, spread):
    for block in range(NBLOCK):
        for part in range(BLOCK // LANES):
            high, low = parts(coefficients_of(full, block * (BLOCK // LANES) + part))
            spread[block, 0:K, cols(part)] = high
            spread[block, K : 2 * K, cols(part)] = low


def begin_kernel(
    snap, basis, sea, snap_out, flat, mine, other, cross, columns,
    raw, held, split, pay, in_sems, out_sems,
):
    deep = BLOCK // 2

    def arrive(piece):
        span = pl.ds(piece * deep * ROWS, deep * ROWS)
        return pltpu.make_async_copy(snap.at[span], raw.at[span], in_sems.at[piece])

    def leave(piece):
        at = (piece // 2, slice(None), pl.ds((piece % 2) * deep, deep))
        return pltpu.make_async_copy(held.at[at], snap_out.at[at], out_sems.at[piece])

    for piece in range(2 * NBLOCK):
        arrive(piece).start()
    for a in range(ROWS):
        value = basis[pl.ds(a, K, stride=ROWS), :] * sea[a : a + 1, :].astype(F32)
        flat[:, cols(a)] = value
        store_split(split, a, value)
    hand_out_edges(flat, DEPTH, other, cross, columns)
    for block in range(NBLOCK):
        for piece in (2 * block, 2 * block + 1):
            arrive(piece).wait()
            span = slice((piece % 2) * deep, (piece % 2 + 1) * deep)
            for a in range(ROWS):
                high, low = parts(raw[pl.ds(piece * deep * ROWS + a, deep, stride=ROWS), :])
                held[block, 0, span, cols(a)] = high
                held[block, 1, span, cols(a)] = low
            leave(piece).start()
        put_coefficients(pay, block, held, split)
    hand_out(pay, mine, other)
    for piece in range(2 * NBLOCK):
        leave(piece).wait()


VM = pl.BlockSpec(memory_space=pltpu.VMEM)
HB = pl.BlockSpec(memory_space=pl.ANY)


def shared_outputs(depth):
    return [
        jax.ShapeDtypeStruct((K, PTS), F32),
        jax.ShapeDtypeStruct((16, depth, LANES), F32),
        jax.ShapeDtypeStruct((16 * depth + K, LANES), F32),
        jax.ShapeDtypeStruct((K, LANES), F32),
        jax.ShapeDtypeStruct((16, LANES), F32),
    ]


def begin(snapshots, basis, sea):
    return pl.pallas_call(
        begin_kernel,
        in_specs=[HB, VM, VM],
        out_specs=[HB, *[VM] * 5],
        out_shape=[
            jax.ShapeDtypeStruct((2 * NBLOCK, 2, BLOCK, PTS), BF16),
            *shared_outputs(DEPTH),
        ],
        scratch_shapes=[
            pltpu.VMEM((NSNAP * ROWS, LANES), F32),
            pltpu.VMEM((NBLOCK, 2, BLOCK, PTS), BF16),
            pltpu.VMEM((2 * K, PTS), BF16),
            pltpu.VMEM((2, 16, DEPTH, LANES), F32),
            pltpu.SemaphoreType.DMA((2 * NBLOCK,)),
            pltpu.SemaphoreType.DMA((2 * NBLOCK,)),
        ],
        compiler_params=pltpu.CompilerParams(vmem_limit_bytes=VMEM_LIMIT),
        name="split_and_project",
    )(snapshots.reshape(NSNAP * ROWS, LANES), basis.reshape(K * ROWS, LANES), sea)


def copy_of(snap, held, sems, block):
    return pltpu.make_async_copy(snap.at[block], held.at[block], sems.at[block])


def begin_copies(snap, held, sems):
    for block in range(NBLOCK):
        copy_of(snap, held, sems, block).start()


def expand(spread, snap, held, sems, total):
    width = 512
    for block in range(NBLOCK):
        copy_of(snap, held, sems, block).wait()
        for left in range(0, PTS, width):
            at = slice(left, left + width)
            both = dot_nn(spread[block], held[block, 0, :, at]) + dot_nn(
                spread[block], held[block, 1, :, at]
            )
            piece = both[0:K] + both[K : 2 * K]
            total[:, at] = piece if block == 0 else total[:, at] + piece


def project(held, split, pay):
    for block in range(NBLOCK):
        put_coefficients(pay, block, held, split)


def rough_field(prev, sides, pen, out):
    for a in range(ROWS):
        out[:, cols(a)] = pen[a : a + 1, :] * smooth(prev, a, *sides)


def applied_field(total, rough, sea, out):
    for a in range(ROWS):
        mask = sea[a : a + 1, :].astype(F32)
        out[:, cols(a)] = mask * (total[:, cols(a)] * (1.0 / NPTS) + rough[:, cols(a)])


def first_kernel(
    got_mine, got_other, snap, prev, pair, near, around, sea, pen,
    field, mine, other, cross, columns,
    full, spread, total, rough, held, split, pay, sems,
):
    begin_copies(snap, held, sems)
    take_in(got_mine, got_other, full)
    spread_coefficients(full, spread)
    rough_field(prev, take_in_edges(pair, near, around), pen, rough)
    expand(spread, snap, held, sems, total)
    applied_field(total, rough, sea, field)
    for a in range(ROWS):
        store_split(split, a, field[:, cols(a)])
    hand_out_edges(field, SHARD, other, cross, columns)
    pay[...] = jnp.zeros_like(pay)
    put_square(pay, 16, folded(dot_nt(split[...], split[...])))
    project(held, split, pay)
    hand_out(pay, mine, other)


def scratch_for_expand(depth):
    return [
        pltpu.VMEM((2, 16, depth, LANES), F32),
        pltpu.VMEM((NBLOCK, 2 * K, BLOCK), BF16),
        pltpu.VMEM((K, PTS), F32),
        pltpu.VMEM((K, PTS), F32),
    ]


def first_step(got, snap, prev, sides, sea, pen):
    return pl.pallas_call(
        first_kernel,
        in_specs=[VM, VM, HB, *[VM] * 6],
        out_specs=[VM] * 5,
        out_shape=shared_outputs(SHARD),
        scratch_shapes=[
            *scratch_for_expand(DEPTH),
            pltpu.VMEM((NBLOCK, 2, BLOCK, PTS), BF16),
            pltpu.VMEM((2 * K, PTS), BF16),
            pltpu.VMEM((2, 16, SHARD, LANES), F32),
            pltpu.SemaphoreType.DMA((NBLOCK,)),
        ],
        compiler_params=pltpu.CompilerParams(vmem_limit_bytes=VMEM_LIMIT),
        name="expand_and_project",
    )(*got, snap, prev, *sides, sea, pen)


def second_kernel(
    got_mine, got_other, snap, prev, pair, near, around, sea, pen,
    field, bottom, last, held,
    full, spread, total, rough, raw, sems,
):
    begin_copies(snap, held, sems)
    take_in(got_mine, got_other, full)
    spread_coefficients(full, spread)
    inverse = inverse_factor(square_of(full, 16))
    rough_field(prev, take_in_edges(pair, near, around), pen, rough)
    expand(spread, snap, held, sems, total)
    applied_field(total, rough, sea, raw)
    field[...] = dot_nn(inverse, raw[...], HIGHEST)
    bottom[0:K, :] = field[:, cols(ROWS - 1)]
    bottom[K : 2 * K, :] = field[:, cols(ROWS - 1)] * pen[ROWS - 1 : ROWS, :]
    _, last[0:K, :] = edge_columns(field)
    for a in range(ROWS):
        raw[:, cols(a)] = field[:, cols(a)] * pen[a : a + 1, :]
    _, last[K : 2 * K, :] = edge_columns(raw)


def second_step(got, snap, prev, sides, sea, pen):
    halo = jax.ShapeDtypeStruct((2 * K, LANES), F32)
    return pl.pallas_call(
        second_kernel,
        in_specs=[VM, VM, HB, *[VM] * 6],
        out_specs=[VM] * 4,
        out_shape=[
            jax.ShapeDtypeStruct((K, PTS), F32),
            halo,
            halo,
            jax.ShapeDtypeStruct((NBLOCK, 2, BLOCK, PTS), BF16),
        ],
        scratch_shapes=[
            *scratch_for_expand(SHARD),
            pltpu.VMEM((K, PTS), F32),
            pltpu.SemaphoreType.DMA((NBLOCK,)),
        ],
        compiler_params=pltpu.CompilerParams(vmem_limit_bytes=MIDDLE_LIMIT),
        name="factor_and_expand",
    )(*got, snap, prev, *sides, sea, pen)


def project_kernel(held, field, pay, split):
    for a in range(ROWS):
        store_split(split, a, field[:, cols(a)])
    pay[...] = jnp.zeros_like(pay)
    put_square(pay, 16, folded(dot_nt(split[...], split[...])))
    project(held, split, pay)


def project_step(held, field):
    return pl.pallas_call(
        project_kernel,
        in_specs=[VM, VM],
        out_specs=VM,
        out_shape=jax.ShapeDtypeStruct((2, 16, SHARD, LANES), F32),
        scratch_shapes=[pltpu.VMEM((2 * K, PTS), BF16)],
        compiler_params=pltpu.CompilerParams(vmem_limit_bytes=MIDDLE_LIMIT),
        name="project",
    )(held, field)


def rough_kernel(field, north, west, pen, base, mine, other, left, right, pay):
    def put(at, first, second):
        high, low = parts(first)
        left[0:K, cols(at)] = high
        left[K : 2 * K, cols(at)] = low
        high, low = parts(second)
        right[0:K, cols(at)] = high
        right[K : 2 * K, cols(at)] = low

    first = jnp.zeros((K, LANES), F32)
    first_weighted = jnp.zeros((K, LANES), F32)
    lane = lane_of((K, LANES))
    for a in range(ROWS):
        here = field[:, cols(a)]
        weighted = here * pen[a : a + 1, :]
        put(a, weighted, smooth(field, a, None, None, None, None))
        first = jnp.where(lane == a, here[:, 0:1], first)
        first_weighted = jnp.where(lane == a, weighted[:, 0:1], first_weighted)
        if a == 0:
            put(ROWS, weighted, north[0:K, :])
            put(ROWS + 1, north[K : 2 * K, :], here)
    put(ROWS + 2, first_weighted, west[0:K, :])
    put(ROWS + 3, west[K : 2 * K, :], first)
    pay[...] = base[...]
    put_square(pay, 17, folded(dot_nt(left[...], right[...])))
    hand_out(pay, mine, other)


def rough_step(field, north, west, pen, base):
    return pl.pallas_call(
        rough_kernel,
        in_specs=[VM] * 5,
        out_specs=[VM] * 2,
        out_shape=[
            jax.ShapeDtypeStruct((16, SHARD, LANES), F32),
            jax.ShapeDtypeStruct((16 * SHARD, LANES), F32),
        ],
        scratch_shapes=[
            pltpu.VMEM((2 * K, PTS + 4 * LANES), BF16),
            pltpu.VMEM((2 * K, PTS + 4 * LANES), BF16),
            pltpu.VMEM((2, 16, SHARD, LANES), F32),
        ],
        compiler_params=pltpu.CompilerParams(vmem_limit_bytes=SMALL_LIMIT),
        name="roughness_products",
    )(field, north, west, pen, base)


def last_kernel(got_mine, got_other, field, basis, matrix, full):
    take_in(got_mine, got_other, full)
    inverse = inverse_factor(square_of(full, 16))
    solved = dot_nn(inverse, field[...], HIGHEST)
    for a in range(ROWS):
        basis[pl.ds(a, K, stride=ROWS), :] = solved[:, cols(a)]
    turned = jnp.concatenate([coefficients_of(full, at) for at in range(NSNAP // LANES)], axis=1)
    rough = square_of(full, 17)[:, 0:K]
    gram = dot_nt(turned, turned, HIGHEST)
    middle = (gram * (1.0 / NPTS) + rough) * (1.0 / NPTS)
    matrix[...] = dot_nt(dot_nn(inverse, middle, HIGHEST), inverse, HIGHEST)


def last_step(got, field):
    basis, matrix = pl.pallas_call(
        last_kernel,
        in_specs=[VM] * 3,
        out_specs=[VM] * 2,
        out_shape=[
            jax.ShapeDtypeStruct((K * ROWS, LANES), F32),
            jax.ShapeDtypeStruct((K, K), F32),
        ],
        scratch_shapes=[pltpu.VMEM((2, 16, SHARD, LANES), F32)],
        compiler_params=pltpu.CompilerParams(vmem_limit_bytes=SMALL_LIMIT),
        name="factor_and_finish",
    )(*got, field)
    return basis.reshape(K, ROWS, LANES), matrix


def exchange(value, axis):
    return lax.all_to_all(value, axis, 0, 0, tiled=True)


def copies(value, count):
    return jnp.broadcast_to(value[None], (count, *value.shape))


def summed_everywhere(mine, other, edges=None):
    depth = mine.shape[1]
    got = lax.ppermute(other, "core", SWAP)
    pair = mine + got[: 16 * depth].reshape(mine.shape)
    if edges is not None:
        cross, columns = edges
        pair, cross = lax.optimization_barrier((pair, cross))
        near = lax.ppermute(cross, LAT, CROSS)
    shares = exchange(pair, CHIPS)
    if edges is not None:
        shares, near = lax.optimization_barrier((shares, near))
    share = shares.sum(axis=0)
    if edges is not None:
        share = jnp.concatenate([share, columns], axis=0)
    around = exchange(copies(share, 8), "z")
    half = exchange(copies(around[:, :depth].sum(axis=0), 16), CHIPS)
    both = (half, lax.ppermute(half, "core", SWAP))
    if edges is None:
        return both, None
    return both, (got[16 * depth :], near, around)


def from_below(value, axis, count):
    return lax.ppermute(value, axis, [(i, i + 1) for i in range(count - 1)])


def local(snapshots, land_sea, penalty, initial_basis):
    snap, start, mine, other, *edges = begin(snapshots, initial_basis, land_sea)
    got, sides = summed_everywhere(mine, other, edges)
    applied, mine, other, *edges = first_step(got, snap, start, sides, land_sea, penalty)
    got, sides = summed_everywhere(mine, other, edges)
    applied, bottom, last, held = second_step(got, snap, applied, sides, land_sea, penalty)
    north = from_below(bottom, LAT, 32)
    west = from_below(last, "z", 8)
    base = project_step(held, applied)
    mine, other = rough_step(applied, north, west, penalty, base)
    got, _ = summed_everywhere(mine, other)
    return last_step(got, applied)


def solution(mesh):
    split_mesh = Mesh(mesh.devices.reshape(4, 4, 2, 8), ("y", "x", "core", "z"))
    flat = P(LAT, "z")
    deep = P(None, LAT, "z")
    return jax.shard_map(
        local,
        mesh=split_mesh,
        in_specs=(deep, flat, flat, deep),
        out_specs=(deep, P()),
        check_vma=False,
    )
```

```python
import jax
import jax.numpy as jnp
from jax import lax
from jax.experimental import pallas as pl
from jax.experimental.pallas import tpu as pltpu
from jax.sharding import Mesh, PartitionSpec as P

K = 64
NSNAP = 1024
NPTS = 524288
ROWS = 16
LANES = 128
PTS = ROWS * LANES
BLOCK = 256
NBLOCK = NSNAP // BLOCK
SHARD = 24
DEPTH = 16
F32 = jnp.float32
BF16 = jnp.bfloat16
HIGHEST = lax.Precision.HIGHEST
CHIPS = ("y", "x")
LAT = ("y", "x", "core")
SWAP = [(0, 1), (1, 0)]
CROSS = [pair for i in range(1, 31, 2) for pair in ((i, i + 1), (i + 1, i))]
VMEM_LIMIT = 50 * 1024 * 1024
FIRST_LIMIT = 53 * 1024 * 1024
MIDDLE_LIMIT = 36 * 1024 * 1024
SMALL_LIMIT = 20 * 1024 * 1024


def parts(value):
    high = value.astype(BF16)
    return high, (value - high.astype(F32)).astype(BF16)


def dot_nt(left, right, precision=None):
    return lax.dot_general(
        left, right, (((1,), (1,)), ((), ())), precision=precision, preferred_element_type=F32
    )


def dot_nn(left, right, precision=None):
    return lax.dot_general(
        left, right, (((1,), (0,)), ((), ())), precision=precision, preferred_element_type=F32
    )


def lane_of(shape):
    return lax.broadcasted_iota(jnp.int32, shape, len(shape) - 1)


def cols(a):
    return slice(a * LANES, (a + 1) * LANES)


def store_split(split_ref, a, value):
    high, low = parts(value)
    split_ref[0:K, cols(a)] = high
    split_ref[K : 2 * K, cols(a)] = low


def edge_columns(field_ref):
    lane = lane_of((K, LANES))
    first = jnp.zeros((K, LANES), F32)
    last = jnp.zeros((K, LANES), F32)
    for a in range(ROWS):
        block = field_ref[:, cols(a)]
        first = jnp.where(lane == a, block[:, 0:1], first)
        last = jnp.where(lane == a, block[:, LANES - 1 : LANES], last)
    return first, last


def packed_columns(strip):
    total = strip[0:8]
    for g in range(1, 8):
        total = total + pltpu.roll(strip[8 * g : 8 * g + 8], 16 * g, 1)
    return total


def unpacked_columns(packed):
    return jnp.concatenate(
        [packed if g == 0 else pltpu.roll(packed, LANES - 16 * g, 1) for g in range(8)], axis=0
    )


def smooth(field_ref, a, north, south, west, east):
    lane = lane_of((K, LANES))
    here = field_ref[:, cols(a)]
    up = field_ref[:, cols(a - 1)] if a > 0 else north
    down = field_ref[:, cols(a + 1)] if a < ROWS - 1 else south
    left = pltpu.roll(here, 1, 1)
    right = pltpu.roll(here, LANES - 1, 1)
    left = jnp.where(lane == 0, 0.0 if west is None else west[:, a : a + 1], left)
    right = jnp.where(lane == LANES - 1, 0.0 if east is None else east[:, a : a + 1], right)
    total = left + right
    if up is not None:
        total = total + up
    if down is not None:
        total = total + down
    return total - 4.0 * here


def hand_out(pay, mine, other):
    me = lax.axis_index("core")
    mine[...] = pay[me]
    depth = pay.shape[2]
    for chip in range(16):
        other[chip * depth : (chip + 1) * depth, :] = pay[1 - me, chip]


def hand_out_edges(field, depth, other, cross, columns):
    me = lax.axis_index("core")
    top = field[:, cols(0)]
    bottom = field[:, cols(ROWS - 1)]
    other[16 * depth : 16 * depth + K, :] = jnp.where(me == 0, bottom, top)
    cross[...] = jnp.where(me == 0, top, bottom)
    first, last = edge_columns(field)
    columns[0:8, :] = packed_columns(first)
    columns[8:16, :] = packed_columns(last)


def take_in_edges(pair, cross, columns):
    me = lax.axis_index("core")
    z = lax.axis_index("z")
    depth = columns.shape[1] - 16
    north = jnp.where(me == 0, cross[...], pair[...])
    south = jnp.where(me == 0, pair[...], cross[...])
    before = columns[jnp.maximum(z - 1, 0), depth + 8 : depth + 16, :]
    after = columns[jnp.minimum(z + 1, 7), depth : depth + 8, :]
    west = unpacked_columns(jnp.where(z > 0, before, 0.0))
    east = unpacked_columns(jnp.where(z < 7, after, 0.0))
    return north, south, west, east


def take_in(mine, other, full):
    me = lax.axis_index("core")
    full[me] = mine[...]
    full[1 - me] = other[...]


def row_of_shards(full, row):
    return jnp.concatenate(
        [full[half, chip, row : row + 1, :] for half in range(2) for chip in range(16)], axis=0
    )


def put_square(pay, row, doubled):
    packed = jnp.where(lane_of((K // 2, LANES)) < K, doubled[0 : K // 2], doubled[K // 2 : K])
    for half in range(2):
        for chip in range(16):
            at = half * 16 + chip
            pay[half, chip, row : row + 1, :] = packed[at : at + 1]


def square_of(full, row):
    packed = row_of_shards(full, row)
    return jnp.concatenate([packed, pltpu.roll(packed, K, 1)], axis=0)


def folded(product):
    rows = product[0:K] + product[K : 2 * K]
    return rows + pltpu.roll(rows, K, 1)


def inverse_factor(square):
    lane = lane_of((8, LANES))
    sub = lax.broadcasted_iota(jnp.int32, (8, LANES), 0)
    count = K // 8
    held = []
    for b in range(count):
        unit = jnp.where(lane - K == sub + 8 * b, 1.0, 0.0)
        held.append(jnp.where(lane < K, square[8 * b : 8 * b + 8] * (1.0 / NPTS), unit))
    for home in range(count):
        columns = [
            [
                jnp.broadcast_to(held[b][:, 8 * home + q : 8 * home + q + 1], (8, LANES))
                for b in range(home, count)
            ]
            for q in range(8)
        ]
        rows, scales = [], []
        for q in range(8):
            inverse = 1.0 / columns[q][0][q : q + 1, :]
            row = held[home][q : q + 1, :]
            scale = [column * inverse for column in columns[q]]
            scale[0] = jnp.where(sub > q, scale[0], 0.0)
            if q < 7:
                held[home] = held[home] - scale[0] * row
            for p in range(q + 1, 8):
                entry = columns[p][0][q : q + 1, :]
                columns[p] = [c - m * entry for c, m in zip(columns[p], scale)]
            rows.append(row)
            scales.append(scale)
        for at, b in enumerate(range(home + 1, count), 1):
            update = scales[0][at] * rows[0]
            for q in range(1, 8):
                update = update + scales[q][at] * rows[q]
            held[b] = held[b] - update
    done = []
    for b in range(count):
        diagonal = jnp.sum(jnp.where(lane == sub + 8 * b, held[b], 0.0), axis=1, keepdims=True)
        done.append(held[b] * lax.rsqrt(diagonal))
    return pltpu.roll(jnp.concatenate(done, axis=0), K, 1)[:, 0:K]


def put_coefficients(pay, block, held, split):
    both = dot_nt(held[block].reshape(2 * BLOCK, PTS), split[...])
    turned = (both[0:BLOCK] + both[BLOCK : 2 * BLOCK]).T
    turned = turned[0:K] + turned[K : 2 * K]
    for part in range(BLOCK // LANES):
        at = block * (BLOCK // LANES) + part
        chips = slice(4 * (at % 4), 4 * (at % 4) + 4)
        pay[at // 4, chips, 0:16, :] = turned[:, cols(part)].reshape(4, 16, LANES)


def coefficients_of(full, at):
    chips = slice(4 * (at % 4), 4 * (at % 4) + 4)
    return full[at // 4, chips, 0:16, :].reshape(K, LANES)


def spread_coefficients(full, spread):
    for block in range(NBLOCK):
        for part in range(BLOCK // LANES):
            high, low = parts(coefficients_of(full, block * (BLOCK // LANES) + part))
            spread[block, 0:K, cols(part)] = high
            spread[block, K : 2 * K, cols(part)] = low


def begin_kernel(
    snap, basis_in, sea_in, snap_out, flat, mine, other, cross, columns,
    raw, held, split, pay, basis, sea, in_sems, out_sems, own_sems,
):
    own = [
        pltpu.make_async_copy(basis_in, basis, own_sems.at[0]),
        pltpu.make_async_copy(sea_in, sea, own_sems.at[1]),
    ]
    for copy in own:
        copy.start()
    deep = BLOCK // 2

    def arrive(piece):
        span = pl.ds(piece * deep * ROWS, deep * ROWS)
        return pltpu.make_async_copy(snap.at[span], raw.at[span], in_sems.at[piece])

    def leave(piece):
        at = (piece // 2, slice(None), pl.ds((piece % 2) * deep, deep))
        return pltpu.make_async_copy(held.at[at], snap_out.at[at], out_sems.at[piece])

    for piece in range(2 * NBLOCK):
        arrive(piece).start()
    for copy in own:
        copy.wait()
    for a in range(ROWS):
        value = basis[pl.ds(a, K, stride=ROWS), :] * sea[a : a + 1, :].astype(F32)
        flat[:, cols(a)] = value
        store_split(split, a, value)
    hand_out_edges(flat, DEPTH, other, cross, columns)
    for block in range(NBLOCK):
        for piece in (2 * block, 2 * block + 1):
            arrive(piece).wait()
            span = slice((piece % 2) * deep, (piece % 2 + 1) * deep)
            for a in range(ROWS):
                high, low = parts(raw[pl.ds(piece * deep * ROWS + a, deep, stride=ROWS), :])
                held[block, 0, span, cols(a)] = high
                held[block, 1, span, cols(a)] = low
            leave(piece).start()
    project(held, split, pay)
    hand_out(pay, mine, other)
    for piece in range(2 * NBLOCK):
        leave(piece).wait()


VM = pl.BlockSpec(memory_space=pltpu.VMEM)
HB = pl.BlockSpec(memory_space=pl.ANY)
HBM = pl.BlockSpec(memory_space=pltpu.HBM)


def shared_outputs(depth):
    return [
        jax.ShapeDtypeStruct((K, PTS), F32),
        jax.ShapeDtypeStruct((16, depth, LANES), F32),
        jax.ShapeDtypeStruct((16 * depth + K, LANES), F32),
        jax.ShapeDtypeStruct((K, LANES), F32),
        jax.ShapeDtypeStruct((16, LANES), F32),
    ]


def begin(snapshots, basis, sea):
    return pl.pallas_call(
        begin_kernel,
        in_specs=[HBM, HBM, HBM],
        out_specs=[HB, *[VM] * 5],
        out_shape=[
            jax.ShapeDtypeStruct((2 * NBLOCK, 2, BLOCK, PTS), BF16),
            *shared_outputs(DEPTH),
        ],
        scratch_shapes=[
            pltpu.VMEM((NSNAP * ROWS, LANES), F32),
            pltpu.VMEM((NBLOCK, 2, BLOCK, PTS), BF16),
            pltpu.VMEM((2 * K, PTS), BF16),
            pltpu.VMEM((2, 16, DEPTH, LANES), F32),
            pltpu.VMEM((K * ROWS, LANES), F32),
            pltpu.VMEM((ROWS, LANES), jnp.int32),
            pltpu.SemaphoreType.DMA((2 * NBLOCK,)),
            pltpu.SemaphoreType.DMA((2 * NBLOCK,)),
            pltpu.SemaphoreType.DMA((2,)),
        ],
        compiler_params=pltpu.CompilerParams(vmem_limit_bytes=FIRST_LIMIT),
        name="split_and_project",
    )(snapshots.reshape(NSNAP * ROWS, LANES), basis.reshape(K * ROWS, LANES), sea)


def copy_of(snap, held, sems, block):
    return pltpu.make_async_copy(snap.at[block], held.at[block], sems.at[block])


def begin_copies(snap, held, sems):
    for block in range(NBLOCK):
        copy_of(snap, held, sems, block).start()


def expand(spread, snap, held, sems, total):
    width = 512
    for block in range(NBLOCK):
        copy_of(snap, held, sems, block).wait()
        for left in range(0, PTS, width):
            at = slice(left, left + width)
            both = dot_nn(spread[block], held[block, 0, :, at]) + dot_nn(
                spread[block], held[block, 1, :, at]
            )
            piece = both[0:K] + both[K : 2 * K]
            total[:, at] = piece if block == 0 else total[:, at] + piece


def project(held, split, pay):
    for block in range(NBLOCK):
        put_coefficients(pay, block, held, split)


def rough_field(prev, sides, pen, out):
    for a in range(ROWS):
        out[:, cols(a)] = pen[a : a + 1, :] * smooth(prev, a, *sides)


def applied_field(total, rough, sea, out):
    for a in range(ROWS):
        mask = sea[a : a + 1, :].astype(F32)
        out[:, cols(a)] = mask * (total[:, cols(a)] * (1.0 / NPTS) + rough[:, cols(a)])


def first_kernel(
    got_mine, got_other, snap, prev, pair, near, around, sea, pen,
    field, mine, other, cross, columns,
    full, spread, total, rough, held, split, pay, sems,
):
    begin_copies(snap, held, sems)
    take_in(got_mine, got_other, full)
    spread_coefficients(full, spread)
    rough_field(prev, take_in_edges(pair, near, around), pen, rough)
    expand(spread, snap, held, sems, total)
    applied_field(total, rough, sea, field)
    for a in range(ROWS):
        store_split(split, a, field[:, cols(a)])
    hand_out_edges(field, SHARD, other, cross, columns)
    pay[...] = jnp.zeros_like(pay)
    put_square(pay, 16, folded(dot_nt(split[...], split[...])))
    project(held, split, pay)
    hand_out(pay, mine, other)


def scratch_for_expand(depth):
    return [
        pltpu.VMEM((2, 16, depth, LANES), F32),
        pltpu.VMEM((NBLOCK, 2 * K, BLOCK), BF16),
        pltpu.VMEM((K, PTS), F32),
        pltpu.VMEM((K, PTS), F32),
    ]


def first_step(got, snap, prev, sides, sea, pen):
    return pl.pallas_call(
        first_kernel,
        in_specs=[VM, VM, HB, *[VM] * 6],
        out_specs=[VM] * 5,
        out_shape=shared_outputs(SHARD),
        scratch_shapes=[
            *scratch_for_expand(DEPTH),
            pltpu.VMEM((NBLOCK, 2, BLOCK, PTS), BF16),
            pltpu.VMEM((2 * K, PTS), BF16),
            pltpu.VMEM((2, 16, SHARD, LANES), F32),
            pltpu.SemaphoreType.DMA((NBLOCK,)),
        ],
        compiler_params=pltpu.CompilerParams(vmem_limit_bytes=VMEM_LIMIT),
        name="expand_and_project",
    )(*got, snap, prev, *sides, sea, pen)


def second_kernel(
    got_mine, got_other, snap, prev, pair, near, around, sea, pen,
    field, bottom, last, held,
    full, spread, total, rough, raw, sems,
):
    begin_copies(snap, held, sems)
    take_in(got_mine, got_other, full)
    spread_coefficients(full, spread)
    inverse = inverse_factor(square_of(full, 16))
    rough_field(prev, take_in_edges(pair, near, around), pen, rough)
    expand(spread, snap, held, sems, total)
    applied_field(total, rough, sea, raw)
    field[...] = dot_nn(inverse, raw[...], HIGHEST)
    bottom[0:K, :] = field[:, cols(ROWS - 1)]
    bottom[K : 2 * K, :] = field[:, cols(ROWS - 1)] * pen[ROWS - 1 : ROWS, :]
    _, last[0:K, :] = edge_columns(field)
    for a in range(ROWS):
        raw[:, cols(a)] = field[:, cols(a)] * pen[a : a + 1, :]
    _, last[K : 2 * K, :] = edge_columns(raw)


def second_step(got, snap, prev, sides, sea, pen):
    halo = jax.ShapeDtypeStruct((2 * K, LANES), F32)
    return pl.pallas_call(
        second_kernel,
        in_specs=[VM, VM, HB, *[VM] * 6],
        out_specs=[VM] * 4,
        out_shape=[
            jax.ShapeDtypeStruct((K, PTS), F32),
            halo,
            halo,
            jax.ShapeDtypeStruct((NBLOCK, 2, BLOCK, PTS), BF16),
        ],
        scratch_shapes=[
            *scratch_for_expand(SHARD),
            pltpu.VMEM((K, PTS), F32),
            pltpu.SemaphoreType.DMA((NBLOCK,)),
        ],
        compiler_params=pltpu.CompilerParams(vmem_limit_bytes=MIDDLE_LIMIT),
        name="factor_and_expand",
    )(*got, snap, prev, *sides, sea, pen)


def project_kernel(held, field, pay, split):
    for a in range(ROWS):
        store_split(split, a, field[:, cols(a)])
    pay[...] = jnp.zeros_like(pay)
    put_square(pay, 16, folded(dot_nt(split[...], split[...])))
    project(held, split, pay)


def project_step(held, field):
    return pl.pallas_call(
        project_kernel,
        in_specs=[VM, VM],
        out_specs=VM,
        out_shape=jax.ShapeDtypeStruct((2, 16, SHARD, LANES), F32),
        scratch_shapes=[pltpu.VMEM((2 * K, PTS), BF16)],
        compiler_params=pltpu.CompilerParams(vmem_limit_bytes=MIDDLE_LIMIT),
        name="project",
    )(held, field)


def rough_kernel(field, north, west, pen, base, mine, other, left, right, pay):
    def put(at, first, second):
        high, low = parts(first)
        left[0:K, cols(at)] = high
        left[K : 2 * K, cols(at)] = low
        high, low = parts(second)
        right[0:K, cols(at)] = high
        right[K : 2 * K, cols(at)] = low

    first = jnp.zeros((K, LANES), F32)
    first_weighted = jnp.zeros((K, LANES), F32)
    lane = lane_of((K, LANES))
    for a in range(ROWS):
        here = field[:, cols(a)]
        weighted = here * pen[a : a + 1, :]
        put(a, weighted, smooth(field, a, None, None, None, None))
        first = jnp.where(lane == a, here[:, 0:1], first)
        first_weighted = jnp.where(lane == a, weighted[:, 0:1], first_weighted)
        if a == 0:
            put(ROWS, weighted, north[0:K, :])
            put(ROWS + 1, north[K : 2 * K, :], here)
    put(ROWS + 2, first_weighted, west[0:K, :])
    put(ROWS + 3, west[K : 2 * K, :], first)
    pay[...] = base[...]
    put_square(pay, 17, folded(dot_nt(left[...], right[...])))
    hand_out(pay, mine, other)


def rough_step(field, north, west, pen, base):
    return pl.pallas_call(
        rough_kernel,
        in_specs=[VM] * 5,
        out_specs=[VM] * 2,
        out_shape=[
            jax.ShapeDtypeStruct((16, SHARD, LANES), F32),
            jax.ShapeDtypeStruct((16 * SHARD, LANES), F32),
        ],
        scratch_shapes=[
            pltpu.VMEM((2 * K, PTS + 4 * LANES), BF16),
            pltpu.VMEM((2 * K, PTS + 4 * LANES), BF16),
            pltpu.VMEM((2, 16, SHARD, LANES), F32),
        ],
        compiler_params=pltpu.CompilerParams(vmem_limit_bytes=SMALL_LIMIT),
        name="roughness_products",
    )(field, north, west, pen, base)


def last_kernel(got_mine, got_other, field, basis, matrix, full):
    take_in(got_mine, got_other, full)
    inverse = inverse_factor(square_of(full, 16))
    solved = dot_nn(inverse, field[...], HIGHEST)
    for a in range(ROWS):
        basis[pl.ds(a, K, stride=ROWS), :] = solved[:, cols(a)]
    turned = jnp.concatenate([coefficients_of(full, at) for at in range(NSNAP // LANES)], axis=1)
    rough = square_of(full, 17)[:, 0:K]
    gram = dot_nt(turned, turned, HIGHEST)
    middle = (gram * (1.0 / NPTS) + rough) * (1.0 / NPTS)
    matrix[...] = dot_nt(dot_nn(inverse, middle, HIGHEST), inverse, HIGHEST)


def last_step(got, field):
    basis, matrix = pl.pallas_call(
        last_kernel,
        in_specs=[VM] * 3,
        out_specs=[VM] * 2,
        out_shape=[
            jax.ShapeDtypeStruct((K * ROWS, LANES), F32),
            jax.ShapeDtypeStruct((K, K), F32),
        ],
        scratch_shapes=[pltpu.VMEM((2, 16, SHARD, LANES), F32)],
        compiler_params=pltpu.CompilerParams(vmem_limit_bytes=SMALL_LIMIT),
        name="factor_and_finish",
    )(*got, field)
    return basis.reshape(K, ROWS, LANES), matrix


def exchange(value, axis):
    return lax.all_to_all(value, axis, 0, 0, tiled=True)


def copies(value, count):
    return jnp.broadcast_to(value[None], (count, *value.shape))


def summed_everywhere(mine, other, edges=None):
    depth = mine.shape[1]
    got = lax.ppermute(other, "core", SWAP)
    pair = mine + got[: 16 * depth].reshape(mine.shape)
    if edges is not None:
        cross, columns = edges
        pair, cross = lax.optimization_barrier((pair, cross))
        near = lax.ppermute(cross, LAT, CROSS)
    shares = exchange(pair, CHIPS)
    if edges is not None:
        shares, near = lax.optimization_barrier((shares, near))
    share = shares.sum(axis=0)
    if edges is not None:
        share = jnp.concatenate([share, columns], axis=0)
    around = exchange(copies(share, 8), "z")
    half = exchange(copies(around[:, :depth].sum(axis=0), 16), CHIPS)
    both = (half, lax.ppermute(half, "core", SWAP))
    if edges is None:
        return both, None
    return both, (got[16 * depth :], near, around)


def from_below(value, axis, count):
    return lax.ppermute(value, axis, [(i, i + 1) for i in range(count - 1)])


def local(snapshots, land_sea, penalty, initial_basis):
    snap, start, mine, other, *edges = begin(snapshots, initial_basis, land_sea)
    got, sides = summed_everywhere(mine, other, edges)
    applied, mine, other, *edges = first_step(got, snap, start, sides, land_sea, penalty)
    got, sides = summed_everywhere(mine, other, edges)
    applied, bottom, last, held = second_step(got, snap, applied, sides, land_sea, penalty)
    north = from_below(bottom, LAT, 32)
    west = from_below(last, "z", 8)
    base = project_step(held, applied)
    mine, other = rough_step(applied, north, west, penalty, base)
    got, _ = summed_everywhere(mine, other)
    return last_step(got, applied)


def solution(mesh):
    split_mesh = Mesh(mesh.devices.reshape(4, 4, 2, 8), ("y", "x", "core", "z"))
    flat = P(LAT, "z")
    deep = P(None, LAT, "z")
    return jax.shard_map(
        local,
        mesh=split_mesh,
        in_specs=(deep, flat, flat, deep),
        out_specs=(deep, P()),
        check_vma=False,
    )
```

```python
import jax
import jax.numpy as jnp
from jax import lax
from jax.experimental import pallas as pl
from jax.experimental.pallas import tpu as pltpu
from jax.sharding import Mesh, PartitionSpec as P

K = 64
NSNAP = 1024
NPTS = 524288
ROWS = 16
LANES = 128
PTS = ROWS * LANES
BLOCK = 256
NBLOCK = NSNAP // BLOCK
SHARD = 24
DEPTH = 16
F32 = jnp.float32
BF16 = jnp.bfloat16
HIGHEST = lax.Precision.HIGHEST
CHIPS = ("y", "x")
LAT = ("y", "x", "core")
SWAP = [(0, 1), (1, 0)]
CROSS = [pair for i in range(1, 31, 2) for pair in ((i, i + 1), (i + 1, i))]
VMEM_LIMIT = 50 * 1024 * 1024
FIRST_LIMIT = 53 * 1024 * 1024
MIDDLE_LIMIT = 36 * 1024 * 1024
SMALL_LIMIT = 20 * 1024 * 1024


def parts(value):
    high = value.astype(BF16)
    return high, (value - high.astype(F32)).astype(BF16)


def dot_nt(left, right, precision=None):
    return lax.dot_general(
        left, right, (((1,), (1,)), ((), ())), precision=precision, preferred_element_type=F32
    )


def dot_nn(left, right, precision=None):
    return lax.dot_general(
        left, right, (((1,), (0,)), ((), ())), precision=precision, preferred_element_type=F32
    )


def lane_of(shape):
    return lax.broadcasted_iota(jnp.int32, shape, len(shape) - 1)


def cols(a):
    return slice(a * LANES, (a + 1) * LANES)


def store_split(split_ref, a, value):
    high, low = parts(value)
    split_ref[0:K, cols(a)] = high
    split_ref[K : 2 * K, cols(a)] = low


def edge_columns(field_ref):
    lane = lane_of((K, LANES))
    first = jnp.zeros((K, LANES), F32)
    last = jnp.zeros((K, LANES), F32)
    for a in range(ROWS):
        block = field_ref[:, cols(a)]
        first = jnp.where(lane == a, block[:, 0:1], first)
        last = jnp.where(lane == a, block[:, LANES - 1 : LANES], last)
    return first, last


def packed_columns(strip):
    total = strip[0:8]
    for g in range(1, 8):
        total = total + pltpu.roll(strip[8 * g : 8 * g + 8], 16 * g, 1)
    return total


def unpacked_columns(packed):
    return jnp.concatenate(
        [packed if g == 0 else pltpu.roll(packed, LANES - 16 * g, 1) for g in range(8)], axis=0
    )


def smooth(field_ref, a, north, south, west, east):
    lane = lane_of((K, LANES))
    here = field_ref[:, cols(a)]
    up = field_ref[:, cols(a - 1)] if a > 0 else north
    down = field_ref[:, cols(a + 1)] if a < ROWS - 1 else south
    left = pltpu.roll(here, 1, 1)
    right = pltpu.roll(here, LANES - 1, 1)
    left = jnp.where(lane == 0, 0.0 if west is None else west[:, a : a + 1], left)
    right = jnp.where(lane == LANES - 1, 0.0 if east is None else east[:, a : a + 1], right)
    total = left + right
    if up is not None:
        total = total + up
    if down is not None:
        total = total + down
    return total - 4.0 * here


def hand_out(pay, mine, other):
    me = lax.axis_index("core")
    mine[...] = pay[me]
    depth = pay.shape[2]
    for chip in range(16):
        other[chip * depth : (chip + 1) * depth, :] = pay[1 - me, chip]


def hand_out_edges(field, depth, other, cross, columns):
    me = lax.axis_index("core")
    top = field[:, cols(0)]
    bottom = field[:, cols(ROWS - 1)]
    other[16 * depth : 16 * depth + K, :] = jnp.where(me == 0, bottom, top)
    cross[...] = jnp.where(me == 0, top, bottom)
    first, last = edge_columns(field)
    columns[0:8, :] = packed_columns(first)
    columns[8:16, :] = packed_columns(last)


def take_in_edges(pair, cross, columns):
    me = lax.axis_index("core")
    z = lax.axis_index("z")
    depth = columns.shape[1] - 16
    north = jnp.where(me == 0, cross[...], pair[...])
    south = jnp.where(me == 0, pair[...], cross[...])
    before = columns[jnp.maximum(z - 1, 0), depth + 8 : depth + 16, :]
    after = columns[jnp.minimum(z + 1, 7), depth : depth + 8, :]
    west = unpacked_columns(jnp.where(z > 0, before, 0.0))
    east = unpacked_columns(jnp.where(z < 7, after, 0.0))
    return north, south, west, east


def row_of_shards(full, row):
    return jnp.concatenate(
        [full[2 * chip + half, row : row + 1, :] for half in range(2) for chip in range(16)], axis=0
    )


def put_square(pay, row, doubled):
    packed = jnp.where(lane_of((K // 2, LANES)) < K, doubled[0 : K // 2], doubled[K // 2 : K])
    for half in range(2):
        for chip in range(16):
            at = half * 16 + chip
            pay[half, chip, row : row + 1, :] = packed[at : at + 1]


def square_of(full, row):
    packed = row_of_shards(full, row)
    return jnp.concatenate([packed, pltpu.roll(packed, K, 1)], axis=0)


def folded(product):
    rows = product[0:K] + product[K : 2 * K]
    return rows + pltpu.roll(rows, K, 1)


def inverse_factor(square):
    lane = lane_of((8, LANES))
    sub = lax.broadcasted_iota(jnp.int32, (8, LANES), 0)
    count = K // 8
    held = []
    for b in range(count):
        unit = jnp.where(lane - K == sub + 8 * b, 1.0, 0.0)
        held.append(jnp.where(lane < K, square[8 * b : 8 * b + 8] * (1.0 / NPTS), unit))
    for home in range(count):
        columns = [
            [
                jnp.broadcast_to(held[b][:, 8 * home + q : 8 * home + q + 1], (8, LANES))
                for b in range(home, count)
            ]
            for q in range(8)
        ]
        rows, scales = [], []
        for q in range(8):
            inverse = 1.0 / columns[q][0][q : q + 1, :]
            row = held[home][q : q + 1, :]
            scale = [column * inverse for column in columns[q]]
            scale[0] = jnp.where(sub > q, scale[0], 0.0)
            if q < 7:
                held[home] = held[home] - scale[0] * row
            for p in range(q + 1, 8):
                entry = columns[p][0][q : q + 1, :]
                columns[p] = [c - m * entry for c, m in zip(columns[p], scale)]
            rows.append(row)
            scales.append(scale)
        for at, b in enumerate(range(home + 1, count), 1):
            update = scales[0][at] * rows[0]
            for q in range(1, 8):
                update = update + scales[q][at] * rows[q]
            held[b] = held[b] - update
    done = []
    for b in range(count):
        diagonal = jnp.sum(jnp.where(lane == sub + 8 * b, held[b], 0.0), axis=1, keepdims=True)
        done.append(held[b] * lax.rsqrt(diagonal))
    return pltpu.roll(jnp.concatenate(done, axis=0), K, 1)[:, 0:K]


def put_coefficients(pay, block, held, split):
    both = dot_nt(held[block].reshape(2 * BLOCK, PTS), split[...])
    turned = (both[0:BLOCK] + both[BLOCK : 2 * BLOCK]).T
    turned = turned[0:K] + turned[K : 2 * K]
    for part in range(BLOCK // LANES):
        at = block * (BLOCK // LANES) + part
        chips = slice(4 * (at % 4), 4 * (at % 4) + 4)
        pay[at // 4, chips, 0:16, :] = turned[:, cols(part)].reshape(4, 16, LANES)


def coefficients_of(full, at):
    chips = range(4 * (at % 4), 4 * (at % 4) + 4)
    return jnp.concatenate([full[2 * chip + at // 4, 0:16, :] for chip in chips], axis=0)


def spread_coefficients(full, spread):
    for block in range(NBLOCK):
        for part in range(BLOCK // LANES):
            high, low = parts(coefficients_of(full, block * (BLOCK // LANES) + part))
            spread[block, 0:K, cols(part)] = high
            spread[block, K : 2 * K, cols(part)] = low


def begin_kernel(
    snap, basis_in, sea_in, snap_out, flat, mine, other, cross, columns,
    raw, held, split, pay, basis, sea, in_sems, out_sems, own_sems,
):
    own = [
        pltpu.make_async_copy(basis_in, basis, own_sems.at[0]),
        pltpu.make_async_copy(sea_in, sea, own_sems.at[1]),
    ]
    for copy in own:
        copy.start()
    deep = BLOCK // 2

    def arrive(piece):
        span = pl.ds(piece * deep * ROWS, deep * ROWS)
        return pltpu.make_async_copy(snap.at[span], raw.at[span], in_sems.at[piece])

    def leave(piece):
        at = (piece // 2, slice(None), pl.ds((piece % 2) * deep, deep))
        return pltpu.make_async_copy(held.at[at], snap_out.at[at], out_sems.at[piece])

    for piece in range(2 * NBLOCK):
        arrive(piece).start()
    for copy in own:
        copy.wait()
    for a in range(ROWS):
        value = basis[pl.ds(a, K, stride=ROWS), :] * sea[a : a + 1, :].astype(F32)
        flat[:, cols(a)] = value
        store_split(split, a, value)
    hand_out_edges(flat, DEPTH, other, cross, columns)
    for block in range(NBLOCK):
        for piece in (2 * block, 2 * block + 1):
            arrive(piece).wait()
            span = slice((piece % 2) * deep, (piece % 2 + 1) * deep)
            for a in range(ROWS):
                high, low = parts(raw[pl.ds(piece * deep * ROWS + a, deep, stride=ROWS), :])
                held[block, 0, span, cols(a)] = high
                held[block, 1, span, cols(a)] = low
            leave(piece).start()
    project(held, split, pay)
    hand_out(pay, mine, other)
    for piece in range(2 * NBLOCK):
        leave(piece).wait()


VM = pl.BlockSpec(memory_space=pltpu.VMEM)
HB = pl.BlockSpec(memory_space=pl.ANY)
HBM = pl.BlockSpec(memory_space=pltpu.HBM)


def shared_outputs(depth):
    return [
        jax.ShapeDtypeStruct((K, PTS), F32),
        jax.ShapeDtypeStruct((16, depth, LANES), F32),
        jax.ShapeDtypeStruct((16 * depth + K, LANES), F32),
        jax.ShapeDtypeStruct((K, LANES), F32),
        jax.ShapeDtypeStruct((16, LANES), F32),
    ]


def begin(snapshots, basis, sea):
    return pl.pallas_call(
        begin_kernel,
        in_specs=[HBM, HBM, HBM],
        out_specs=[HB, *[VM] * 5],
        out_shape=[
            jax.ShapeDtypeStruct((2 * NBLOCK, 2, BLOCK, PTS), BF16),
            *shared_outputs(DEPTH),
        ],
        scratch_shapes=[
            pltpu.VMEM((NSNAP * ROWS, LANES), F32),
            pltpu.VMEM((NBLOCK, 2, BLOCK, PTS), BF16),
            pltpu.VMEM((2 * K, PTS), BF16),
            pltpu.VMEM((2, 16, DEPTH, LANES), F32),
            pltpu.VMEM((K * ROWS, LANES), F32),
            pltpu.VMEM((ROWS, LANES), jnp.int32),
            pltpu.SemaphoreType.DMA((2 * NBLOCK,)),
            pltpu.SemaphoreType.DMA((2 * NBLOCK,)),
            pltpu.SemaphoreType.DMA((2,)),
        ],
        compiler_params=pltpu.CompilerParams(vmem_limit_bytes=FIRST_LIMIT),
        name="split_and_project",
    )(snapshots.reshape(NSNAP * ROWS, LANES), basis.reshape(K * ROWS, LANES), sea)


def copy_of(snap, held, sems, block):
    return pltpu.make_async_copy(snap.at[block], held.at[block], sems.at[block])


def begin_copies(snap, held, sems):
    for block in range(NBLOCK):
        copy_of(snap, held, sems, block).start()


def expand(spread, snap, held, sems, total):
    width = 512
    for block in range(NBLOCK):
        copy_of(snap, held, sems, block).wait()
        for left in range(0, PTS, width):
            at = slice(left, left + width)
            both = dot_nn(spread[block], held[block, 0, :, at]) + dot_nn(
                spread[block], held[block, 1, :, at]
            )
            piece = both[0:K] + both[K : 2 * K]
            total[:, at] = piece if block == 0 else total[:, at] + piece


def project(held, split, pay):
    for block in range(NBLOCK):
        put_coefficients(pay, block, held, split)


def rough_field(prev, sides, pen, out):
    for a in range(ROWS):
        out[:, cols(a)] = pen[a : a + 1, :] * smooth(prev, a, *sides)


def applied_field(total, rough, sea, out):
    for a in range(ROWS):
        mask = sea[a : a + 1, :].astype(F32)
        out[:, cols(a)] = mask * (total[:, cols(a)] * (1.0 / NPTS) + rough[:, cols(a)])


def first_kernel(
    full, snap, prev, pair, near, around, sea, pen,
    field, mine, other, cross, columns,
    spread, total, rough, held, split, pay, sems,
):
    begin_copies(snap, held, sems)
    spread_coefficients(full, spread)
    rough_field(prev, take_in_edges(pair, near, around), pen, rough)
    expand(spread, snap, held, sems, total)
    applied_field(total, rough, sea, field)
    for a in range(ROWS):
        store_split(split, a, field[:, cols(a)])
    hand_out_edges(field, SHARD, other, cross, columns)
    pay[...] = jnp.zeros_like(pay)
    put_square(pay, 16, folded(dot_nt(split[...], split[...])))
    project(held, split, pay)
    hand_out(pay, mine, other)


def scratch_for_expand():
    return [
        pltpu.VMEM((NBLOCK, 2 * K, BLOCK), BF16),
        pltpu.VMEM((K, PTS), F32),
        pltpu.VMEM((K, PTS), F32),
    ]


def first_step(got, snap, prev, sides, sea, pen):
    return pl.pallas_call(
        first_kernel,
        in_specs=[VM, HB, *[VM] * 6],
        out_specs=[VM] * 5,
        out_shape=shared_outputs(SHARD),
        scratch_shapes=[
            *scratch_for_expand(),
            pltpu.VMEM((NBLOCK, 2, BLOCK, PTS), BF16),
            pltpu.VMEM((2 * K, PTS), BF16),
            pltpu.VMEM((2, 16, SHARD, LANES), F32),
            pltpu.SemaphoreType.DMA((NBLOCK,)),
        ],
        compiler_params=pltpu.CompilerParams(vmem_limit_bytes=VMEM_LIMIT),
        name="expand_and_project",
    )(got, snap, prev, *sides, sea, pen)


def second_kernel(
    full, snap, prev, pair, near, around, sea, pen,
    field, bottom, last, held,
    spread, total, rough, raw, sems,
):
    begin_copies(snap, held, sems)
    spread_coefficients(full, spread)
    inverse = inverse_factor(square_of(full, 16))
    rough_field(prev, take_in_edges(pair, near, around), pen, rough)
    expand(spread, snap, held, sems, total)
    applied_field(total, rough, sea, raw)
    field[...] = dot_nn(inverse, raw[...], HIGHEST)
    bottom[0:K, :] = field[:, cols(ROWS - 1)]
    bottom[K : 2 * K, :] = field[:, cols(ROWS - 1)] * pen[ROWS - 1 : ROWS, :]
    _, last[0:K, :] = edge_columns(field)
    for a in range(ROWS):
        raw[:, cols(a)] = field[:, cols(a)] * pen[a : a + 1, :]
    _, last[K : 2 * K, :] = edge_columns(raw)


def second_step(got, snap, prev, sides, sea, pen):
    halo = jax.ShapeDtypeStruct((2 * K, LANES), F32)
    return pl.pallas_call(
        second_kernel,
        in_specs=[VM, HB, *[VM] * 6],
        out_specs=[VM] * 4,
        out_shape=[
            jax.ShapeDtypeStruct((K, PTS), F32),
            halo,
            halo,
            jax.ShapeDtypeStruct((NBLOCK, 2, BLOCK, PTS), BF16),
        ],
        scratch_shapes=[
            *scratch_for_expand(),
            pltpu.VMEM((K, PTS), F32),
            pltpu.SemaphoreType.DMA((NBLOCK,)),
        ],
        compiler_params=pltpu.CompilerParams(vmem_limit_bytes=MIDDLE_LIMIT),
        name="factor_and_expand",
    )(got, snap, prev, *sides, sea, pen)


def project_kernel(held, field, pay, split):
    for a in range(ROWS):
        store_split(split, a, field[:, cols(a)])
    pay[...] = jnp.zeros_like(pay)
    put_square(pay, 16, folded(dot_nt(split[...], split[...])))
    project(held, split, pay)


def project_step(held, field):
    return pl.pallas_call(
        project_kernel,
        in_specs=[VM, VM],
        out_specs=VM,
        out_shape=jax.ShapeDtypeStruct((2, 16, SHARD, LANES), F32),
        scratch_shapes=[pltpu.VMEM((2 * K, PTS), BF16)],
        compiler_params=pltpu.CompilerParams(vmem_limit_bytes=MIDDLE_LIMIT),
        name="project",
    )(held, field)


def rough_kernel(field, north, west, pen, base, mine, other, left, right, pay):
    def put(at, first, second):
        high, low = parts(first)
        left[0:K, cols(at)] = high
        left[K : 2 * K, cols(at)] = low
        high, low = parts(second)
        right[0:K, cols(at)] = high
        right[K : 2 * K, cols(at)] = low

    first = jnp.zeros((K, LANES), F32)
    first_weighted = jnp.zeros((K, LANES), F32)
    lane = lane_of((K, LANES))
    for a in range(ROWS):
        here = field[:, cols(a)]
        weighted = here * pen[a : a + 1, :]
        put(a, weighted, smooth(field, a, None, None, None, None))
        first = jnp.where(lane == a, here[:, 0:1], first)
        first_weighted = jnp.where(lane == a, weighted[:, 0:1], first_weighted)
        if a == 0:
            put(ROWS, weighted, north[0:K, :])
            put(ROWS + 1, north[K : 2 * K, :], here)
    put(ROWS + 2, first_weighted, west[0:K, :])
    put(ROWS + 3, west[K : 2 * K, :], first)
    pay[...] = base[...]
    put_square(pay, 17, folded(dot_nt(left[...], right[...])))
    hand_out(pay, mine, other)


def rough_step(field, north, west, pen, base):
    return pl.pallas_call(
        rough_kernel,
        in_specs=[VM] * 5,
        out_specs=[VM] * 2,
        out_shape=[
            jax.ShapeDtypeStruct((16, SHARD, LANES), F32),
            jax.ShapeDtypeStruct((16 * SHARD, LANES), F32),
        ],
        scratch_shapes=[
            pltpu.VMEM((2 * K, PTS + 4 * LANES), BF16),
            pltpu.VMEM((2 * K, PTS + 4 * LANES), BF16),
            pltpu.VMEM((2, 16, SHARD, LANES), F32),
        ],
        compiler_params=pltpu.CompilerParams(vmem_limit_bytes=SMALL_LIMIT),
        name="roughness_products",
    )(field, north, west, pen, base)


def last_kernel(full, field, basis, matrix):
    inverse = inverse_factor(square_of(full, 16))
    solved = dot_nn(inverse, field[...], HIGHEST)
    for a in range(ROWS):
        basis[pl.ds(a, K, stride=ROWS), :] = solved[:, cols(a)]
    turned = jnp.concatenate([coefficients_of(full, at) for at in range(NSNAP // LANES)], axis=1)
    rough = square_of(full, 17)[:, 0:K]
    gram = dot_nt(turned, turned, HIGHEST)
    middle = (gram * (1.0 / NPTS) + rough) * (1.0 / NPTS)
    matrix[...] = dot_nt(dot_nn(inverse, middle, HIGHEST), inverse, HIGHEST)


def last_step(got, field):
    basis, matrix = pl.pallas_call(
        last_kernel,
        in_specs=[VM] * 2,
        out_specs=[VM] * 2,
        out_shape=[
            jax.ShapeDtypeStruct((K * ROWS, LANES), F32),
            jax.ShapeDtypeStruct((K, K), F32),
        ],
        compiler_params=pltpu.CompilerParams(vmem_limit_bytes=SMALL_LIMIT),
        name="factor_and_finish",
    )(got, field)
    return basis.reshape(K, ROWS, LANES), matrix


def exchange(value, axis):
    return lax.all_to_all(value, axis, 0, 0, tiled=True)


def copies(value, count):
    return jnp.broadcast_to(value[None], (count, *value.shape))


def summed_everywhere(mine, other, edges=None):
    depth = mine.shape[1]
    got = lax.ppermute(other, "core", SWAP)
    pair = mine + got[: 16 * depth].reshape(mine.shape)
    if edges is not None:
        cross, columns = edges
        pair, cross = lax.optimization_barrier((pair, cross))
        near = lax.ppermute(cross, LAT, CROSS)
    shares = exchange(pair, CHIPS)
    if edges is not None:
        shares, near = lax.optimization_barrier((shares, near))
    share = shares.sum(axis=0)
    if edges is not None:
        share = jnp.concatenate([share, columns], axis=0)
    around = exchange(copies(share, 8), "z")
    full = exchange(copies(around[:, :depth].sum(axis=0), 32), LAT)
    if edges is None:
        return full, None
    return full, (got[16 * depth :], near, around)


def from_below(value, axis, count):
    return lax.ppermute(value, axis, [(i, i + 1) for i in range(count - 1)])


def local(snapshots, land_sea, penalty, initial_basis):
    snap, start, mine, other, *edges = begin(snapshots, initial_basis, land_sea)
    got, sides = summed_everywhere(mine, other, edges)
    applied, mine, other, *edges = first_step(got, snap, start, sides, land_sea, penalty)
    got, sides = summed_everywhere(mine, other, edges)
    applied, bottom, last, held = second_step(got, snap, applied, sides, land_sea, penalty)
    north = from_below(bottom, LAT, 32)
    west = from_below(last, "z", 8)
    base = project_step(held, applied)
    mine, other = rough_step(applied, north, west, penalty, base)
    got, _ = summed_everywhere(mine, other)
    return last_step(got, applied)


def solution(mesh):
    split_mesh = Mesh(mesh.devices.reshape(4, 4, 2, 8), ("y", "x", "core", "z"))
    flat = P(LAT, "z")
    deep = P(None, LAT, "z")
    return jax.shard_map(
        local,
        mesh=split_mesh,
        in_specs=(deep, flat, flat, deep),
        out_specs=(deep, P()),
        check_vma=False,
    )
```

```python
import jax
import jax.numpy as jnp
from jax import lax
from jax.experimental import pallas as pl
from jax.experimental.pallas import tpu as pltpu
from jax.sharding import Mesh, PartitionSpec as P

K = 64
NSNAP = 1024
NPTS = 524288
ROWS = 16
LANES = 128
PTS = ROWS * LANES
BLOCK = 256
NBLOCK = NSNAP // BLOCK
HALF = BLOCK // 2
SHARD = 24
DEPTH = 16
F32 = jnp.float32
BF16 = jnp.bfloat16
HIGHEST = lax.Precision.HIGHEST
CHIPS = ("y", "x")
LAT = ("y", "x", "core")
SWAP = [(0, 1), (1, 0)]
CROSS = [pair for i in range(1, 31, 2) for pair in ((i, i + 1), (i + 1, i))]
VMEM_LIMIT = 50 * 1024 * 1024
FIRST_LIMIT = 53 * 1024 * 1024
MIDDLE_LIMIT = 36 * 1024 * 1024
LATE = 2
SMALL_LIMIT = 20 * 1024 * 1024


def parts(value):
    high = value.astype(BF16)
    return high, (value - high.astype(F32)).astype(BF16)


def dot_nt(left, right, precision=None):
    return lax.dot_general(
        left, right, (((1,), (1,)), ((), ())), precision=precision, preferred_element_type=F32
    )


def dot_nn(left, right, precision=None):
    return lax.dot_general(
        left, right, (((1,), (0,)), ((), ())), precision=precision, preferred_element_type=F32
    )


def lane_of(shape):
    return lax.broadcasted_iota(jnp.int32, shape, len(shape) - 1)


def cols(a):
    return slice(a * LANES, (a + 1) * LANES)


def store_split(split_ref, a, value):
    high, low = parts(value)
    split_ref[0:K, cols(a)] = high
    split_ref[K : 2 * K, cols(a)] = low


def edge_columns(field_ref):
    lane = lane_of((K, LANES))
    first = jnp.zeros((K, LANES), F32)
    last = jnp.zeros((K, LANES), F32)
    for a in range(ROWS):
        block = field_ref[:, cols(a)]
        first = jnp.where(lane == a, block[:, 0:1], first)
        last = jnp.where(lane == a, block[:, LANES - 1 : LANES], last)
    return first, last


def packed_columns(strip):
    total = strip[0:8]
    for g in range(1, 8):
        total = total + pltpu.roll(strip[8 * g : 8 * g + 8], 16 * g, 1)
    return total


def unpacked_columns(packed):
    return jnp.concatenate(
        [packed if g == 0 else pltpu.roll(packed, LANES - 16 * g, 1) for g in range(8)], axis=0
    )


def smooth(field_ref, a, north, south, west, east):
    lane = lane_of((K, LANES))
    here = field_ref[:, cols(a)]
    up = field_ref[:, cols(a - 1)] if a > 0 else north
    down = field_ref[:, cols(a + 1)] if a < ROWS - 1 else south
    left = pltpu.roll(here, 1, 1)
    right = pltpu.roll(here, LANES - 1, 1)
    left = jnp.where(lane == 0, 0.0 if west is None else west[:, a : a + 1], left)
    right = jnp.where(lane == LANES - 1, 0.0 if east is None else east[:, a : a + 1], right)
    total = left + right
    if up is not None:
        total = total + up
    if down is not None:
        total = total + down
    return total - 4.0 * here


def hand_out(pay, mine, other):
    me = lax.axis_index("core")
    mine[...] = pay[me]
    depth = pay.shape[2]
    for chip in range(16):
        other[chip * depth : (chip + 1) * depth, :] = pay[1 - me, chip]


def hand_out_edges(field, depth, other, cross, columns):
    me = lax.axis_index("core")
    top = field[:, cols(0)]
    bottom = field[:, cols(ROWS - 1)]
    other[16 * depth : 16 * depth + K, :] = jnp.where(me == 0, bottom, top)
    cross[...] = jnp.where(me == 0, top, bottom)
    first, last = edge_columns(field)
    columns[0:8, :] = packed_columns(first)
    columns[8:16, :] = packed_columns(last)


def take_in_edges(pair, cross, columns):
    me = lax.axis_index("core")
    z = lax.axis_index("z")
    depth = columns.shape[1] - 16
    north = jnp.where(me == 0, cross[...], pair[...])
    south = jnp.where(me == 0, pair[...], cross[...])
    before = columns[jnp.maximum(z - 1, 0), depth + 8 : depth + 16, :]
    after = columns[jnp.minimum(z + 1, 7), depth : depth + 8, :]
    west = unpacked_columns(jnp.where(z > 0, before, 0.0))
    east = unpacked_columns(jnp.where(z < 7, after, 0.0))
    return north, south, west, east


def take_in(mine, other, full):
    me = lax.axis_index("core")
    full[me] = mine[...]
    full[1 - me] = other[...]


def row_of_shards(full, row):
    return jnp.concatenate(
        [full[half, chip, row : row + 1, :] for half in range(2) for chip in range(16)], axis=0
    )


def put_square(pay, row, doubled):
    packed = jnp.where(lane_of((K // 2, LANES)) < K, doubled[0 : K // 2], doubled[K // 2 : K])
    for half in range(2):
        for chip in range(16):
            at = half * 16 + chip
            pay[half, chip, row : row + 1, :] = packed[at : at + 1]


def square_of(full, row):
    packed = row_of_shards(full, row)
    return jnp.concatenate([packed, pltpu.roll(packed, K, 1)], axis=0)


def folded(product):
    rows = product[0:K] + product[K : 2 * K]
    return rows + pltpu.roll(rows, K, 1)


def inverse_factor(square):
    lane = lane_of((8, LANES))
    sub = lax.broadcasted_iota(jnp.int32, (8, LANES), 0)
    count = K // 8
    held = []
    for b in range(count):
        unit = jnp.where(lane - K == sub + 8 * b, 1.0, 0.0)
        held.append(jnp.where(lane < K, square[8 * b : 8 * b + 8] * (1.0 / NPTS), unit))
    for home in range(count):
        columns = [
            [
                jnp.broadcast_to(held[b][:, 8 * home + q : 8 * home + q + 1], (8, LANES))
                for b in range(home, count)
            ]
            for q in range(8)
        ]
        rows, scales = [], []
        for q in range(8):
            inverse = 1.0 / columns[q][0][q : q + 1, :]
            row = held[home][q : q + 1, :]
            scale = [column * inverse for column in columns[q]]
            scale[0] = jnp.where(sub > q, scale[0], 0.0)
            if q < 7:
                held[home] = held[home] - scale[0] * row
            for p in range(q + 1, 8):
                entry = columns[p][0][q : q + 1, :]
                columns[p] = [c - m * entry for c, m in zip(columns[p], scale)]
            rows.append(row)
            scales.append(scale)
        for at, b in enumerate(range(home + 1, count), 1):
            update = scales[0][at] * rows[0]
            for q in range(1, 8):
                update = update + scales[q][at] * rows[q]
            held[b] = held[b] - update
    done = []
    for b in range(count):
        diagonal = jnp.sum(jnp.where(lane == sub + 8 * b, held[b], 0.0), axis=1, keepdims=True)
        done.append(held[b] * lax.rsqrt(diagonal))
    return pltpu.roll(jnp.concatenate(done, axis=0), K, 1)[:, 0:K]


def put_coefficients(pay, block, held, split):
    both = dot_nt(held[block].reshape(2 * BLOCK, PTS), split[...])
    turned = (both[0:BLOCK] + both[BLOCK : 2 * BLOCK]).T
    turned = turned[0:K] + turned[K : 2 * K]
    for part in range(BLOCK // LANES):
        at = block * (BLOCK // LANES) + part
        chips = slice(4 * (at % 4), 4 * (at % 4) + 4)
        pay[at // 4, chips, 0:16, :] = turned[:, cols(part)].reshape(4, 16, LANES)


def coefficients_of(full, at):
    chips = slice(4 * (at % 4), 4 * (at % 4) + 4)
    return full[at // 4, chips, 0:16, :].reshape(K, LANES)


def spread_coefficients(full, spread):
    for block in range(NBLOCK):
        for part in range(BLOCK // LANES):
            high, low = parts(coefficients_of(full, block * (BLOCK // LANES) + part))
            spread[block, 0:K, cols(part)] = high
            spread[block, K : 2 * K, cols(part)] = low


def arrival(snap, raw, sems, piece):
    span = pl.ds(piece * HALF * ROWS, HALF * ROWS)
    return pltpu.make_async_copy(snap.at[span], raw.at[span], sems.at[piece])


def split_piece(raw, held, piece):
    span = slice((piece % 2) * HALF, (piece % 2 + 1) * HALF)
    for a in range(ROWS):
        high, low = parts(raw[pl.ds(piece * HALF * ROWS + a, HALF, stride=ROWS), :])
        held[piece // 2, 0, span, cols(a)] = high
        held[piece // 2, 1, span, cols(a)] = low


def begin_kernel(
    snap, basis_in, sea_in, snap_out, flat, mine, other, cross, columns,
    raw, held, split, pay, basis, sea, in_sems, out_sems, own_sems,
):
    own = [
        pltpu.make_async_copy(basis_in, basis, own_sems.at[0]),
        pltpu.make_async_copy(sea_in, sea, own_sems.at[1]),
    ]
    for copy in own:
        copy.start()
    def leave(piece):
        at = (piece // 2, slice(None), pl.ds((piece % 2) * HALF, HALF))
        return pltpu.make_async_copy(held.at[at], snap_out.at[at], out_sems.at[piece])

    for piece in range(2 * NBLOCK):
        arrival(snap, raw, in_sems, piece).start(priority=piece % 2)
    for copy in own:
        copy.wait()
    for a in range(ROWS):
        value = basis[pl.ds(a, K, stride=ROWS), :] * sea[a : a + 1, :].astype(F32)
        flat[:, cols(a)] = value
        store_split(split, a, value)
    hand_out_edges(flat, DEPTH, other, cross, columns)
    for block in range(NBLOCK):
        for piece in (2 * block, 2 * block + 1):
            arrival(snap, raw, in_sems, piece).wait()
            split_piece(raw, held, piece)
            if block >= LATE:
                leave(piece).start(priority=piece % 2)
    project(held, split, pay)
    hand_out(pay, mine, other)
    for piece in range(2 * LATE, 2 * NBLOCK):
        leave(piece).wait()


VM = pl.BlockSpec(memory_space=pltpu.VMEM)
HB = pl.BlockSpec(memory_space=pl.ANY)
HBM = pl.BlockSpec(memory_space=pltpu.HBM)


def shared_outputs(depth):
    return [
        jax.ShapeDtypeStruct((K, PTS), F32),
        jax.ShapeDtypeStruct((16, depth, LANES), F32),
        jax.ShapeDtypeStruct((16 * depth + K, LANES), F32),
        jax.ShapeDtypeStruct((K, LANES), F32),
        jax.ShapeDtypeStruct((16, LANES), F32),
    ]


def begin(snapshots, basis, sea):
    return pl.pallas_call(
        begin_kernel,
        in_specs=[HBM, HBM, HBM],
        out_specs=[HB, *[VM] * 5],
        out_shape=[
            jax.ShapeDtypeStruct((2 * NBLOCK, 2, BLOCK, PTS), BF16),
            *shared_outputs(DEPTH),
        ],
        scratch_shapes=[
            pltpu.VMEM((NSNAP * ROWS, LANES), F32),
            pltpu.VMEM((NBLOCK, 2, BLOCK, PTS), BF16),
            pltpu.VMEM((2 * K, PTS), BF16),
            pltpu.VMEM((2, 16, DEPTH, LANES), F32),
            pltpu.VMEM((K * ROWS, LANES), F32),
            pltpu.VMEM((ROWS, LANES), jnp.int32),
            pltpu.SemaphoreType.DMA((2 * NBLOCK,)),
            pltpu.SemaphoreType.DMA((2 * NBLOCK,)),
            pltpu.SemaphoreType.DMA((2,)),
        ],
        compiler_params=pltpu.CompilerParams(vmem_limit_bytes=FIRST_LIMIT),
        name="split_and_project",
    )(snapshots.reshape(NSNAP * ROWS, LANES), basis.reshape(K * ROWS, LANES), sea)


def copy_of(snap, held, sems, block):
    return pltpu.make_async_copy(snap.at[block], held.at[block], sems.at[block])


def expand(spread, held, total, arrive):
    width = 512
    for block in range(NBLOCK):
        arrive(block)
        for left in range(0, PTS, width):
            at = slice(left, left + width)
            both = dot_nn(spread[block], held[block, 0, :, at]) + dot_nn(
                spread[block], held[block, 1, :, at]
            )
            piece = both[0:K] + both[K : 2 * K]
            total[:, at] = piece if block == 0 else total[:, at] + piece


def project(held, split, pay):
    for block in range(NBLOCK):
        put_coefficients(pay, block, held, split)


def rough_field(prev, sides, pen, out):
    for a in range(ROWS):
        out[:, cols(a)] = pen[a : a + 1, :] * smooth(prev, a, *sides)


def applied_field(total, rough, sea, out):
    for a in range(ROWS):
        mask = sea[a : a + 1, :].astype(F32)
        out[:, cols(a)] = mask * (total[:, cols(a)] * (1.0 / NPTS) + rough[:, cols(a)])


def first_kernel(
    got_mine, got_other, fresh, snap, prev, pair, near, around, sea, pen,
    snap_out, field, mine, other, cross, columns,
    full, spread, total, rough, held, split, pay, raw, sems, fresh_sems, out_sems,
):
    for piece in range(2 * LATE):
        arrival(fresh, raw, fresh_sems, piece).start(priority=piece % 2)
    for block in range(LATE, NBLOCK):
        copy_of(snap, held, sems, block).start(priority=block % 2)
    take_in(got_mine, got_other, full)
    spread_coefficients(full, spread)
    rough_field(prev, take_in_edges(pair, near, around), pen, rough)

    def leave(block):
        return pltpu.make_async_copy(held.at[block], snap_out.at[block], out_sems.at[block])

    def arrive(block):
        if block >= LATE:
            copy_of(snap, held, sems, block).wait()
            return
        for piece in (2 * block, 2 * block + 1):
            arrival(fresh, raw, fresh_sems, piece).wait()
            split_piece(raw, held, piece)
        leave(block).start(priority=block % 2)

    expand(spread, held, total, arrive)
    applied_field(total, rough, sea, field)
    for a in range(ROWS):
        store_split(split, a, field[:, cols(a)])
    hand_out_edges(field, SHARD, other, cross, columns)
    pay[...] = jnp.zeros_like(pay)
    put_square(pay, 16, folded(dot_nt(split[...], split[...])))
    project(held, split, pay)
    hand_out(pay, mine, other)
    for block in range(LATE):
        leave(block).wait()


def scratch_for_expand(depth):
    return [
        pltpu.VMEM((2, 16, depth, LANES), F32),
        pltpu.VMEM((NBLOCK, 2 * K, BLOCK), BF16),
        pltpu.VMEM((K, PTS), F32),
        pltpu.VMEM((K, PTS), F32),
    ]


def first_step(got, fresh, snap, prev, sides, sea, pen):
    return pl.pallas_call(
        first_kernel,
        in_specs=[VM, VM, HB, HB, *[VM] * 6],
        out_specs=[HB, *[VM] * 5],
        out_shape=[
            jax.ShapeDtypeStruct((2 * NBLOCK, 2, BLOCK, PTS), BF16),
            *shared_outputs(SHARD),
        ],
        scratch_shapes=[
            *scratch_for_expand(DEPTH),
            pltpu.VMEM((NBLOCK, 2, BLOCK, PTS), BF16),
            pltpu.VMEM((2 * K, PTS), BF16),
            pltpu.VMEM((2, 16, SHARD, LANES), F32),
            pltpu.VMEM((LATE * BLOCK * ROWS, LANES), F32),
            pltpu.SemaphoreType.DMA((NBLOCK,)),
            pltpu.SemaphoreType.DMA((2 * LATE,)),
            pltpu.SemaphoreType.DMA((LATE,)),
        ],
        compiler_params=pltpu.CompilerParams(vmem_limit_bytes=VMEM_LIMIT),
        name="expand_and_project",
    )(*got, fresh.reshape(NSNAP * ROWS, LANES), snap, prev, *sides, sea, pen)


def solved(inverse, field, split):
    for a in range(ROWS):
        store_split(split, a, field[:, cols(a)])
    high, low = parts(inverse)
    left = [jnp.concatenate([part, part], axis=1) for part in (high, low)]
    both = dot_nn(jnp.concatenate(left, axis=0), split[...])
    return both[0:K] + both[K : 2 * K]


def second_kernel(
    got_mine, got_other, early, snap, prev, pair, near, around, sea, pen,
    field, bottom, last, held,
    full, spread, total, rough, raw, split, sems,
):
    def copy(block):
        return copy_of(early if block < LATE else snap, held, sems, block)

    for block in range(NBLOCK):
        copy(block).start(priority=block % 2)
    take_in(got_mine, got_other, full)
    spread_coefficients(full, spread)
    inverse = inverse_factor(square_of(full, 16))
    rough_field(prev, take_in_edges(pair, near, around), pen, rough)
    expand(spread, held, total, lambda block: copy(block).wait())
    applied_field(total, rough, sea, raw)
    field[...] = solved(inverse, raw, split)
    bottom[0:K, :] = field[:, cols(ROWS - 1)]
    bottom[K : 2 * K, :] = field[:, cols(ROWS - 1)] * pen[ROWS - 1 : ROWS, :]
    _, last[0:K, :] = edge_columns(field)
    for a in range(ROWS):
        raw[:, cols(a)] = field[:, cols(a)] * pen[a : a + 1, :]
    _, last[K : 2 * K, :] = edge_columns(raw)


def second_step(got, early, snap, prev, sides, sea, pen):
    halo = jax.ShapeDtypeStruct((2 * K, LANES), F32)
    return pl.pallas_call(
        second_kernel,
        in_specs=[VM, VM, HB, HB, *[VM] * 6],
        out_specs=[VM] * 4,
        out_shape=[
            jax.ShapeDtypeStruct((K, PTS), F32),
            halo,
            halo,
            jax.ShapeDtypeStruct((NBLOCK, 2, BLOCK, PTS), BF16),
        ],
        scratch_shapes=[
            *scratch_for_expand(SHARD),
            pltpu.VMEM((K, PTS), F32),
            pltpu.VMEM((2 * K, PTS), BF16),
            pltpu.SemaphoreType.DMA((NBLOCK,)),
        ],
        compiler_params=pltpu.CompilerParams(vmem_limit_bytes=MIDDLE_LIMIT),
        name="factor_and_expand",
    )(*got, early, snap, prev, *sides, sea, pen)


def project_kernel(held, field, pay, split):
    for a in range(ROWS):
        store_split(split, a, field[:, cols(a)])
    pay[...] = jnp.zeros_like(pay)
    put_square(pay, 16, folded(dot_nt(split[...], split[...])))
    project(held, split, pay)


def project_step(held, field):
    return pl.pallas_call(
        project_kernel,
        in_specs=[VM, VM],
        out_specs=VM,
        out_shape=jax.ShapeDtypeStruct((2, 16, SHARD, LANES), F32),
        scratch_shapes=[pltpu.VMEM((2 * K, PTS), BF16)],
        compiler_params=pltpu.CompilerParams(vmem_limit_bytes=MIDDLE_LIMIT),
        name="project",
    )(held, field)


def rough_kernel(field, north, west, pen, base, mine, other, left, right, pay):
    def put(at, first, second):
        high, low = parts(first)
        left[0:K, cols(at)] = high
        left[K : 2 * K, cols(at)] = low
        high, low = parts(second)
        right[0:K, cols(at)] = high
        right[K : 2 * K, cols(at)] = low

    first = jnp.zeros((K, LANES), F32)
    first_weighted = jnp.zeros((K, LANES), F32)
    lane = lane_of((K, LANES))
    for a in range(ROWS):
        here = field[:, cols(a)]
        weighted = here * pen[a : a + 1, :]
        put(a, weighted, smooth(field, a, None, None, None, None))
        first = jnp.where(lane == a, here[:, 0:1], first)
        first_weighted = jnp.where(lane == a, weighted[:, 0:1], first_weighted)
        if a == 0:
            put(ROWS, weighted, north[0:K, :])
            put(ROWS + 1, north[K : 2 * K, :], here)
    put(ROWS + 2, first_weighted, west[0:K, :])
    put(ROWS + 3, west[K : 2 * K, :], first)
    pay[...] = base[...]
    put_square(pay, 17, folded(dot_nt(left[...], right[...])))
    hand_out(pay, mine, other)


def rough_step(field, north, west, pen, base):
    return pl.pallas_call(
        rough_kernel,
        in_specs=[VM] * 5,
        out_specs=[VM] * 2,
        out_shape=[
            jax.ShapeDtypeStruct((16, SHARD, LANES), F32),
            jax.ShapeDtypeStruct((16 * SHARD, LANES), F32),
        ],
        scratch_shapes=[
            pltpu.VMEM((2 * K, PTS + 4 * LANES), BF16),
            pltpu.VMEM((2 * K, PTS + 4 * LANES), BF16),
            pltpu.VMEM((2, 16, SHARD, LANES), F32),
        ],
        compiler_params=pltpu.CompilerParams(vmem_limit_bytes=SMALL_LIMIT),
        name="roughness_products",
    )(field, north, west, pen, base)


def last_kernel(got_mine, got_other, field, basis, matrix, full, split):
    take_in(got_mine, got_other, full)
    inverse = inverse_factor(square_of(full, 16))
    final = solved(inverse, field, split)
    for a in range(ROWS):
        basis[pl.ds(a, K, stride=ROWS), :] = final[:, cols(a)]
    turned = jnp.concatenate([coefficients_of(full, at) for at in range(NSNAP // LANES)], axis=1)
    rough = square_of(full, 17)[:, 0:K]
    gram = dot_nt(turned, turned, HIGHEST)
    middle = (gram * (1.0 / NPTS) + rough) * (1.0 / NPTS)
    matrix[...] = dot_nt(dot_nn(inverse, middle, HIGHEST), inverse, HIGHEST)


def last_step(got, field):
    basis, matrix = pl.pallas_call(
        last_kernel,
        in_specs=[VM] * 3,
        out_specs=[VM] * 2,
        out_shape=[
            jax.ShapeDtypeStruct((K * ROWS, LANES), F32),
            jax.ShapeDtypeStruct((K, K), F32),
        ],
        scratch_shapes=[
            pltpu.VMEM((2, 16, SHARD, LANES), F32),
            pltpu.VMEM((2 * K, PTS), BF16),
        ],
        compiler_params=pltpu.CompilerParams(vmem_limit_bytes=SMALL_LIMIT),
        name="factor_and_finish",
    )(*got, field)
    return basis.reshape(K, ROWS, LANES), matrix


def exchange(value, axis):
    return lax.all_to_all(value, axis, 0, 0, tiled=True)


def copies(value, count):
    return jnp.broadcast_to(value[None], (count, *value.shape))


def summed_everywhere(mine, other, edges=None):
    depth = mine.shape[1]
    got = lax.ppermute(other, "core", SWAP)
    pair = mine + got[: 16 * depth].reshape(mine.shape)
    if edges is not None:
        cross, columns = edges
        pair, cross = lax.optimization_barrier((pair, cross))
        near = lax.ppermute(cross, LAT, CROSS)
    shares = exchange(pair, CHIPS)
    if edges is not None:
        shares, near = lax.optimization_barrier((shares, near))
    share = shares.sum(axis=0)
    if edges is not None:
        share = jnp.concatenate([share, columns], axis=0)
    around = exchange(copies(share, 8), "z")
    half = exchange(copies(around[:, :depth].sum(axis=0), 16), CHIPS)
    both = (half, lax.ppermute(half, "core", SWAP))
    if edges is None:
        return both, None
    return both, (got[16 * depth :], near, around)


def from_below(value, axis, count):
    return lax.ppermute(value, axis, [(i, i + 1) for i in range(count - 1)])


def local(snapshots, land_sea, penalty, initial_basis):
    snap, start, mine, other, *edges = begin(snapshots, initial_basis, land_sea)
    got, sides = summed_everywhere(mine, other, edges)
    early, applied, mine, other, *edges = first_step(
        got, snapshots, snap, start, sides, land_sea, penalty
    )
    got, sides = summed_everywhere(mine, other, edges)
    applied, bottom, last, held = second_step(got, early, snap, applied, sides, land_sea, penalty)
    north = from_below(bottom, LAT, 32)
    west = from_below(last, "z", 8)
    base = project_step(held, applied)
    mine, other = rough_step(applied, north, west, penalty, base)
    got, _ = summed_everywhere(mine, other)
    return last_step(got, applied)


def solution(mesh):
    split_mesh = Mesh(mesh.devices.reshape(4, 4, 2, 8), ("y", "x", "core", "z"))
    flat = P(LAT, "z")
    deep = P(None, LAT, "z")
    return jax.shard_map(
        local,
        mesh=split_mesh,
        in_specs=(deep, flat, flat, deep),
        out_specs=(deep, P()),
        check_vma=False,
    )
```

```python
import jax
import jax.numpy as jnp
from jax import lax
from jax.experimental import pallas as pl
from jax.experimental.pallas import tpu as pltpu
from jax.sharding import Mesh, PartitionSpec as P

K = 64
NSNAP = 1024
NPTS = 524288
ROWS = 16
LANES = 128
PTS = ROWS * LANES
BLOCK = 256
NBLOCK = NSNAP // BLOCK
SHARD = 24
DEPTH = 16
F32 = jnp.float32
BF16 = jnp.bfloat16
HIGHEST = lax.Precision.HIGHEST
CHIPS = ("y", "x")
LAT = ("y", "x", "core")
SWAP = [(0, 1), (1, 0)]
CROSS = [pair for i in range(1, 31, 2) for pair in ((i, i + 1), (i + 1, i))]
VMEM_LIMIT = 50 * 1024 * 1024
FIRST_LIMIT = 53 * 1024 * 1024
MIDDLE_LIMIT = 36 * 1024 * 1024
SMALL_LIMIT = 20 * 1024 * 1024


def parts(value):
    high = value.astype(BF16)
    return high, (value - high.astype(F32)).astype(BF16)


def dot_nt(left, right, precision=None):
    return lax.dot_general(
        left, right, (((1,), (1,)), ((), ())), precision=precision, preferred_element_type=F32
    )


def dot_nn(left, right, precision=None):
    return lax.dot_general(
        left, right, (((1,), (0,)), ((), ())), precision=precision, preferred_element_type=F32
    )


def lane_of(shape):
    return lax.broadcasted_iota(jnp.int32, shape, len(shape) - 1)


def cols(a):
    return slice(a * LANES, (a + 1) * LANES)


def store_split(split_ref, a, value):
    high, low = parts(value)
    split_ref[0:K, cols(a)] = high
    split_ref[K : 2 * K, cols(a)] = low


def edge_columns(field_ref):
    lane = lane_of((K, LANES))
    first = jnp.zeros((K, LANES), F32)
    last = jnp.zeros((K, LANES), F32)
    for a in range(ROWS):
        block = field_ref[:, cols(a)]
        first = jnp.where(lane == a, block[:, 0:1], first)
        last = jnp.where(lane == a, block[:, LANES - 1 : LANES], last)
    return first, last


def packed_columns(strip):
    total = strip[0:8]
    for g in range(1, 8):
        total = total + pltpu.roll(strip[8 * g : 8 * g + 8], 16 * g, 1)
    return total


def unpacked_columns(packed):
    return jnp.concatenate(
        [packed if g == 0 else pltpu.roll(packed, LANES - 16 * g, 1) for g in range(8)], axis=0
    )


def smooth(field_ref, a, north, south, west, east):
    lane = lane_of((K, LANES))
    here = field_ref[:, cols(a)]
    up = field_ref[:, cols(a - 1)] if a > 0 else north
    down = field_ref[:, cols(a + 1)] if a < ROWS - 1 else south
    left = pltpu.roll(here, 1, 1)
    right = pltpu.roll(here, LANES - 1, 1)
    left = jnp.where(lane == 0, 0.0 if west is None else west[:, a : a + 1], left)
    right = jnp.where(lane == LANES - 1, 0.0 if east is None else east[:, a : a + 1], right)
    total = left + right
    if up is not None:
        total = total + up
    if down is not None:
        total = total + down
    return total - 4.0 * here


def hand_out(pay, mine, other):
    me = lax.axis_index("core")
    mine[...] = pay[me]
    depth = pay.shape[2]
    for chip in range(16):
        other[chip * depth : (chip + 1) * depth, :] = pay[1 - me, chip]


def hand_out_edges(field, depth, other, cross, columns):
    me = lax.axis_index("core")
    top = field[:, cols(0)]
    bottom = field[:, cols(ROWS - 1)]
    other[16 * depth : 16 * depth + K, :] = jnp.where(me == 0, bottom, top)
    cross[...] = jnp.where(me == 0, top, bottom)
    first, last = edge_columns(field)
    columns[0:8, :] = packed_columns(first)
    columns[8:16, :] = packed_columns(last)


def take_in_edges(pair, cross, columns):
    me = lax.axis_index("core")
    z = lax.axis_index("z")
    depth = columns.shape[1] - 16
    north = jnp.where(me == 0, cross[...], pair[...])
    south = jnp.where(me == 0, pair[...], cross[...])
    before = columns[jnp.maximum(z - 1, 0), depth + 8 : depth + 16, :]
    after = columns[jnp.minimum(z + 1, 7), depth : depth + 8, :]
    west = unpacked_columns(jnp.where(z > 0, before, 0.0))
    east = unpacked_columns(jnp.where(z < 7, after, 0.0))
    return north, south, west, east


def take_in(mine, other, full):
    me = lax.axis_index("core")
    full[me] = mine[...]
    full[1 - me] = other[...]


def row_of_shards(full, row):
    return jnp.concatenate(
        [full[half, chip, row : row + 1, :] for half in range(2) for chip in range(16)], axis=0
    )


def put_square(pay, row, doubled):
    packed = jnp.where(lane_of((K // 2, LANES)) < K, doubled[0 : K // 2], doubled[K // 2 : K])
    for half in range(2):
        for chip in range(16):
            at = half * 16 + chip
            pay[half, chip, row : row + 1, :] = packed[at : at + 1]


def square_of(full, row):
    packed = row_of_shards(full, row)
    return jnp.concatenate([packed, pltpu.roll(packed, K, 1)], axis=0)


def folded(product):
    rows = product[0:K] + product[K : 2 * K]
    return rows + pltpu.roll(rows, K, 1)


def inverse_factor(square):
    lane = lane_of((8, LANES))
    sub = lax.broadcasted_iota(jnp.int32, (8, LANES), 0)
    count = K // 8
    held = []
    for b in range(count):
        unit = jnp.where(lane - K == sub + 8 * b, 1.0, 0.0)
        held.append(jnp.where(lane < K, square[8 * b : 8 * b + 8] * (1.0 / NPTS), unit))
    for home in range(count):
        columns = [
            [
                jnp.broadcast_to(held[b][:, 8 * home + q : 8 * home + q + 1], (8, LANES))
                for b in range(home, count)
            ]
            for q in range(8)
        ]
        rows, scales = [], []
        for q in range(8):
            inverse = 1.0 / columns[q][0][q : q + 1, :]
            row = held[home][q : q + 1, :]
            scale = [column * inverse for column in columns[q]]
            scale[0] = jnp.where(sub > q, scale[0], 0.0)
            if q < 7:
                held[home] = held[home] - scale[0] * row
            for p in range(q + 1, 8):
                entry = columns[p][0][q : q + 1, :]
                columns[p] = [c - m * entry for c, m in zip(columns[p], scale)]
            rows.append(row)
            scales.append(scale)
        for at, b in enumerate(range(home + 1, count), 1):
            update = scales[0][at] * rows[0]
            for q in range(1, 8):
                update = update + scales[q][at] * rows[q]
            held[b] = held[b] - update
    done = []
    for b in range(count):
        diagonal = jnp.sum(jnp.where(lane == sub + 8 * b, held[b], 0.0), axis=1, keepdims=True)
        done.append(held[b] * lax.rsqrt(diagonal))
    return pltpu.roll(jnp.concatenate(done, axis=0), K, 1)[:, 0:K]


def put_coefficients(pay, block, held, split):
    both = dot_nt(held[block].reshape(2 * BLOCK, PTS), split[...])
    turned = (both[0:BLOCK] + both[BLOCK : 2 * BLOCK]).T
    turned = turned[0:K] + turned[K : 2 * K]
    for part in range(BLOCK // LANES):
        at = block * (BLOCK // LANES) + part
        chips = slice(4 * (at % 4), 4 * (at % 4) + 4)
        pay[at // 4, chips, 0:16, :] = turned[:, cols(part)].reshape(4, 16, LANES)


def coefficients_of(full, at):
    chips = slice(4 * (at % 4), 4 * (at % 4) + 4)
    return full[at // 4, chips, 0:16, :].reshape(K, LANES)


def spread_coefficients(full, spread):
    for block in range(NBLOCK):
        for part in range(BLOCK // LANES):
            high, low = parts(coefficients_of(full, block * (BLOCK // LANES) + part))
            spread[block, 0:K, cols(part)] = high
            spread[block, K : 2 * K, cols(part)] = low


def begin_kernel(
    snap, basis_in, sea_in, snap_out, flat, mine, other, cross, columns,
    raw, held, split, pay, basis, sea, in_sems, out_sems, own_sems,
):
    own = [
        pltpu.make_async_copy(basis_in, basis, own_sems.at[0]),
        pltpu.make_async_copy(sea_in, sea, own_sems.at[1]),
    ]
    for copy in own:
        copy.start()
    deep = BLOCK // 2

    def arrive(piece):
        span = pl.ds(piece * deep * ROWS, deep * ROWS)
        return pltpu.make_async_copy(snap.at[span], raw.at[span], in_sems.at[piece])

    def leave(piece):
        at = (piece // 2, slice(None), pl.ds((piece % 2) * deep, deep))
        return pltpu.make_async_copy(held.at[at], snap_out.at[at], out_sems.at[piece])

    for piece in range(2 * NBLOCK):
        arrive(piece).start()
    for copy in own:
        copy.wait()
    for a in range(ROWS):
        value = basis[pl.ds(a, K, stride=ROWS), :] * sea[a : a + 1, :].astype(F32)
        flat[:, cols(a)] = value
        store_split(split, a, value)
    hand_out_edges(flat, DEPTH, other, cross, columns)
    for block in range(NBLOCK):
        for piece in (2 * block, 2 * block + 1):
            arrive(piece).wait()
            span = slice((piece % 2) * deep, (piece % 2 + 1) * deep)
            for a in range(ROWS):
                high, low = parts(raw[pl.ds(piece * deep * ROWS + a, deep, stride=ROWS), :])
                held[block, 0, span, cols(a)] = high
                held[block, 1, span, cols(a)] = low
            leave(piece).start()
    project(held, split, pay)
    hand_out(pay, mine, other)
    for piece in range(2 * NBLOCK):
        leave(piece).wait()


VM = pl.BlockSpec(memory_space=pltpu.VMEM)
HB = pl.BlockSpec(memory_space=pl.ANY)
HBM = pl.BlockSpec(memory_space=pltpu.HBM)


def shared_outputs(depth):
    return [
        jax.ShapeDtypeStruct((K, PTS), F32),
        jax.ShapeDtypeStruct((16, depth, LANES), F32),
        jax.ShapeDtypeStruct((16 * depth + K, LANES), F32),
        jax.ShapeDtypeStruct((K, LANES), F32),
        jax.ShapeDtypeStruct((16, LANES), F32),
    ]


def begin(snapshots, basis, sea):
    return pl.pallas_call(
        begin_kernel,
        in_specs=[HBM, HBM, HBM],
        out_specs=[HB, *[VM] * 5],
        out_shape=[
            jax.ShapeDtypeStruct((2 * NBLOCK, 2, BLOCK, PTS), BF16),
            *shared_outputs(DEPTH),
        ],
        scratch_shapes=[
            pltpu.VMEM((NSNAP * ROWS, LANES), F32),
            pltpu.VMEM((NBLOCK, 2, BLOCK, PTS), BF16),
            pltpu.VMEM((2 * K, PTS), BF16),
            pltpu.VMEM((2, 16, DEPTH, LANES), F32),
            pltpu.VMEM((K * ROWS, LANES), F32),
            pltpu.VMEM((ROWS, LANES), jnp.int32),
            pltpu.SemaphoreType.DMA((2 * NBLOCK,)),
            pltpu.SemaphoreType.DMA((2 * NBLOCK,)),
            pltpu.SemaphoreType.DMA((2,)),
        ],
        compiler_params=pltpu.CompilerParams(vmem_limit_bytes=FIRST_LIMIT),
        name="split_and_project",
    )(snapshots.reshape(NSNAP * ROWS, LANES), basis.reshape(K * ROWS, LANES), sea)


def copy_of(snap, held, sems, block):
    return pltpu.make_async_copy(snap.at[block], held.at[block], sems.at[block])


def begin_copies(snap, held, sems):
    for block in range(NBLOCK):
        copy_of(snap, held, sems, block).start()


def expand(spread, snap, held, sems, total):
    width = 512
    for block in range(NBLOCK):
        copy_of(snap, held, sems, block).wait()
        for left in range(0, PTS, width):
            at = slice(left, left + width)
            both = dot_nn(spread[block], held[block, 0, :, at]) + dot_nn(
                spread[block], held[block, 1, :, at]
            )
            piece = both[0:K] + both[K : 2 * K]
            total[:, at] = piece if block == 0 else total[:, at] + piece


def project(held, split, pay):
    for block in range(NBLOCK):
        put_coefficients(pay, block, held, split)


def rough_field(prev, sides, pen, out):
    for a in range(ROWS):
        out[:, cols(a)] = pen[a : a + 1, :] * smooth(prev, a, *sides)


def applied_field(total, rough, sea, out):
    for a in range(ROWS):
        mask = sea[a : a + 1, :].astype(F32)
        out[:, cols(a)] = mask * (total[:, cols(a)] * (1.0 / NPTS) + rough[:, cols(a)])


def first_kernel(
    got_mine, got_other, snap, prev, pair, near, around, sea, pen,
    field, mine, other, cross, columns,
    full, spread, total, rough, held, split, pay, sems,
):
    begin_copies(snap, held, sems)
    take_in(got_mine, got_other, full)
    spread_coefficients(full, spread)
    rough_field(prev, take_in_edges(pair, near, around), pen, rough)
    expand(spread, snap, held, sems, total)
    applied_field(total, rough, sea, field)
    for a in range(ROWS):
        store_split(split, a, field[:, cols(a)])
    hand_out_edges(field, SHARD, other, cross, columns)
    pay[...] = jnp.zeros_like(pay)
    put_square(pay, 16, folded(dot_nt(split[...], split[...])))
    project(held, split, pay)
    hand_out(pay, mine, other)


def scratch_for_expand(depth):
    return [
        pltpu.VMEM((2, 16, depth, LANES), F32),
        pltpu.VMEM((NBLOCK, 2 * K, BLOCK), BF16),
        pltpu.VMEM((K, PTS), F32),
        pltpu.VMEM((K, PTS), F32),
    ]


def first_step(got, snap, prev, sides, sea, pen):
    return pl.pallas_call(
        first_kernel,
        in_specs=[VM, VM, HB, *[VM] * 6],
        out_specs=[VM] * 5,
        out_shape=shared_outputs(SHARD),
        scratch_shapes=[
            *scratch_for_expand(DEPTH),
            pltpu.VMEM((NBLOCK, 2, BLOCK, PTS), BF16),
            pltpu.VMEM((2 * K, PTS), BF16),
            pltpu.VMEM((2, 16, SHARD, LANES), F32),
            pltpu.SemaphoreType.DMA((NBLOCK,)),
        ],
        compiler_params=pltpu.CompilerParams(vmem_limit_bytes=VMEM_LIMIT),
        name="expand_and_project",
    )(*got, snap, prev, *sides, sea, pen)


def solved(inverse, field, split):
    for a in range(ROWS):
        store_split(split, a, field[:, cols(a)])
    high, low = parts(inverse)
    left = [jnp.concatenate([part, part], axis=1) for part in (high, low)]
    both = dot_nn(jnp.concatenate(left, axis=0), split[...])
    return both[0:K] + both[K : 2 * K]


def second_kernel(
    got_mine, got_other, snap, prev, pair, near, around, sea, pen,
    field, bottom, last, held,
    full, spread, total, rough, raw, split, sems,
):
    begin_copies(snap, held, sems)
    take_in(got_mine, got_other, full)
    spread_coefficients(full, spread)
    inverse = inverse_factor(square_of(full, 16))
    rough_field(prev, take_in_edges(pair, near, around), pen, rough)
    expand(spread, snap, held, sems, total)
    applied_field(total, rough, sea, raw)
    field[...] = solved(inverse, raw, split)
    bottom[0:K, :] = field[:, cols(ROWS - 1)]
    bottom[K : 2 * K, :] = field[:, cols(ROWS - 1)] * pen[ROWS - 1 : ROWS, :]
    _, last[0:K, :] = edge_columns(field)
    for a in range(ROWS):
        raw[:, cols(a)] = field[:, cols(a)] * pen[a : a + 1, :]
    _, last[K : 2 * K, :] = edge_columns(raw)


def second_step(got, snap, prev, sides, sea, pen):
    halo = jax.ShapeDtypeStruct((2 * K, LANES), F32)
    return pl.pallas_call(
        second_kernel,
        in_specs=[VM, VM, HB, *[VM] * 6],
        out_specs=[VM] * 4,
        out_shape=[
            jax.ShapeDtypeStruct((K, PTS), F32),
            halo,
            halo,
            jax.ShapeDtypeStruct((NBLOCK, 2, BLOCK, PTS), BF16),
        ],
        scratch_shapes=[
            *scratch_for_expand(SHARD),
            pltpu.VMEM((K, PTS), F32),
            pltpu.VMEM((2 * K, PTS), BF16),
            pltpu.SemaphoreType.DMA((NBLOCK,)),
        ],
        compiler_params=pltpu.CompilerParams(vmem_limit_bytes=MIDDLE_LIMIT),
        name="factor_and_expand",
    )(*got, snap, prev, *sides, sea, pen)


def project_kernel(held, field, pay, split):
    for a in range(ROWS):
        store_split(split, a, field[:, cols(a)])
    pay[...] = jnp.zeros_like(pay)
    put_square(pay, 16, folded(dot_nt(split[...], split[...])))
    project(held, split, pay)


def project_step(held, field):
    return pl.pallas_call(
        project_kernel,
        in_specs=[VM, VM],
        out_specs=VM,
        out_shape=jax.ShapeDtypeStruct((2, 16, SHARD, LANES), F32),
        scratch_shapes=[pltpu.VMEM((2 * K, PTS), BF16)],
        compiler_params=pltpu.CompilerParams(vmem_limit_bytes=MIDDLE_LIMIT),
        name="project",
    )(held, field)


def rough_kernel(field, north, west, pen, base, mine, other, left, right, pay):
    def put(at, first, second):
        high, low = parts(first)
        left[0:K, cols(at)] = high
        left[K : 2 * K, cols(at)] = low
        high, low = parts(second)
        right[0:K, cols(at)] = high
        right[K : 2 * K, cols(at)] = low

    first = jnp.zeros((K, LANES), F32)
    first_weighted = jnp.zeros((K, LANES), F32)
    lane = lane_of((K, LANES))
    for a in range(ROWS):
        here = field[:, cols(a)]
        weighted = here * pen[a : a + 1, :]
        put(a, weighted, smooth(field, a, None, None, None, None))
        first = jnp.where(lane == a, here[:, 0:1], first)
        first_weighted = jnp.where(lane == a, weighted[:, 0:1], first_weighted)
        if a == 0:
            put(ROWS, weighted, north[0:K, :])
            put(ROWS + 1, north[K : 2 * K, :], here)
    put(ROWS + 2, first_weighted, west[0:K, :])
    put(ROWS + 3, west[K : 2 * K, :], first)
    pay[...] = base[...]
    put_square(pay, 17, folded(dot_nt(left[...], right[...])))
    hand_out(pay, mine, other)


def rough_step(field, north, west, pen, base):
    return pl.pallas_call(
        rough_kernel,
        in_specs=[VM] * 5,
        out_specs=[VM] * 2,
        out_shape=[
            jax.ShapeDtypeStruct((16, SHARD, LANES), F32),
            jax.ShapeDtypeStruct((16 * SHARD, LANES), F32),
        ],
        scratch_shapes=[
            pltpu.VMEM((2 * K, PTS + 4 * LANES), BF16),
            pltpu.VMEM((2 * K, PTS + 4 * LANES), BF16),
            pltpu.VMEM((2, 16, SHARD, LANES), F32),
        ],
        compiler_params=pltpu.CompilerParams(vmem_limit_bytes=SMALL_LIMIT),
        name="roughness_products",
    )(field, north, west, pen, base)


def last_kernel(got_mine, got_other, field, basis, matrix, full, split, wide):
    take_in(got_mine, got_other, full)
    inverse = inverse_factor(square_of(full, 16))
    final = solved(inverse, field, split)
    for a in range(ROWS):
        basis[pl.ds(a, K, stride=ROWS), :] = final[:, cols(a)]
    for at in range(NSNAP // LANES):
        store_split(wide, at, coefficients_of(full, at))
    rough = square_of(full, 17)[:, 0:K]
    gram = folded(dot_nt(wide[...], wide[...]))[:, 0:K]
    middle = (gram * (1.0 / NPTS) + rough) * (1.0 / NPTS)
    matrix[...] = dot_nt(dot_nn(inverse, middle, HIGHEST), inverse, HIGHEST)


def last_step(got, field):
    basis, matrix = pl.pallas_call(
        last_kernel,
        in_specs=[VM] * 3,
        out_specs=[VM] * 2,
        out_shape=[
            jax.ShapeDtypeStruct((K * ROWS, LANES), F32),
            jax.ShapeDtypeStruct((K, K), F32),
        ],
        scratch_shapes=[
            pltpu.VMEM((2, 16, SHARD, LANES), F32),
            pltpu.VMEM((2 * K, PTS), BF16),
            pltpu.VMEM((2 * K, NSNAP), BF16),
        ],
        compiler_params=pltpu.CompilerParams(vmem_limit_bytes=SMALL_LIMIT),
        name="factor_and_finish",
    )(*got, field)
    return basis.reshape(K, ROWS, LANES), matrix


def exchange(value, axis):
    return lax.all_to_all(value, axis, 0, 0, tiled=True)


def copies(value, count):
    return jnp.broadcast_to(value[None], (count, *value.shape))


def summed_everywhere(mine, other, edges=None):
    depth = mine.shape[1]
    got = lax.ppermute(other, "core", SWAP)
    pair = mine + got[: 16 * depth].reshape(mine.shape)
    if edges is not None:
        cross, columns = edges
        pair, cross = lax.optimization_barrier((pair, cross))
        near = lax.ppermute(cross, LAT, CROSS)
    shares = exchange(pair, CHIPS)
    if edges is not None:
        shares, near = lax.optimization_barrier((shares, near))
    share = shares.sum(axis=0)
    if edges is not None:
        share = jnp.concatenate([share, columns], axis=0)
    around = exchange(copies(share, 8), "z")
    half = exchange(copies(around[:, :depth].sum(axis=0), 16), CHIPS)
    both = (half, lax.ppermute(half, "core", SWAP))
    if edges is None:
        return both, None
    return both, (got[16 * depth :], near, around)


def from_below(value, axis, count):
    return lax.ppermute(value, axis, [(i, i + 1) for i in range(count - 1)])


def local(snapshots, land_sea, penalty, initial_basis):
    snap, start, mine, other, *edges = begin(snapshots, initial_basis, land_sea)
    got, sides = summed_everywhere(mine, other, edges)
    applied, mine, other, *edges = first_step(got, snap, start, sides, land_sea, penalty)
    got, sides = summed_everywhere(mine, other, edges)
    applied, bottom, last, held = second_step(got, snap, applied, sides, land_sea, penalty)
    north = from_below(bottom, LAT, 32)
    west = from_below(last, "z", 8)
    base = project_step(held, applied)
    mine, other = rough_step(applied, north, west, penalty, base)
    got, _ = summed_everywhere(mine, other)
    return last_step(got, applied)


def solution(mesh):
    split_mesh = Mesh(mesh.devices.reshape(4, 4, 2, 8), ("y", "x", "core", "z"))
    flat = P(LAT, "z")
    deep = P(None, LAT, "z")
    return jax.shard_map(
        local,
        mesh=split_mesh,
        in_specs=(deep, flat, flat, deep),
        out_specs=(deep, P()),
        check_vma=False,
    )
```

```python
import jax
import jax.numpy as jnp
from jax import lax
from jax.experimental import pallas as pl
from jax.experimental.pallas import tpu as pltpu
from jax.sharding import Mesh, PartitionSpec as P

K = 64
NSNAP = 1024
NPTS = 524288
ROWS = 16
LANES = 128
PTS = ROWS * LANES
BLOCK = 256
NBLOCK = NSNAP // BLOCK
SHARD = 24
DEPTH = 16
F32 = jnp.float32
BF16 = jnp.bfloat16
HIGHEST = lax.Precision.HIGHEST
CHIPS = ("y", "x")
LAT = ("y", "x", "core")
SWAP = [(0, 1), (1, 0)]
CROSS = [pair for i in range(1, 31, 2) for pair in ((i, i + 1), (i + 1, i))]
VMEM_LIMIT = 50 * 1024 * 1024
FIRST_LIMIT = 53 * 1024 * 1024
MIDDLE_LIMIT = 36 * 1024 * 1024
SMALL_LIMIT = 20 * 1024 * 1024


def parts(value):
    high = value.astype(BF16)
    return high, (value - high.astype(F32)).astype(BF16)


def dot_nt(left, right, precision=None):
    return lax.dot_general(
        left, right, (((1,), (1,)), ((), ())), precision=precision, preferred_element_type=F32
    )


def dot_nn(left, right, precision=None):
    return lax.dot_general(
        left, right, (((1,), (0,)), ((), ())), precision=precision, preferred_element_type=F32
    )


def lane_of(shape):
    return lax.broadcasted_iota(jnp.int32, shape, len(shape) - 1)


def cols(a):
    return slice(a * LANES, (a + 1) * LANES)


def store_split(split_ref, a, value):
    high, low = parts(value)
    split_ref[0:K, cols(a)] = high
    split_ref[K : 2 * K, cols(a)] = low


def edge_columns(field_ref):
    lane = lane_of((K, LANES))
    first = jnp.zeros((K, LANES), F32)
    last = jnp.zeros((K, LANES), F32)
    for a in range(ROWS):
        block = field_ref[:, cols(a)]
        first = jnp.where(lane == a, block[:, 0:1], first)
        last = jnp.where(lane == a, block[:, LANES - 1 : LANES], last)
    return first, last


def packed_columns(strip):
    total = strip[0:8]
    for g in range(1, 8):
        total = total + pltpu.roll(strip[8 * g : 8 * g + 8], 16 * g, 1)
    return total


def unpacked_columns(packed):
    return jnp.concatenate(
        [packed if g == 0 else pltpu.roll(packed, LANES - 16 * g, 1) for g in range(8)], axis=0
    )


def smooth(field_ref, a, north, south, west, east):
    lane = lane_of((K, LANES))
    here = field_ref[:, cols(a)]
    up = field_ref[:, cols(a - 1)] if a > 0 else north
    down = field_ref[:, cols(a + 1)] if a < ROWS - 1 else south
    left = pltpu.roll(here, 1, 1)
    right = pltpu.roll(here, LANES - 1, 1)
    left = jnp.where(lane == 0, 0.0 if west is None else west[:, a : a + 1], left)
    right = jnp.where(lane == LANES - 1, 0.0 if east is None else east[:, a : a + 1], right)
    total = left + right
    if up is not None:
        total = total + up
    if down is not None:
        total = total + down
    return total - 4.0 * here


def hand_out(pay, mine, other):
    me = lax.axis_index("core")
    mine[...] = pay[me]
    depth = pay.shape[2]
    for chip in range(16):
        other[chip * depth : (chip + 1) * depth, :] = pay[1 - me, chip]


def hand_out_edges(field, depth, other, cross, columns):
    me = lax.axis_index("core")
    top = field[:, cols(0)]
    bottom = field[:, cols(ROWS - 1)]
    other[16 * depth : 16 * depth + K, :] = jnp.where(me == 0, bottom, top)
    cross[...] = jnp.where(me == 0, top, bottom)
    first, last = edge_columns(field)
    columns[0:8, :] = packed_columns(first)
    columns[8:16, :] = packed_columns(last)


def take_in_edges(pair, cross, columns):
    me = lax.axis_index("core")
    z = lax.axis_index("z")
    depth = columns.shape[1] - 8
    north = jnp.where(me == 0, cross[...], pair[...])
    south = jnp.where(me == 0, pair[...], cross[...])
    before = columns[jnp.maximum(z - 1, 0), depth : depth + 8, :]
    after = columns[jnp.minimum(z + 1, 7), depth : depth + 8, :]
    west = unpacked_columns(jnp.where(z > 0, before, 0.0))
    east = unpacked_columns(jnp.where(z < 7, after, 0.0))
    return north, south, west, east


def take_in(mine, other, full):
    me = lax.axis_index("core")
    full[me] = mine[...]
    full[1 - me] = other[...]


def row_of_shards(full, row):
    return jnp.concatenate(
        [full[half, chip, row : row + 1, :] for half in range(2) for chip in range(16)], axis=0
    )


def put_square(pay, row, doubled):
    packed = jnp.where(lane_of((K // 2, LANES)) < K, doubled[0 : K // 2], doubled[K // 2 : K])
    for half in range(2):
        for chip in range(16):
            at = half * 16 + chip
            pay[half, chip, row : row + 1, :] = packed[at : at + 1]


def square_of(full, row):
    packed = row_of_shards(full, row)
    return jnp.concatenate([packed, pltpu.roll(packed, K, 1)], axis=0)


def folded(product):
    rows = product[0:K] + product[K : 2 * K]
    return rows + pltpu.roll(rows, K, 1)


def inverse_factor(square):
    lane = lane_of((8, LANES))
    sub = lax.broadcasted_iota(jnp.int32, (8, LANES), 0)
    count = K // 8
    held = []
    for b in range(count):
        unit = jnp.where(lane - K == sub + 8 * b, 1.0, 0.0)
        held.append(jnp.where(lane < K, square[8 * b : 8 * b + 8] * (1.0 / NPTS), unit))
    for home in range(count):
        columns = [
            [
                jnp.broadcast_to(held[b][:, 8 * home + q : 8 * home + q + 1], (8, LANES))
                for b in range(home, count)
            ]
            for q in range(8)
        ]
        rows, scales = [], []
        for q in range(8):
            inverse = 1.0 / columns[q][0][q : q + 1, :]
            row = held[home][q : q + 1, :]
            scale = [column * inverse for column in columns[q]]
            scale[0] = jnp.where(sub > q, scale[0], 0.0)
            if q < 7:
                held[home] = held[home] - scale[0] * row
            for p in range(q + 1, 8):
                entry = columns[p][0][q : q + 1, :]
                columns[p] = [c - m * entry for c, m in zip(columns[p], scale)]
            rows.append(row)
            scales.append(scale)
        for at, b in enumerate(range(home + 1, count), 1):
            update = scales[0][at] * rows[0]
            for q in range(1, 8):
                update = update + scales[q][at] * rows[q]
            held[b] = held[b] - update
    done = []
    for b in range(count):
        diagonal = jnp.sum(jnp.where(lane == sub + 8 * b, held[b], 0.0), axis=1, keepdims=True)
        done.append(held[b] * lax.rsqrt(diagonal))
    return pltpu.roll(jnp.concatenate(done, axis=0), K, 1)[:, 0:K]


def put_coefficients(pay, block, held, split):
    both = dot_nt(held[block].reshape(2 * BLOCK, PTS), split[...])
    turned = (both[0:BLOCK] + both[BLOCK : 2 * BLOCK]).T
    turned = turned[0:K] + turned[K : 2 * K]
    for part in range(BLOCK // LANES):
        at = block * (BLOCK // LANES) + part
        chips = slice(4 * (at % 4), 4 * (at % 4) + 4)
        pay[at // 4, chips, 0:16, :] = turned[:, cols(part)].reshape(4, 16, LANES)


def coefficients_of(full, at):
    chips = slice(4 * (at % 4), 4 * (at % 4) + 4)
    return full[at // 4, chips, 0:16, :].reshape(K, LANES)


def spread_coefficients(full, spread):
    for block in range(NBLOCK):
        for part in range(BLOCK // LANES):
            high, low = parts(coefficients_of(full, block * (BLOCK // LANES) + part))
            spread[block, 0:K, cols(part)] = high
            spread[block, K : 2 * K, cols(part)] = low


def begin_kernel(
    snap, basis_in, sea_in, snap_out, flat, mine, other, cross, columns,
    raw, held, split, pay, basis, sea, in_sems, out_sems, own_sems,
):
    own = [
        pltpu.make_async_copy(basis_in, basis, own_sems.at[0]),
        pltpu.make_async_copy(sea_in, sea, own_sems.at[1]),
    ]
    for copy in own:
        copy.start()
    deep = BLOCK // 2

    def arrive(piece):
        span = pl.ds(piece * deep * ROWS, deep * ROWS)
        return pltpu.make_async_copy(snap.at[span], raw.at[span], in_sems.at[piece])

    def leave(piece):
        at = (piece // 2, slice(None), pl.ds((piece % 2) * deep, deep))
        return pltpu.make_async_copy(held.at[at], snap_out.at[at], out_sems.at[piece])

    for piece in range(2 * NBLOCK):
        arrive(piece).start()
    for copy in own:
        copy.wait()
    for a in range(ROWS):
        value = basis[pl.ds(a, K, stride=ROWS), :] * sea[a : a + 1, :].astype(F32)
        flat[:, cols(a)] = value
        store_split(split, a, value)
    hand_out_edges(flat, DEPTH, other, cross, columns)
    for block in range(NBLOCK):
        for piece in (2 * block, 2 * block + 1):
            arrive(piece).wait()
            span = slice((piece % 2) * deep, (piece % 2 + 1) * deep)
            for a in range(ROWS):
                high, low = parts(raw[pl.ds(piece * deep * ROWS + a, deep, stride=ROWS), :])
                held[block, 0, span, cols(a)] = high
                held[block, 1, span, cols(a)] = low
            leave(piece).start()
    project(held, split, pay)
    hand_out(pay, mine, other)
    for piece in range(2 * NBLOCK):
        leave(piece).wait()


VM = pl.BlockSpec(memory_space=pltpu.VMEM)
HB = pl.BlockSpec(memory_space=pl.ANY)
HBM = pl.BlockSpec(memory_space=pltpu.HBM)


def shared_outputs(depth):
    return [
        jax.ShapeDtypeStruct((K, PTS), F32),
        jax.ShapeDtypeStruct((16, depth, LANES), F32),
        jax.ShapeDtypeStruct((16 * depth + K, LANES), F32),
        jax.ShapeDtypeStruct((K, LANES), F32),
        jax.ShapeDtypeStruct((16, LANES), F32),
    ]


def begin(snapshots, basis, sea):
    return pl.pallas_call(
        begin_kernel,
        in_specs=[HBM, HBM, HBM],
        out_specs=[HB, *[VM] * 5],
        out_shape=[
            jax.ShapeDtypeStruct((2 * NBLOCK, 2, BLOCK, PTS), BF16),
            *shared_outputs(DEPTH),
        ],
        scratch_shapes=[
            pltpu.VMEM((NSNAP * ROWS, LANES), F32),
            pltpu.VMEM((NBLOCK, 2, BLOCK, PTS), BF16),
            pltpu.VMEM((2 * K, PTS), BF16),
            pltpu.VMEM((2, 16, DEPTH, LANES), F32),
            pltpu.VMEM((K * ROWS, LANES), F32),
            pltpu.VMEM((ROWS, LANES), jnp.int32),
            pltpu.SemaphoreType.DMA((2 * NBLOCK,)),
            pltpu.SemaphoreType.DMA((2 * NBLOCK,)),
            pltpu.SemaphoreType.DMA((2,)),
        ],
        compiler_params=pltpu.CompilerParams(vmem_limit_bytes=FIRST_LIMIT),
        name="split_and_project",
    )(snapshots.reshape(NSNAP * ROWS, LANES), basis.reshape(K * ROWS, LANES), sea)


def copy_of(snap, held, sems, block):
    return pltpu.make_async_copy(snap.at[block], held.at[block], sems.at[block])


def begin_copies(snap, held, sems):
    for block in range(NBLOCK):
        copy_of(snap, held, sems, block).start()


def expand(spread, snap, held, sems, total):
    width = 512
    for block in range(NBLOCK):
        copy_of(snap, held, sems, block).wait()
        for left in range(0, PTS, width):
            at = slice(left, left + width)
            both = dot_nn(spread[block], held[block, 0, :, at]) + dot_nn(
                spread[block], held[block, 1, :, at]
            )
            piece = both[0:K] + both[K : 2 * K]
            total[:, at] = piece if block == 0 else total[:, at] + piece


def project(held, split, pay):
    for block in range(NBLOCK):
        put_coefficients(pay, block, held, split)


def rough_field(prev, sides, pen, out):
    for a in range(ROWS):
        out[:, cols(a)] = pen[a : a + 1, :] * smooth(prev, a, *sides)


def applied_field(total, rough, sea, out):
    for a in range(ROWS):
        mask = sea[a : a + 1, :].astype(F32)
        out[:, cols(a)] = mask * (total[:, cols(a)] * (1.0 / NPTS) + rough[:, cols(a)])


def first_kernel(
    got_mine, got_other, snap, prev, pair, near, around, sea, pen,
    field, mine, other, cross, columns,
    full, spread, total, rough, held, split, pay, sems,
):
    begin_copies(snap, held, sems)
    take_in(got_mine, got_other, full)
    spread_coefficients(full, spread)
    rough_field(prev, take_in_edges(pair, near, around), pen, rough)
    expand(spread, snap, held, sems, total)
    applied_field(total, rough, sea, field)
    for a in range(ROWS):
        store_split(split, a, field[:, cols(a)])
    hand_out_edges(field, SHARD, other, cross, columns)
    pay[...] = jnp.zeros_like(pay)
    put_square(pay, 16, folded(dot_nt(split[...], split[...])))
    project(held, split, pay)
    hand_out(pay, mine, other)


def scratch_for_expand(depth):
    return [
        pltpu.VMEM((2, 16, depth, LANES), F32),
        pltpu.VMEM((NBLOCK, 2 * K, BLOCK), BF16),
        pltpu.VMEM((K, PTS), F32),
        pltpu.VMEM((K, PTS), F32),
    ]


def first_step(got, snap, prev, sides, sea, pen):
    return pl.pallas_call(
        first_kernel,
        in_specs=[VM, VM, HB, *[VM] * 6],
        out_specs=[VM] * 5,
        out_shape=shared_outputs(SHARD),
        scratch_shapes=[
            *scratch_for_expand(DEPTH),
            pltpu.VMEM((NBLOCK, 2, BLOCK, PTS), BF16),
            pltpu.VMEM((2 * K, PTS), BF16),
            pltpu.VMEM((2, 16, SHARD, LANES), F32),
            pltpu.SemaphoreType.DMA((NBLOCK,)),
        ],
        compiler_params=pltpu.CompilerParams(vmem_limit_bytes=VMEM_LIMIT),
        name="expand_and_project",
    )(*got, snap, prev, *sides, sea, pen)


def solved(inverse, field, split):
    for a in range(ROWS):
        store_split(split, a, field[:, cols(a)])
    high, low = parts(inverse)
    left = [jnp.concatenate([part, part], axis=1) for part in (high, low)]
    both = dot_nn(jnp.concatenate(left, axis=0), split[...])
    return both[0:K] + both[K : 2 * K]


def second_kernel(
    got_mine, got_other, snap, prev, pair, near, around, sea, pen,
    field, bottom, last, held,
    full, spread, total, rough, raw, split, sems,
):
    begin_copies(snap, held, sems)
    take_in(got_mine, got_other, full)
    spread_coefficients(full, spread)
    inverse = inverse_factor(square_of(full, 16))
    rough_field(prev, take_in_edges(pair, near, around), pen, rough)
    expand(spread, snap, held, sems, total)
    applied_field(total, rough, sea, raw)
    field[...] = solved(inverse, raw, split)
    bottom[0:K, :] = field[:, cols(ROWS - 1)]
    bottom[K : 2 * K, :] = field[:, cols(ROWS - 1)] * pen[ROWS - 1 : ROWS, :]
    _, last[0:K, :] = edge_columns(field)
    for a in range(ROWS):
        raw[:, cols(a)] = field[:, cols(a)] * pen[a : a + 1, :]
    _, last[K : 2 * K, :] = edge_columns(raw)


def second_step(got, snap, prev, sides, sea, pen):
    halo = jax.ShapeDtypeStruct((2 * K, LANES), F32)
    return pl.pallas_call(
        second_kernel,
        in_specs=[VM, VM, HB, *[VM] * 6],
        out_specs=[VM] * 4,
        out_shape=[
            jax.ShapeDtypeStruct((K, PTS), F32),
            halo,
            halo,
            jax.ShapeDtypeStruct((NBLOCK, 2, BLOCK, PTS), BF16),
        ],
        scratch_shapes=[
            *scratch_for_expand(SHARD),
            pltpu.VMEM((K, PTS), F32),
            pltpu.VMEM((2 * K, PTS), BF16),
            pltpu.SemaphoreType.DMA((NBLOCK,)),
        ],
        compiler_params=pltpu.CompilerParams(vmem_limit_bytes=MIDDLE_LIMIT),
        name="factor_and_expand",
    )(*got, snap, prev, *sides, sea, pen)


def project_kernel(held, field, pay, split):
    for a in range(ROWS):
        store_split(split, a, field[:, cols(a)])
    pay[...] = jnp.zeros_like(pay)
    put_square(pay, 16, folded(dot_nt(split[...], split[...])))
    project(held, split, pay)


def project_step(held, field):
    return pl.pallas_call(
        project_kernel,
        in_specs=[VM, VM],
        out_specs=VM,
        out_shape=jax.ShapeDtypeStruct((2, 16, SHARD, LANES), F32),
        scratch_shapes=[pltpu.VMEM((2 * K, PTS), BF16)],
        compiler_params=pltpu.CompilerParams(vmem_limit_bytes=MIDDLE_LIMIT),
        name="project",
    )(held, field)


def rough_kernel(field, north, west, pen, base, mine, other, left, right, pay):
    def put(at, first, second):
        high, low = parts(first)
        left[0:K, cols(at)] = high
        left[K : 2 * K, cols(at)] = low
        high, low = parts(second)
        right[0:K, cols(at)] = high
        right[K : 2 * K, cols(at)] = low

    first = jnp.zeros((K, LANES), F32)
    first_weighted = jnp.zeros((K, LANES), F32)
    lane = lane_of((K, LANES))
    for a in range(ROWS):
        here = field[:, cols(a)]
        weighted = here * pen[a : a + 1, :]
        put(a, weighted, smooth(field, a, None, None, None, None))
        first = jnp.where(lane == a, here[:, 0:1], first)
        first_weighted = jnp.where(lane == a, weighted[:, 0:1], first_weighted)
        if a == 0:
            put(ROWS, weighted, north[0:K, :])
            put(ROWS + 1, north[K : 2 * K, :], here)
    put(ROWS + 2, first_weighted, west[0:K, :])
    put(ROWS + 3, west[K : 2 * K, :], first)
    pay[...] = base[...]
    put_square(pay, 17, folded(dot_nt(left[...], right[...])))
    hand_out(pay, mine, other)


def rough_step(field, north, west, pen, base):
    return pl.pallas_call(
        rough_kernel,
        in_specs=[VM] * 5,
        out_specs=[VM] * 2,
        out_shape=[
            jax.ShapeDtypeStruct((16, SHARD, LANES), F32),
            jax.ShapeDtypeStruct((16 * SHARD, LANES), F32),
        ],
        scratch_shapes=[
            pltpu.VMEM((2 * K, PTS + 4 * LANES), BF16),
            pltpu.VMEM((2 * K, PTS + 4 * LANES), BF16),
            pltpu.VMEM((2, 16, SHARD, LANES), F32),
        ],
        compiler_params=pltpu.CompilerParams(vmem_limit_bytes=SMALL_LIMIT),
        name="roughness_products",
    )(field, north, west, pen, base)


def last_kernel(got_mine, got_other, field, basis, matrix, full, split):
    take_in(got_mine, got_other, full)
    inverse = inverse_factor(square_of(full, 16))
    final = solved(inverse, field, split)
    for a in range(ROWS):
        basis[pl.ds(a, K, stride=ROWS), :] = final[:, cols(a)]
    turned = jnp.concatenate([coefficients_of(full, at) for at in range(NSNAP // LANES)], axis=1)
    rough = square_of(full, 17)[:, 0:K]
    gram = dot_nt(turned, turned, HIGHEST)
    middle = (gram * (1.0 / NPTS) + rough) * (1.0 / NPTS)
    matrix[...] = dot_nt(dot_nn(inverse, middle, HIGHEST), inverse, HIGHEST)


def last_step(got, field):
    basis, matrix = pl.pallas_call(
        last_kernel,
        in_specs=[VM] * 3,
        out_specs=[VM] * 2,
        out_shape=[
            jax.ShapeDtypeStruct((K * ROWS, LANES), F32),
            jax.ShapeDtypeStruct((K, K), F32),
        ],
        scratch_shapes=[
            pltpu.VMEM((2, 16, SHARD, LANES), F32),
            pltpu.VMEM((2 * K, PTS), BF16),
        ],
        compiler_params=pltpu.CompilerParams(vmem_limit_bytes=SMALL_LIMIT),
        name="factor_and_finish",
    )(*got, field)
    return basis.reshape(K, ROWS, LANES), matrix


def exchange(value, axis):
    return lax.all_to_all(value, axis, 0, 0, tiled=True)


def copies(value, count):
    return jnp.broadcast_to(value[None], (count, *value.shape))


def summed_everywhere(mine, other, edges=None):
    depth = mine.shape[1]
    got = lax.ppermute(other, "core", SWAP)
    pair = mine + got[: 16 * depth].reshape(mine.shape)
    if edges is not None:
        cross, columns = edges
        pair, cross = lax.optimization_barrier((pair, cross))
        near = lax.ppermute(cross, LAT, CROSS)
    shares = exchange(pair, CHIPS)
    if edges is not None:
        shares, near = lax.optimization_barrier((shares, near))
    sent = copies(shares.sum(axis=0), 8)
    if edges is not None:
        below = lax.broadcasted_iota(jnp.int32, (8, 1, 1), 0) < lax.axis_index("z")
        sent = jnp.concatenate([sent, jnp.where(below, columns[0:8], columns[8:16])], axis=1)
    around = exchange(sent, "z")
    half = exchange(copies(around[:, :depth].sum(axis=0), 16), CHIPS)
    both = (half, lax.ppermute(half, "core", SWAP))
    if edges is None:
        return both, None
    return both, (got[16 * depth :], near, around)


def from_below(value, axis, count):
    return lax.ppermute(value, axis, [(i, i + 1) for i in range(count - 1)])


def local(snapshots, land_sea, penalty, initial_basis):
    snap, start, mine, other, *edges = begin(snapshots, initial_basis, land_sea)
    got, sides = summed_everywhere(mine, other, edges)
    applied, mine, other, *edges = first_step(got, snap, start, sides, land_sea, penalty)
    got, sides = summed_everywhere(mine, other, edges)
    applied, bottom, last, held = second_step(got, snap, applied, sides, land_sea, penalty)
    north = from_below(bottom, LAT, 32)
    west = from_below(last, "z", 8)
    base = project_step(held, applied)
    mine, other = rough_step(applied, north, west, penalty, base)
    got, _ = summed_everywhere(mine, other)
    return last_step(got, applied)


def solution(mesh):
    split_mesh = Mesh(mesh.devices.reshape(4, 4, 2, 8), ("y", "x", "core", "z"))
    flat = P(LAT, "z")
    deep = P(None, LAT, "z")
    return jax.shard_map(
        local,
        mesh=split_mesh,
        in_specs=(deep, flat, flat, deep),
        out_specs=(deep, P()),
        check_vma=False,
    )
```
